128 devices in a mesh: seq: 16 (over x, z), rep: 8 (over y, core).
Axes of the slice: x: 4, y: 4, z: 4, core: 2. Of those that a mesh axis runs over, the one named last changes fastest.
Arguments:
- residual_in: bfloat16 [8192, 5120], P('seq', 'rep'), may hold values from -3 to 3
- queries: bfloat16 [8192, 5120], P('seq'), may hold values from -36 to 36
- keys: bfloat16 [8192, 5120], P('seq'), may hold values from -36 to 36
- values: bfloat16 [8192, 5120], P('seq'), may hold values from -6 to 6
- w_out: bfloat16 [5120, 5120], P(None, 'rep'), may hold values from -0.078125 to 0.078125
- gate_scale: float32 [5120], P('rep'), may hold values from 0.5 to 2
- tile_mask: int32 [40, 64, 64], replicated, may hold values from 0 to 1, as said below
Outputs:
- block_out: bfloat16 [8192, 5120], P('seq', 'rep')
The draws below stay inside these ranges and needn't reach their ends.
Inputs may be any that keep to these rules, and one draw needn't show every extreme that they name: Every diagonal entry tile_mask[h, a, a] is 1 and each head's mask is symmetric.
All inputs are finite; a program needn't handle non-finite values.
Results may differ from the reference program's by a relative error of at most 0.0037.
Values may be sent and summed in bfloat16 or wider, within the bound.
No kernel may reach another device: no remote copies, remote signals or barrier semaphores. Data moves between devices by JAX's collectives and lax.ppermute only.
A program may use at most 192 MiB of HBM per device.

```python
import math
import jax
import jax.numpy as jnp
from jax import lax

D = 5120
HEADS = 40
HEAD_DIM = 128
TILE = 128
TOKENS = 8192
TILES = 64


def draw_queries(key, part):
    key = jax.random.fold_in(key, 11)
    result = 1.5 * jnp.clip(jax.random.normal(key, (TOKENS, D), jnp.float32), -6.0, 6.0)
    return result.astype(jnp.bfloat16)


def draw_keys(key, part):
    key = jax.random.fold_in(key, 12)
    result = 1.5 * jnp.clip(jax.random.normal(key, (TOKENS, D), jnp.float32), -6.0, 6.0)
    return result.astype(jnp.bfloat16)


def within_reach(coords, reach):
    distance = jnp.abs(coords[:, None] - coords[None, :])
    return distance[None, :, :] <= reach[:, None, None]


def draw_tile_mask(key, part):
    key = jax.random.fold_in(key, 13)
    radius_set = jax.random.randint(key, (HEADS, 3), 0, 3)
    tile_ids = jnp.arange(TILES)
    tile_frame = tile_ids // 16
    tile_row = tile_ids // 4 % 4
    tile_col = tile_ids % 4
    allowed = within_reach(tile_frame, radius_set[:, 0]) & within_reach(tile_row, radius_set[:, 1]) & within_reach(tile_col, radius_set[:, 2])
    return allowed.astype(jnp.int32)


def block_levels(rng, shape, shards, low, high):
    def one(position, shards_of):
        draws = jax.random.uniform(jax.random.fold_in(jax.random.fold_in(rng, 6), position), (shards_of,), jnp.float32, low / len(shards), high / len(shards))
        return jnp.repeat(jnp.exp(draws), shape[position] // shards_of).reshape((-1,) + (1,) * (len(shape) - position - 1))

    gain = one(*shards[0])
    for cut in shards[1:]:
        gain = gain * one(*cut)
    return gain


def bell_draw(rng, shape, spread, bound, split=(), kind=jnp.bfloat16):
    entries = jax.random.normal(rng, shape, jnp.float32) * spread
    if len(split) > 0:
        entries = block_levels(rng, shape, split, -0.22, 0.18) * entries
    return jnp.clip(entries, min=-bound, max=bound).astype(kind)


def setup_inputs(seed: int = 0) -> dict:
    splits = jax.random.split(jax.random.key(seed), 8)
    return {
        "residual_in": bell_draw(splits[0], (TOKENS, D), 0.5, 3.0, ((0, 16), (1, 8))),
        "queries": draw_queries(jax.random.fold_in(splits[7], 71), 0),
        "keys": draw_keys(jax.random.fold_in(splits[7], 71), 0),
        "values": bell_draw(splits[3], (TOKENS, D), 1.0, 6.0, ((0, 16),)),
        "w_out": bell_draw(splits[4], (D, D), D ** -0.5, 0.078125, ((1, 8),)),
        "gate_scale": jnp.clip(jnp.exp(math.log(2.0) - 1.3862944 * jax.random.uniform(splits[5], (D,), jnp.float32) ** block_levels(splits[5], (D,), ((0, 8),), -0.2, 0.2)), 0.5, 2.0),
        "tile_mask": draw_tile_mask(jax.random.fold_in(splits[7], 71), 0),
    }


def head_major(array):
    return array.reshape(TOKENS, HEADS, HEAD_DIM).transpose(1, 0, 2)


def reference(residual_in, queries, keys, values, w_out, gate_scale, tile_mask):
    tile_ids = (jnp.arange(TOKENS) // TILE).astype(jnp.int32)

    def per_head(operands):
        query_head, key_head, value_head, mask_head = operands
        scores = jnp.einsum("qc,kc->qk", query_head.astype(jnp.float32), key_head.astype(jnp.float32)) * (HEAD_DIM ** -0.5)
        allowed = mask_head[tile_ids][:, tile_ids] > 0
        scores = jnp.where(allowed, scores, -jnp.inf)
        row_max = jnp.max(scores, axis=1, keepdims=True)
        exp_scores = jnp.exp(scores - row_max)
        row_sum = jnp.sum(exp_scores, axis=1, keepdims=True)
        weights = (exp_scores / row_sum).astype(jnp.bfloat16)
        return jnp.dot(weights, value_head, preferred_element_type=jnp.float32).astype(jnp.bfloat16)

    attended = lax.map(per_head, (head_major(queries), head_major(keys), head_major(values), tile_mask))
    merged = attended.transpose(1, 0, 2).reshape(TOKENS, D)
    projected = jnp.dot(merged, w_out, preferred_element_type=jnp.float32)
    return (residual_in.astype(jnp.float32) + gate_scale * projected).astype(jnp.bfloat16)
```

```python
import functools

import jax
import jax.numpy as jnp
from jax import lax
from jax.experimental import pallas as pl
from jax.experimental.pallas import tpu as pltpu
from jax.sharding import Mesh
from jax.sharding import PartitionSpec as P

TILE = 128
HEADS = 40
PLANES = 4
PLANE_HEADS = HEADS // PLANES
CHIPS = 16
HALF = 256
GROUP = 4
UNROLL = 4
ITEMS = 512
LOG2E = 1.4426950408889634
TOKENS_AXES = ("x", "z")
LOW = -1e30


def head_plan(work):
    ids = jnp.arange(HEADS)
    ahead = (work[None, :] > work[:, None]) | ((work[None, :] == work[:, None]) & (ids[None, :] < ids[:, None]))
    rank = jnp.sum(ahead.astype(jnp.int32), axis=1)
    row, col = rank // PLANES, rank % PLANES
    plane = jnp.where(row % 2 == 1, PLANES - 1 - col, col)
    place = plane * PLANE_HEADS + row
    hit = (place[None, :] == ids[:, None]).astype(jnp.int32)
    head_at = jnp.sum(hit * ids[None, :], axis=1)
    work_at = jnp.sum(hit * work[None, :], axis=1)
    return head_at, work_at


def chip_plan(work_at):
    extra = CHIPS - PLANE_HEADS
    quota = (work_at[:, None].astype(jnp.float32) / jnp.arange(1, extra + 1).astype(jnp.float32)[None, :]).reshape(-1)
    ids = jnp.arange(quota.shape[0])
    ahead = (quota[None, :] > quota[:, None]) | ((quota[None, :] == quota[:, None]) & (ids[None, :] < ids[:, None]))
    won = (jnp.sum(ahead.astype(jnp.int32), axis=1) < extra).astype(jnp.int32)
    chips = 1 + jnp.sum(won.reshape(PLANE_HEADS, extra), axis=1)
    slots = jnp.arange(PLANE_HEADS)
    first = jnp.sum(jnp.where(slots[None, :] < slots[:, None], chips[None, :], 0), axis=1)
    return chips, first


def pack_kernel(heads, q_ref, k_ref, v_ref, out_ref):
    out_ref[0, 0] = k_ref[...]
    for sub in range(2):
        rows = pl.ds(sub * TILE, TILE)
        out_ref[0, 1, rows, :] = v_ref[rows, :].T
    out_ref[0, 2] = q_ref[...]


def pack(queries, keys, values, chip_heads, core):
    scalars = jnp.concatenate([chip_heads, core[None]]).astype(jnp.int32)
    spec = pl.BlockSpec((HALF, TILE), lambda t, s: (s[CHIPS], s[t]))
    return pl.pallas_call(
        pack_kernel,
        grid_spec=pltpu.PrefetchScalarGridSpec(
            num_scalar_prefetch=1,
            grid=(CHIPS,),
            in_specs=[spec] * 3,
            out_specs=pl.BlockSpec((1, 3, HALF, TILE), lambda t, s: (t, 0, 0, 0)),
        ),
        out_shape=jax.ShapeDtypeStruct((CHIPS, 3, HALF, TILE), jnp.bfloat16),
    )(scalars, queries, keys, values)


def attend_kernel(scale, meta, q_of, k_of, valid_of, own_ref, other_ref, out_ref, k_s, v_s, acc_s, max_s, sum_s):
    core = meta[0]

    def place(t, _):
        for sub in range(2):
            rows = pl.ds(sub * TILE, TILE)
            mine = 4 * t + 2 * core + sub
            theirs = 4 * t + 2 * (1 - core) + sub
            k_s[mine] = own_ref[t, 0, rows, :]
            v_s[mine] = own_ref[t, 1, rows, :]
            k_s[theirs] = other_ref[t, 0, rows, :]
            v_s[theirs] = other_ref[t, 1, rows, :]
        return 0

    lax.fori_loop(0, CHIPS, place, 0)
    acc_s[...] = jnp.zeros_like(acc_s)
    sum_s[...] = jnp.zeros_like(sum_s)
    max_s[...] = jnp.full_like(max_s, LOW)

    def body(step, _):
        parts = []
        for u in range(UNROLL):
            e = step * UNROLL + u
            t = q_of[e]
            kid = [k_of[e * GROUP + g] for g in range(GROUP)]
            valid = valid_of[e]
            q = own_ref[t // 2, 2, pl.ds(pl.multiple_of((t % 2) * TILE, TILE), TILE), :]
            keys = jnp.concatenate([k_s[i] for i in kid], axis=0)
            scores = lax.dot_general(keys, q, (((1,), (1,)), ((), ())), preferred_element_type=jnp.float32)
            top = jnp.max(scores, axis=0, keepdims=True) * scale
            weights = []
            total = jnp.zeros((1, TILE), jnp.float32)
            for g in range(GROUP):
                shift = top + jnp.where(g < valid, 0.0, -LOW)
                w = jnp.exp2(scores[g * TILE : (g + 1) * TILE] * scale - shift)
                total = total + jnp.sum(w, axis=0, keepdims=True)
                weights.append(w.astype(jnp.bfloat16))
            vals = jnp.concatenate([v_s[i] for i in kid], axis=1)
            part = jnp.dot(vals, jnp.concatenate(weights, axis=0), preferred_element_type=jnp.float32)
            parts.append((t, top, total, part))
        for t, top, total, part in parts:
            old = max_s[t]
            new = jnp.maximum(old, top)
            a = jnp.exp2(old - new)
            b = jnp.exp2(top - new)
            max_s[t] = new
            sum_s[t] = sum_s[t] * a + total * b
            acc_s[t] = acc_s[t] * a + part * b
        return 0

    lax.fori_loop(0, meta[1], body, 0)

    def finish(t, _):
        out_ref[t] = (acc_s[t] / jnp.maximum(sum_s[t], 1e-30)).astype(jnp.bfloat16)
        return 0

    lax.fori_loop(0, 2 * CHIPS, finish, 0)


def attend(meta, q_of, k_of, valid_of, own, other):
    smem = pl.BlockSpec(memory_space=pltpu.SMEM)
    vmem = pl.BlockSpec(memory_space=pltpu.VMEM)
    return pl.pallas_call(
        functools.partial(attend_kernel, TILE**-0.5 * LOG2E),
        in_specs=[smem] * 4 + [vmem] * 2,
        out_specs=vmem,
        out_shape=jax.ShapeDtypeStruct((2 * CHIPS, TILE, TILE), jnp.bfloat16),
        scratch_shapes=[
            pltpu.VMEM((4 * CHIPS, TILE, TILE), jnp.bfloat16),
            pltpu.VMEM((4 * CHIPS, TILE, TILE), jnp.bfloat16),
            pltpu.VMEM((2 * CHIPS, TILE, TILE), jnp.float32),
            pltpu.VMEM((2 * CHIPS, 1, TILE), jnp.float32),
            pltpu.VMEM((2 * CHIPS, 1, TILE), jnp.float32),
        ],
        compiler_params=pltpu.CompilerParams(vmem_limit_bytes=40 * 2**20),
    )(meta, q_of, k_of, valid_of, own, other)


def item_lists(allowed, mine):
    tiles = allowed.shape[1]
    count = jnp.sum(allowed, axis=1) * mine
    groups = (count + GROUP - 1) // GROUP
    slots = jnp.arange(groups.shape[0])
    end = jnp.sum(jnp.where(slots[None, :] <= slots[:, None], groups[None, :], 0), axis=1)
    steps = (end[-1] + UNROLL - 1) // UNROLL
    key_ids = jnp.arange(tiles)
    before = jnp.sum(allowed[:, None, :] * (key_ids[None, :] < key_ids[:, None])[None].astype(jnp.int32), axis=2)
    listed = jnp.sum(
        jnp.where((before[:, :, None] == key_ids[None, None, :]) & (allowed[:, :, None] > 0), key_ids[None, :, None], 0),
        axis=1,
    )
    item = jnp.arange(ITEMS)
    real = (item < end[-1]).astype(jnp.int32)
    held = jnp.minimum(item, end[-1] - 1)
    q_of = jnp.sum((end[None, :] <= held[:, None]).astype(jnp.int32), axis=1)
    pick = (q_of[:, None] == slots[None, :]).astype(jnp.int32)
    start = 4 * (held - jnp.sum(pick * (end - groups)[None, :], axis=1))
    left = jnp.sum(pick * count[None, :], axis=1) - start
    rows = jnp.dot(pick.astype(jnp.float32), listed.astype(jnp.float32))
    offset = jnp.arange(GROUP)
    where = start[:, None] + jnp.where(offset[None, :] < left[:, None], offset[None, :], 0)
    k_of = jnp.sum(jnp.where(where[:, :, None] == key_ids[None, None, :], rows[:, None, :], 0.0), axis=2)
    valid = jnp.minimum(left, GROUP) * real
    return steps, q_of, k_of.astype(jnp.int32).reshape(-1), valid


def select_kernel(source, got_ref, out_ref):
    for i in range(PLANE_HEADS):
        for sub in range(2):
            tile = got_ref[source[2 * i + sub], sub]
            out_ref[pl.ds(sub * TILE, TILE), pl.ds(i * TILE, TILE)] = tile.T


def select(source, got):
    vmem = pl.BlockSpec(memory_space=pltpu.VMEM)
    return pl.pallas_call(
        select_kernel,
        in_specs=[pl.BlockSpec(memory_space=pltpu.SMEM), vmem],
        out_specs=vmem,
        out_shape=jax.ShapeDtypeStruct((HALF, PLANE_HEADS * TILE), jnp.bfloat16),
    )(source, got)


def exchange(block):
    return lax.all_to_all(block, TOKENS_AXES, split_axis=0, concat_axis=0, tiled=True)


def along_y(block, step):
    return lax.ppermute(block, "y", [(i, (i + step) % PLANES) for i in range(PLANES)])


def swap(block):
    return lax.ppermute(block, "c", [(0, 1), (1, 0)])


def shards(residual_in, queries, keys, values, w_out, gate_scale, tile_mask):
    chip = lax.axis_index("x") * 4 + lax.axis_index("z")
    plane = lax.axis_index("y")
    core = lax.axis_index("c")
    tile_work = jnp.sum(tile_mask, axis=2)
    head_at, work_at = head_plan(jnp.sum(tile_work, axis=1))
    plane_heads = lax.dynamic_slice_in_dim(head_at, plane * PLANE_HEADS, PLANE_HEADS)
    chips, first = chip_plan(lax.dynamic_slice_in_dim(work_at, plane * PLANE_HEADS, PLANE_HEADS))
    chip_ids = jnp.arange(CHIPS)
    on_chip = (first[None, :] <= chip_ids[:, None]) & (chip_ids[:, None] < (first + chips)[None, :])
    chip_heads = jnp.sum(jnp.where(on_chip, plane_heads[None, :], 0), axis=1)
    got = exchange(pack(queries, keys, values, chip_heads, core))
    got_other = swap(got)

    half_work = lax.dynamic_index_in_dim(tile_work.reshape(HEADS, CHIPS, 2, 2), core, 2, keepdims=False)
    half_work = jnp.take(half_work.reshape(HEADS, 2 * CHIPS), plane_heads, axis=0)
    tile_ids = jnp.arange(2 * CHIPS)
    done = jnp.sum(
        jnp.where((tile_ids[None, :] < tile_ids[:, None])[None], half_work[:, None, :], 0), axis=2
    )
    total = jnp.sum(half_work, axis=1, keepdims=True)
    owner = first[:, None] + ((2 * done + half_work) * chips[:, None]) // (2 * total)
    my_slot = jnp.sum(jnp.where(on_chip[chip], jnp.arange(PLANE_HEADS), 0))
    my_head = chip_heads[chip]
    allowed = lax.dynamic_index_in_dim(tile_mask, my_head, 0, keepdims=False)
    allowed = lax.dynamic_index_in_dim(allowed.reshape(CHIPS, 2, 2, 4 * CHIPS), core, 1, keepdims=False)
    steps, q_of, k_of, valid = item_lists(
        allowed.reshape(2 * CHIPS, 4 * CHIPS), (owner[my_slot] == chip).astype(jnp.int32)
    )
    meta = jnp.stack([core, steps]).astype(jnp.int32)
    attended = attend(meta, q_of, k_of, valid, got, got_other)
    back = exchange(attended.reshape(CHIPS, 2, TILE, TILE))
    source = lax.dynamic_slice_in_dim(owner, 2 * chip, 2, 1).reshape(-1)
    own = select(source, back)

    order = (plane + jnp.array([0, 3, 1, 2])) % PLANES
    w_heads = w_out.reshape(HEADS, TILE, w_out.shape[1])
    w_order = jnp.take(head_at.reshape(PLANES, PLANE_HEADS), order, axis=0).reshape(-1)
    weights = jnp.take(w_heads, w_order, axis=0).reshape(PLANES, PLANE_HEADS * TILE, w_out.shape[1])
    blocks = [own, along_y(own, 1), along_y(own, 3), along_y(own, 2)]
    mine = jnp.zeros((HALF, w_out.shape[1]), jnp.float32)
    theirs = mine
    for k, block in enumerate(blocks):
        other = swap(block)
        mine = mine + jnp.dot(block, weights[k], preferred_element_type=jnp.float32)
        theirs = theirs + jnp.dot(other, weights[k], preferred_element_type=jnp.float32)
    low = jnp.where(core == 0, mine, theirs)
    high = jnp.where(core == 0, theirs, mine)
    projected = jnp.concatenate([low, high], axis=0)
    return (residual_in.astype(jnp.float32) + gate_scale * projected).astype(jnp.bfloat16)


def solution(mesh):
    fine = Mesh(mesh.devices.reshape(4, 4, 4, 2), ("x", "z", "y", "c"))
    seq, rep = TOKENS_AXES, ("y", "c")
    in_specs = (
        P(seq, rep),
        P(seq, None),
        P(seq, None),
        P(seq, None),
        P(None, rep),
        P(rep),
        P(),
    )
    return jax.shard_map(shards, mesh=fine, in_specs=in_specs, out_specs=P(seq, rep), check_vma=False)
```

```python
import functools

import jax
import jax.numpy as jnp
from jax import lax
from jax.experimental import pallas as pl
from jax.experimental.pallas import tpu as pltpu
from jax.sharding import Mesh
from jax.sharding import PartitionSpec as P

TILE = 128
HEADS = 40
PLANES = 4
PLANE_HEADS = HEADS // PLANES
CHIPS = 16
HALF = 256
GROUP = 4
UNROLL = 8
ITEMS = 256
LOG2E = 1.4426950408889634
TOKENS_AXES = ("x", "z")
LOW = -1e30


def head_plan(work):
    ids = jnp.arange(HEADS)
    ahead = (work[None, :] > work[:, None]) | ((work[None, :] == work[:, None]) & (ids[None, :] < ids[:, None]))
    rank = jnp.sum(ahead.astype(jnp.int32), axis=1)
    row, col = rank // PLANES, rank % PLANES
    plane = jnp.where(row % 2 == 1, PLANES - 1 - col, col)
    place = plane * PLANE_HEADS + row
    hit = (place[None, :] == ids[:, None]).astype(jnp.int32)
    head_at = jnp.sum(hit * ids[None, :], axis=1)
    work_at = jnp.sum(hit * work[None, :], axis=1)
    return head_at, work_at


def chip_plan(work_at):
    extra = CHIPS - PLANE_HEADS
    quota = (work_at[:, None].astype(jnp.float32) / jnp.arange(1, extra + 1).astype(jnp.float32)[None, :]).reshape(-1)
    ids = jnp.arange(quota.shape[0])
    ahead = (quota[None, :] > quota[:, None]) | ((quota[None, :] == quota[:, None]) & (ids[None, :] < ids[:, None]))
    won = (jnp.sum(ahead.astype(jnp.int32), axis=1) < extra).astype(jnp.int32)
    chips = 1 + jnp.sum(won.reshape(PLANE_HEADS, extra), axis=1)
    slots = jnp.arange(PLANE_HEADS)
    first = jnp.sum(jnp.where(slots[None, :] < slots[:, None], chips[None, :], 0), axis=1)
    return chips, first


def pack_kernel(heads, q_ref, k_ref, v_ref, out_ref, held, turned, sem_in, sem_out):
    rows = pl.ds(pl.multiple_of(heads[CHIPS] * HALF, HALF), HALF)
    loads, stores = [], []
    for t in range(CHIPS):
        cols = pl.ds(pl.multiple_of(heads[t] * TILE, TILE), TILE)
        for j, ref in enumerate((k_ref, v_ref, q_ref)):
            loads.append(pltpu.make_async_copy(ref.at[rows, cols], held.at[t, j], sem_in.at[t, j]))
            loads[-1].start()
    for t in range(CHIPS):
        for j in range(3):
            loads[3 * t + j].wait()
            source = held.at[t, j]
            if j == 1:
                for sub in range(2):
                    part = pl.ds(sub * TILE, TILE)
                    turned[t, part, :] = held[t, 1, part, :].T
                source = turned.at[t]
            stores.append(pltpu.make_async_copy(source, out_ref.at[t, j], sem_out.at[t, j]))
            stores[-1].start()
    for store in stores:
        store.wait()


def pack(queries, keys, values, chip_heads, core):
    scalars = jnp.concatenate([chip_heads, core[None]]).astype(jnp.int32)
    hbm = pl.BlockSpec(memory_space=pl.ANY)
    return pl.pallas_call(
        pack_kernel,
        in_specs=[pl.BlockSpec(memory_space=pltpu.SMEM)] + [hbm] * 3,
        out_specs=hbm,
        out_shape=jax.ShapeDtypeStruct((CHIPS, 3, HALF, TILE), jnp.bfloat16),
        scratch_shapes=[
            pltpu.VMEM((CHIPS, 3, HALF, TILE), jnp.bfloat16),
            pltpu.VMEM((CHIPS, HALF, TILE), jnp.bfloat16),
            pltpu.SemaphoreType.DMA((CHIPS, 3)),
            pltpu.SemaphoreType.DMA((CHIPS, 3)),
        ],
        compiler_params=pltpu.CompilerParams(vmem_limit_bytes=16 * 2**20),
    )(scalars, queries, keys, values)


def attend_kernel(scale, meta, q_of, k_of, valid_of, own_ref, other_ref, out_ref, kv_s, q_s, acc_s, max_s, sum_s, sems):
    core, sub = meta[0], meta[2]
    loads = [
        pltpu.make_async_copy(own_ref.at[:, pl.ds(0, 4)], kv_s.at[core], sems.at[0]),
        pltpu.make_async_copy(other_ref.at[:, pl.ds(0, 4)], kv_s.at[1 - core], sems.at[1]),
        pltpu.make_async_copy(own_ref.at[:, pl.ds(4 + sub, 1)], q_s, sems.at[2]),
    ]
    for load in loads:
        load.start()
    acc_s[...] = jnp.zeros_like(acc_s)
    sum_s[...] = jnp.zeros_like(sum_s)
    max_s[...] = jnp.full_like(max_s, LOW)
    for load in loads:
        load.wait()

    def body(step, _):
        parts = []
        for u in range(UNROLL):
            e = step * UNROLL + u
            t = q_of[e]
            kid = [k_of[e * GROUP + g] for g in range(GROUP)]
            valid = valid_of[e]
            keys = jnp.concatenate([kv_s[i // 64, i % 64 // 4, i % 4] for i in kid], axis=0)
            scores = lax.dot_general(keys, q_s[t, 0], (((1,), (1,)), ((), ())), preferred_element_type=jnp.float32)
            top = jnp.max(scores, axis=0, keepdims=True) * scale
            weights = []
            total = jnp.zeros((1, TILE), jnp.float32)
            for g in range(GROUP):
                shift = top + jnp.where(g < valid, 0.0, -LOW)
                w = jnp.exp2(scores[g * TILE : (g + 1) * TILE] * scale - shift)
                total = total + jnp.sum(w, axis=0, keepdims=True)
                weights.append(w.astype(jnp.bfloat16))
            vals = jnp.concatenate([kv_s[i // 64, i % 64 // 4, i % 4 + 2] for i in kid], axis=1)
            part = jnp.dot(vals, jnp.concatenate(weights, axis=0), preferred_element_type=jnp.float32)
            parts.append((t, top, total, part))
        for t, top, total, part in parts:
            old = max_s[t]
            new = jnp.maximum(old, top)
            a = jnp.exp2(old - new)
            b = jnp.exp2(top - new)
            max_s[t] = new
            sum_s[t] = sum_s[t] * a + total * b
            acc_s[t] = acc_s[t] * a + part * b
        return 0

    lax.fori_loop(0, meta[1], body, 0)

    def finish(t, _):
        inverse = 1.0 / jnp.maximum(sum_s[t], 1e-30)
        out_ref[t] = (acc_s[t] * inverse).astype(jnp.bfloat16)
        return 0

    lax.fori_loop(0, CHIPS, finish, 0)


def attend(meta, q_of, k_of, valid_of, own, other):
    smem = pl.BlockSpec(memory_space=pltpu.SMEM)
    hbm = pl.BlockSpec(memory_space=pl.ANY)
    return pl.pallas_call(
        functools.partial(attend_kernel, TILE**-0.5 * LOG2E),
        in_specs=[smem] * 4 + [hbm] * 2,
        out_specs=pl.BlockSpec(memory_space=pltpu.VMEM),
        out_shape=jax.ShapeDtypeStruct((CHIPS, TILE, TILE), jnp.bfloat16),
        scratch_shapes=[
            pltpu.VMEM((2, CHIPS, 4, TILE, TILE), jnp.bfloat16),
            pltpu.VMEM((CHIPS, 1, TILE, TILE), jnp.bfloat16),
            pltpu.VMEM((CHIPS, TILE, TILE), jnp.float32),
            pltpu.VMEM((CHIPS, 1, TILE), jnp.float32),
            pltpu.VMEM((CHIPS, 1, TILE), jnp.float32),
            pltpu.SemaphoreType.DMA((3,)),
        ],
        compiler_params=pltpu.CompilerParams(vmem_limit_bytes=40 * 2**20),
    )(meta, q_of, k_of, valid_of, own, other)


def item_lists(allowed, mine):
    tiles = allowed.shape[1]
    count = jnp.sum(allowed, axis=1) * mine
    groups = (count + GROUP - 1) // GROUP
    slots = jnp.arange(groups.shape[0])
    end = jnp.sum(jnp.where(slots[None, :] <= slots[:, None], groups[None, :], 0), axis=1)
    steps = (end[-1] + UNROLL - 1) // UNROLL
    key_ids = jnp.arange(tiles)
    before = jnp.sum(allowed[:, None, :] * (key_ids[None, :] < key_ids[:, None])[None].astype(jnp.int32), axis=2)
    held_at = (key_ids // 2 % 2) * 64 + key_ids // 4 * 4 + key_ids % 2
    listed = jnp.sum(
        jnp.where((before[:, :, None] == key_ids[None, None, :]) & (allowed[:, :, None] > 0), held_at[None, :, None], 0),
        axis=1,
    )
    item = jnp.arange(ITEMS)
    real = (item < end[-1]).astype(jnp.int32)
    held = jnp.maximum(jnp.minimum(item, end[-1] - 1), 0)
    q_of = jnp.minimum(jnp.sum((end[None, :] <= held[:, None]).astype(jnp.int32), axis=1), CHIPS - 1)
    pick = (q_of[:, None] == slots[None, :]).astype(jnp.int32)
    start = GROUP * (held - jnp.sum(pick * (end - groups)[None, :], axis=1))
    left = jnp.sum(pick * count[None, :], axis=1) - start
    rows = jnp.dot(pick.astype(jnp.float32), listed.astype(jnp.float32))
    offset = jnp.arange(GROUP)
    where = start[:, None] + jnp.where(offset[None, :] < left[:, None], offset[None, :], 0)
    k_of = jnp.sum(jnp.where(where[:, :, None] == key_ids[None, None, :], rows[:, None, :], 0.0), axis=2)
    valid = jnp.minimum(left, GROUP) * real
    return steps, q_of, k_of.astype(jnp.int32).reshape(-1), valid


def select_kernel(source, got_ref, out_ref):
    for i in range(PLANE_HEADS):
        out_ref[:, pl.ds(i * TILE, TILE)] = got_ref[source[i]].T


def select(source, got):
    vmem = pl.BlockSpec(memory_space=pltpu.VMEM)
    return pl.pallas_call(
        select_kernel,
        in_specs=[pl.BlockSpec(memory_space=pltpu.SMEM), vmem],
        out_specs=vmem,
        out_shape=jax.ShapeDtypeStruct((TILE, PLANE_HEADS * TILE), jnp.bfloat16),
    )(source, got)


def exchange(block):
    return lax.all_to_all(block, TOKENS_AXES, split_axis=0, concat_axis=0, tiled=True)


def along_y(block, step):
    return lax.ppermute(block, "y", [(i, (i + step) % PLANES) for i in range(PLANES)])


def swap(block):
    return lax.ppermute(block, "c", [(0, 1), (1, 0)])


def shards(residual_in, queries, keys, values, w_out, gate_scale, tile_mask):
    chip = lax.axis_index("x") * 4 + lax.axis_index("z")
    plane = lax.axis_index("y")
    core = lax.axis_index("c")
    tile_work = jnp.sum(tile_mask, axis=2)
    head_at, work_at = head_plan(jnp.sum(tile_work, axis=1))
    plane_heads = lax.dynamic_slice_in_dim(head_at, plane * PLANE_HEADS, PLANE_HEADS)
    chips, first = chip_plan(lax.dynamic_slice_in_dim(work_at, plane * PLANE_HEADS, PLANE_HEADS))
    chip_ids = jnp.arange(CHIPS)
    on_chip = (first[None, :] <= chip_ids[:, None]) & (chip_ids[:, None] < (first + chips)[None, :])
    chip_heads = jnp.sum(jnp.where(on_chip, plane_heads[None, :], 0), axis=1)
    got = exchange(pack(queries, keys, values, chip_heads, core)).reshape(CHIPS, 6, TILE, TILE)

    half_work = lax.dynamic_index_in_dim(tile_work.reshape(HEADS, CHIPS, 2, 2), core, 2, keepdims=False)
    half_work = jnp.take(half_work.reshape(HEADS, 2 * CHIPS), plane_heads, axis=0, mode="clip")
    tile_ids = jnp.arange(2 * CHIPS)
    done = jnp.sum(
        jnp.where((tile_ids[None, :] < tile_ids[:, None])[None], half_work[:, None, :], 0), axis=2
    )
    total = jnp.sum(half_work, axis=1, keepdims=True)
    owner = first[:, None] + ((2 * done + half_work) * chips[:, None]) // (2 * total)
    my_slot = jnp.sum(jnp.where(on_chip[chip], jnp.arange(PLANE_HEADS), 0))
    my_head = chip_heads[chip]
    mine_tiles = (owner[my_slot] == chip).astype(jnp.int32).reshape(CHIPS, 2)
    allowed = lax.dynamic_index_in_dim(tile_mask, my_head, 0, keepdims=False)
    allowed = lax.dynamic_index_in_dim(allowed.reshape(CHIPS, 2, 2, 4 * CHIPS), core, 1, keepdims=False)
    source = lax.dynamic_slice_in_dim(owner, 2 * chip, 2, 1)

    w_heads = w_out.reshape(HEADS, TILE, w_out.shape[1])
    weights = []
    for ahead in (0, 3, 1, 2):
        w_order = lax.dynamic_slice_in_dim(head_at, (plane + ahead) % PLANES * PLANE_HEADS, PLANE_HEADS)
        weights.append(jnp.take(w_heads, w_order, axis=0, mode="clip").reshape(PLANE_HEADS * TILE, -1))
    lists = [item_lists(allowed[:, sub], mine_tiles[:, sub]) for sub in range(2)]
    got, lists, weights = lax.optimization_barrier((got, lists, weights))
    got_other = swap(got)

    halves = []
    for sub in range(2):
        steps, q_of, k_of, valid = lists[sub]
        meta = jnp.stack([core, steps, jnp.int32(sub)]).astype(jnp.int32)
        attended = attend(meta, q_of, k_of, valid, got, got_other)
        own = select(source[:, sub], exchange(attended))
        blocks = [own, along_y(own, 1), along_y(own, 3), along_y(own, 2)]
        total = jnp.zeros((2 * TILE, w_out.shape[1]), jnp.float32)
        for k, block in enumerate(blocks):
            both = jnp.concatenate([block, swap(block)], axis=0)
            total = total + jnp.dot(both, weights[k], preferred_element_type=jnp.float32)
        halves.append(total.reshape(2, TILE, -1))
    mine, theirs = (jnp.concatenate([halves[0][i], halves[1][i]], axis=0) for i in range(2))
    low = jnp.where(core == 0, mine, theirs)
    high = jnp.where(core == 0, theirs, mine)
    projected = jnp.concatenate([low, high], axis=0)
    return (residual_in.astype(jnp.float32) + gate_scale * projected).astype(jnp.bfloat16)


def solution(mesh):
    fine = Mesh(mesh.devices.reshape(4, 4, 4, 2), ("x", "z", "y", "c"))
    seq, rep = TOKENS_AXES, ("y", "c")
    in_specs = (
        P(seq, rep),
        P(seq, None),
        P(seq, None),
        P(seq, None),
        P(None, rep),
        P(rep),
        P(),
    )
    return jax.shard_map(shards, mesh=fine, in_specs=in_specs, out_specs=P(seq, rep), check_vma=False)
```

```python
import functools

import jax
import jax.numpy as jnp
from jax import lax
from jax.experimental import pallas as pl
from jax.experimental.pallas import tpu as pltpu
from jax.sharding import Mesh
from jax.sharding import PartitionSpec as P

TILE = 128
HEADS = 40
PLANES = 4
PLANE_HEADS = HEADS // PLANES
CHIPS = 16
HALF = 256
GROUP = 4
UNROLL = 16
ITEMS = 256
LOG2E = 1.4426950408889634
TOKENS_AXES = ("x", "z")
LOW = -1e30


def head_plan(work):
    ids = jnp.arange(HEADS)
    ahead = (work[None, :] > work[:, None]) | ((work[None, :] == work[:, None]) & (ids[None, :] < ids[:, None]))
    rank = jnp.sum(ahead.astype(jnp.int32), axis=1)
    row, col = rank // PLANES, rank % PLANES
    plane = jnp.where(row % 2 == 1, PLANES - 1 - col, col)
    place = plane * PLANE_HEADS + row
    hit = (place[None, :] == ids[:, None]).astype(jnp.int32)
    head_at = jnp.sum(hit * ids[None, :], axis=1)
    work_at = jnp.sum(hit * work[None, :], axis=1)
    return head_at, work_at


def chip_plan(work_at):
    extra = CHIPS - PLANE_HEADS
    quota = (work_at[:, None].astype(jnp.float32) / jnp.arange(1, extra + 1).astype(jnp.float32)[None, :]).reshape(-1)
    ids = jnp.arange(quota.shape[0])
    ahead = (quota[None, :] > quota[:, None]) | ((quota[None, :] == quota[:, None]) & (ids[None, :] < ids[:, None]))
    won = (jnp.sum(ahead.astype(jnp.int32), axis=1) < extra).astype(jnp.int32)
    chips = 1 + jnp.sum(won.reshape(PLANE_HEADS, extra), axis=1)
    slots = jnp.arange(PLANE_HEADS)
    first = jnp.sum(jnp.where(slots[None, :] < slots[:, None], chips[None, :], 0), axis=1)
    return chips, first


def pack_kernel(heads, q_ref, k_ref, v_ref, out_ref, held, turned, sem_in, sem_out):
    rows = pl.ds(pl.multiple_of(heads[CHIPS] * HALF, HALF), HALF)
    loads, stores = [], []
    for t in range(CHIPS):
        cols = pl.ds(pl.multiple_of(heads[t] * TILE, TILE), TILE)
        for j, ref in enumerate((k_ref, v_ref, q_ref)):
            loads.append(pltpu.make_async_copy(ref.at[rows, cols], held.at[t, j], sem_in.at[t, j]))
            loads[-1].start()
    for t in range(CHIPS):
        for j in range(3):
            loads[3 * t + j].wait()
            source = held.at[t, j]
            if j == 1:
                for sub in range(2):
                    part = pl.ds(sub * TILE, TILE)
                    turned[t, part, :] = held[t, 1, part, :].T
                source = turned.at[t]
            stores.append(pltpu.make_async_copy(source, out_ref.at[t, j], sem_out.at[t, j]))
            stores[-1].start()
    for store in stores:
        store.wait()


def pack(queries, keys, values, chip_heads, core):
    scalars = jnp.concatenate([chip_heads, core[None]]).astype(jnp.int32)
    hbm = pl.BlockSpec(memory_space=pl.ANY)
    return pl.pallas_call(
        pack_kernel,
        in_specs=[pl.BlockSpec(memory_space=pltpu.SMEM)] + [hbm] * 3,
        out_specs=hbm,
        out_shape=jax.ShapeDtypeStruct((CHIPS, 3, HALF, TILE), jnp.bfloat16),
        scratch_shapes=[
            pltpu.VMEM((CHIPS, 3, HALF, TILE), jnp.bfloat16),
            pltpu.VMEM((CHIPS, HALF, TILE), jnp.bfloat16),
            pltpu.SemaphoreType.DMA((CHIPS, 3)),
            pltpu.SemaphoreType.DMA((CHIPS, 3)),
        ],
        compiler_params=pltpu.CompilerParams(vmem_limit_bytes=60 * 2**20),
    )(scalars, queries, keys, values)


def attend_kernel(scale, meta, q_of, k_of, valid_of, own_ref, other_ref, out_ref, kv_s, q_s, acc_s, max_s, sum_s, sems):
    core, sub = meta[0], meta[2]
    loads = [
        pltpu.make_async_copy(own_ref.at[:, pl.ds(0, 4)], kv_s.at[core], sems.at[0]),
        pltpu.make_async_copy(other_ref.at[:, pl.ds(0, 4)], kv_s.at[1 - core], sems.at[1]),
        pltpu.make_async_copy(own_ref.at[:, pl.ds(4 + sub, 1)], q_s, sems.at[2]),
    ]
    for load in loads:
        load.start()
    acc_s[...] = jnp.zeros_like(acc_s)
    sum_s[...] = jnp.zeros_like(sum_s)
    max_s[...] = jnp.full_like(max_s, LOW)
    for load in loads:
        load.wait()

    def body(step, _):
        parts = []
        for u in range(UNROLL):
            e = step * UNROLL + u
            t = q_of[e]
            kid = [k_of[e * GROUP + g] for g in range(GROUP)]
            valid = valid_of[e]
            keys = jnp.concatenate([kv_s[i // 64, i % 64 // 4, i % 4] for i in kid], axis=0)
            scores = lax.dot_general(keys, q_s[t, 0], (((1,), (1,)), ((), ())), preferred_element_type=jnp.float32)
            top = jnp.max(scores, axis=0, keepdims=True) * scale
            weights = []
            total = jnp.zeros((1, TILE), jnp.float32)
            for g in range(GROUP):
                shift = top + jnp.where(g < valid, 0.0, -LOW)
                w = jnp.exp2(scores[g * TILE : (g + 1) * TILE] * scale - shift)
                total = total + jnp.sum(w, axis=0, keepdims=True)
                weights.append(w.astype(jnp.bfloat16))
            vals = jnp.concatenate([kv_s[i // 64, i % 64 // 4, i % 4 + 2] for i in kid], axis=1)
            part = jnp.dot(vals, jnp.concatenate(weights, axis=0), preferred_element_type=jnp.float32)
            parts.append((t, top, total, part))
        for t, top, total, part in parts:
            old = max_s[t]
            new = jnp.maximum(old, top)
            a = jnp.exp2(old - new)
            b = jnp.exp2(top - new)
            max_s[t] = new
            sum_s[t] = sum_s[t] * a + total * b
            acc_s[t] = acc_s[t] * a + part * b
        return 0

    lax.fori_loop(0, meta[1], body, 0)

    def finish(t, _):
        inverse = 1.0 / jnp.maximum(sum_s[t], 1e-30)
        out_ref[t] = (acc_s[t] * inverse).astype(jnp.bfloat16)
        return 0

    lax.fori_loop(0, CHIPS, finish, 0)


def attend(meta, q_of, k_of, valid_of, own, other):
    smem = pl.BlockSpec(memory_space=pltpu.SMEM)
    hbm = pl.BlockSpec(memory_space=pl.ANY)
    return pl.pallas_call(
        functools.partial(attend_kernel, TILE**-0.5 * LOG2E),
        in_specs=[smem] * 4 + [hbm] * 2,
        out_specs=pl.BlockSpec(memory_space=pltpu.VMEM),
        out_shape=jax.ShapeDtypeStruct((CHIPS, TILE, TILE), jnp.bfloat16),
        scratch_shapes=[
            pltpu.VMEM((2, CHIPS, 4, TILE, TILE), jnp.bfloat16),
            pltpu.VMEM((CHIPS, 1, TILE, TILE), jnp.bfloat16),
            pltpu.VMEM((CHIPS, TILE, TILE), jnp.float32),
            pltpu.VMEM((CHIPS, 1, TILE), jnp.float32),
            pltpu.VMEM((CHIPS, 1, TILE), jnp.float32),
            pltpu.SemaphoreType.DMA((3,)),
        ],
        compiler_params=pltpu.CompilerParams(vmem_limit_bytes=60 * 2**20),
    )(meta, q_of, k_of, valid_of, own, other)


def item_lists(allowed, mine):
    tiles = allowed.shape[1]
    count = jnp.sum(allowed, axis=1) * mine
    groups = (count + GROUP - 1) // GROUP
    slots = jnp.arange(groups.shape[0])
    end = jnp.sum(jnp.where(slots[None, :] <= slots[:, None], groups[None, :], 0), axis=1)
    steps = (end[-1] + UNROLL - 1) // UNROLL
    key_ids = jnp.arange(tiles)
    before = jnp.sum(allowed[:, None, :] * (key_ids[None, :] < key_ids[:, None])[None].astype(jnp.int32), axis=2)
    held_at = (key_ids // 2 % 2) * 64 + key_ids // 4 * 4 + key_ids % 2
    listed = jnp.sum(
        jnp.where((before[:, :, None] == key_ids[None, None, :]) & (allowed[:, :, None] > 0), held_at[None, :, None], 0),
        axis=1,
    )
    item = jnp.arange(ITEMS)
    real = (item < end[-1]).astype(jnp.int32)
    held = jnp.maximum(jnp.minimum(item, end[-1] - 1), 0)
    q_of = jnp.minimum(jnp.sum((end[None, :] <= held[:, None]).astype(jnp.int32), axis=1), CHIPS - 1)
    pick = (q_of[:, None] == slots[None, :]).astype(jnp.int32)
    start = GROUP * (held - jnp.sum(pick * (end - groups)[None, :], axis=1))
    left = jnp.sum(pick * count[None, :], axis=1) - start
    rows = jnp.dot(pick.astype(jnp.float32), listed.astype(jnp.float32))
    offset = jnp.arange(GROUP)
    where = start[:, None] + jnp.where(offset[None, :] < left[:, None], offset[None, :], 0)
    k_of = jnp.sum(jnp.where(where[:, :, None] == key_ids[None, None, :], rows[:, None, :], 0.0), axis=2)
    valid = jnp.minimum(left, GROUP) * real
    return steps, q_of, k_of.astype(jnp.int32).reshape(-1), valid


def select_kernel(source, got_ref, out_ref):
    for i in range(PLANE_HEADS):
        out_ref[:, pl.ds(i * TILE, TILE)] = got_ref[source[i]].T


def select(source, got):
    vmem = pl.BlockSpec(memory_space=pltpu.VMEM)
    return pl.pallas_call(
        select_kernel,
        in_specs=[pl.BlockSpec(memory_space=pltpu.SMEM), vmem],
        out_specs=vmem,
        out_shape=jax.ShapeDtypeStruct((TILE, PLANE_HEADS * TILE), jnp.bfloat16),
    )(source, got)


def exchange(block):
    return lax.all_to_all(block, TOKENS_AXES, split_axis=0, concat_axis=0, tiled=True)


def along_y(block, step):
    return lax.ppermute(block, "y", [(i, (i + step) % PLANES) for i in range(PLANES)])


def swap(block):
    return lax.ppermute(block, "c", [(0, 1), (1, 0)])


def shards(residual_in, queries, keys, values, w_out, gate_scale, tile_mask):
    chip = lax.axis_index("x") * 4 + lax.axis_index("z")
    plane = lax.axis_index("y")
    core = lax.axis_index("c")
    tile_work = jnp.sum(tile_mask, axis=2)
    head_at, work_at = head_plan(jnp.sum(tile_work, axis=1))
    plane_heads = lax.dynamic_slice_in_dim(head_at, plane * PLANE_HEADS, PLANE_HEADS)
    chips, first = chip_plan(lax.dynamic_slice_in_dim(work_at, plane * PLANE_HEADS, PLANE_HEADS))
    chip_ids = jnp.arange(CHIPS)
    on_chip = (first[None, :] <= chip_ids[:, None]) & (chip_ids[:, None] < (first + chips)[None, :])
    chip_heads = jnp.sum(jnp.where(on_chip, plane_heads[None, :], 0), axis=1)
    got = exchange(pack(queries, keys, values, chip_heads, core)).reshape(CHIPS, 6, TILE, TILE)

    half_work = lax.dynamic_index_in_dim(tile_work.reshape(HEADS, CHIPS, 2, 2), core, 2, keepdims=False)
    half_work = jnp.take(half_work.reshape(HEADS, 2 * CHIPS), plane_heads, axis=0, mode="clip")
    tile_ids = jnp.arange(2 * CHIPS)
    done = jnp.sum(
        jnp.where((tile_ids[None, :] < tile_ids[:, None])[None], half_work[:, None, :], 0), axis=2
    )
    total = jnp.sum(half_work, axis=1, keepdims=True)
    owner = first[:, None] + ((2 * done + half_work) * chips[:, None]) // (2 * total)
    my_slot = jnp.sum(jnp.where(on_chip[chip], jnp.arange(PLANE_HEADS), 0))
    my_head = chip_heads[chip]
    mine_tiles = (owner[my_slot] == chip).astype(jnp.int32).reshape(CHIPS, 2)
    allowed = lax.dynamic_index_in_dim(tile_mask, my_head, 0, keepdims=False)
    allowed = lax.dynamic_index_in_dim(allowed.reshape(CHIPS, 2, 2, 4 * CHIPS), core, 1, keepdims=False)
    source = lax.dynamic_slice_in_dim(owner, 2 * chip, 2, 1)

    w_heads = w_out.reshape(HEADS, TILE, w_out.shape[1])
    weights = []
    for ahead in (0, 3, 1, 2):
        w_order = lax.dynamic_slice_in_dim(head_at, (plane + ahead) % PLANES * PLANE_HEADS, PLANE_HEADS)
        weights.append(jnp.take(w_heads, w_order, axis=0, mode="clip").reshape(PLANE_HEADS * TILE, -1))
    lists = [item_lists(allowed[:, sub], mine_tiles[:, sub]) for sub in range(2)]
    got, lists, weights = lax.optimization_barrier((got, lists, weights))
    got_other = swap(got)

    halves = []
    for sub in range(2):
        steps, q_of, k_of, valid = lists[sub]
        meta = jnp.stack([core, steps, jnp.int32(sub)]).astype(jnp.int32)
        attended = attend(meta, q_of, k_of, valid, got, got_other)
        own = select(source[:, sub], exchange(attended))
        blocks = [own, along_y(own, 1), along_y(own, 3), along_y(own, 2)]
        total = jnp.zeros((2 * TILE, w_out.shape[1]), jnp.float32)
        for k, block in enumerate(blocks):
            both = jnp.concatenate([block, swap(block)], axis=0)
            total = total + jnp.dot(both, weights[k], preferred_element_type=jnp.float32)
        halves.append(total.reshape(2, TILE, -1))
    mine, theirs = (jnp.concatenate([halves[0][i], halves[1][i]], axis=0) for i in range(2))
    low = jnp.where(core == 0, mine, theirs)
    high = jnp.where(core == 0, theirs, mine)
    projected = jnp.concatenate([low, high], axis=0)
    return (residual_in.astype(jnp.float32) + gate_scale * projected).astype(jnp.bfloat16)


def solution(mesh):
    fine = Mesh(mesh.devices.reshape(4, 4, 4, 2), ("x", "z", "y", "c"))
    seq, rep = TOKENS_AXES, ("y", "c")
    in_specs = (
        P(seq, rep),
        P(seq, None),
        P(seq, None),
        P(seq, None),
        P(None, rep),
        P(rep),
        P(),
    )
    return jax.shard_map(shards, mesh=fine, in_specs=in_specs, out_specs=P(seq, rep), check_vma=False)
```

```python
import functools

import jax
import jax.numpy as jnp
from jax import lax
from jax.experimental import pallas as pl
from jax.experimental.pallas import tpu as pltpu
from jax.sharding import Mesh
from jax.sharding import PartitionSpec as P

TILE = 128
HEADS = 40
PLANES = 4
PLANE_HEADS = HEADS // PLANES
CHIPS = 16
HALF = 256
GROUP = 4
UNROLL = 16
ITEMS = 256
LOG2E = 1.4426950408889634
TOKENS_AXES = ("x", "z")
LOW = -1e30


def head_plan(work):
    ids = jnp.arange(HEADS)
    ahead = (work[None, :] > work[:, None]) | ((work[None, :] == work[:, None]) & (ids[None, :] < ids[:, None]))
    rank = jnp.sum(ahead.astype(jnp.int32), axis=1)
    row, col = rank // PLANES, rank % PLANES
    plane = jnp.where(row % 2 == 1, PLANES - 1 - col, col)
    place = plane * PLANE_HEADS + row
    hit = (place[None, :] == ids[:, None]).astype(jnp.int32)
    head_at = jnp.sum(hit * ids[None, :], axis=1)
    work_at = jnp.sum(hit * work[None, :], axis=1)
    return head_at, work_at


def chip_plan(work_at):
    extra = CHIPS - PLANE_HEADS
    quota = (work_at[:, None].astype(jnp.float32) / jnp.arange(1, extra + 1).astype(jnp.float32)[None, :]).reshape(-1)
    ids = jnp.arange(quota.shape[0])
    ahead = (quota[None, :] > quota[:, None]) | ((quota[None, :] == quota[:, None]) & (ids[None, :] < ids[:, None]))
    won = (jnp.sum(ahead.astype(jnp.int32), axis=1) < extra).astype(jnp.int32)
    chips = 1 + jnp.sum(won.reshape(PLANE_HEADS, extra), axis=1)
    slots = jnp.arange(PLANE_HEADS)
    first = jnp.sum(jnp.where(slots[None, :] < slots[:, None], chips[None, :], 0), axis=1)
    return chips, first


def pack_kernel(heads, q_ref, k_ref, v_ref, first_ref, second_ref, held, turned, sem_in, sem_out):
    start = pl.multiple_of(heads[CHIPS] * HALF, HALF)
    rows = pl.ds(start, HALF)
    loads, stores = [], []
    for t in range(CHIPS):
        cols = pl.ds(pl.multiple_of(heads[t] * TILE, TILE), TILE)
        loads.append(
            [
                pltpu.make_async_copy(k_ref.at[rows, cols], held.at[t, pl.ds(0, HALF)], sem_in.at[t, 0]),
                pltpu.make_async_copy(v_ref.at[rows, cols], held.at[t, pl.ds(HALF, HALF)], sem_in.at[t, 1]),
                pltpu.make_async_copy(q_ref.at[rows, cols], held.at[t, pl.ds(2 * HALF, HALF)], sem_in.at[t, 2]),
            ]
        )
        for load in loads[-1]:
            load.start()
    for t in range(CHIPS):
        for load in loads[t]:
            load.wait()
        for sub in range(2):
            part = pl.ds(sub * TILE, TILE)
            turned[t, part, :] = held[t, pl.ds(HALF + sub * TILE, TILE), :].T
        stores += [
            pltpu.make_async_copy(held.at[t, pl.ds(0, HALF)], first_ref.at[t, pl.ds(0, HALF)], sem_out.at[t, 0]),
            pltpu.make_async_copy(turned.at[t], first_ref.at[t, pl.ds(HALF, HALF)], sem_out.at[t, 1]),
            pltpu.make_async_copy(
                held.at[t, pl.ds(2 * HALF, TILE)], first_ref.at[t, pl.ds(2 * HALF, TILE)], sem_out.at[t, 2]
            ),
            pltpu.make_async_copy(held.at[t, pl.ds(2 * HALF + TILE, TILE)], second_ref.at[t], sem_out.at[t, 3]),
        ]
        for store in stores[-4:]:
            store.start()
    for store in stores:
        store.wait()


def pack(queries, keys, values, chip_heads, core):
    scalars = jnp.concatenate([chip_heads, core[None]]).astype(jnp.int32)
    hbm = pl.BlockSpec(memory_space=pl.ANY)
    return pl.pallas_call(
        pack_kernel,
        in_specs=[pl.BlockSpec(memory_space=pltpu.SMEM)] + [hbm] * 3,
        out_specs=[hbm, hbm],
        out_shape=[
            jax.ShapeDtypeStruct((CHIPS, 5 * TILE, TILE), jnp.bfloat16),
            jax.ShapeDtypeStruct((CHIPS, TILE, TILE), jnp.bfloat16),
        ],
        scratch_shapes=[
            pltpu.VMEM((CHIPS, 3 * HALF, TILE), jnp.bfloat16),
            pltpu.VMEM((CHIPS, HALF, TILE), jnp.bfloat16),
            pltpu.SemaphoreType.DMA((CHIPS, 3)),
            pltpu.SemaphoreType.DMA((CHIPS, 4)),
        ],
        compiler_params=pltpu.CompilerParams(vmem_limit_bytes=60 * 2**20),
    )(scalars, queries, keys, values)


def attend_kernel(
    scale, query_at, meta, q_of, k_of, valid_of, own_ref, other_ref, query_ref, out_ref, kv_s, q_s, acc_s, max_s, sum_s, sems
):
    core = meta[0]
    loads = [
        pltpu.make_async_copy(own_ref.at[:, pl.ds(0, 4)], kv_s.at[core], sems.at[0]),
        pltpu.make_async_copy(other_ref.at[:, pl.ds(0, 4)], kv_s.at[1 - core], sems.at[1]),
        pltpu.make_async_copy(query_ref.at[:, pl.ds(query_at, 1)], q_s, sems.at[2]),
    ]
    for load in loads:
        load.start()
    acc_s[...] = jnp.zeros_like(acc_s)
    sum_s[...] = jnp.zeros_like(sum_s)
    max_s[...] = jnp.full_like(max_s, LOW)
    for load in loads:
        load.wait()

    def body(step, _):
        parts = []
        for u in range(UNROLL):
            e = step * UNROLL + u
            t = q_of[e]
            kid = [k_of[e * GROUP + g] for g in range(GROUP)]
            valid = valid_of[e]
            keys = jnp.concatenate([kv_s[i // 64, i % 64 // 4, i % 4] for i in kid], axis=0)
            scores = lax.dot_general(keys, q_s[t, 0], (((1,), (1,)), ((), ())), preferred_element_type=jnp.float32)
            top = jnp.max(scores, axis=0, keepdims=True) * scale
            weights = []
            total = jnp.zeros((1, TILE), jnp.float32)
            for g in range(GROUP):
                shift = top + jnp.where(g < valid, 0.0, -LOW)
                w = jnp.exp2(scores[g * TILE : (g + 1) * TILE] * scale - shift)
                total = total + jnp.sum(w, axis=0, keepdims=True)
                weights.append(w.astype(jnp.bfloat16))
            vals = jnp.concatenate([kv_s[i // 64, i % 64 // 4, i % 4 + 2] for i in kid], axis=1)
            part = jnp.dot(vals, jnp.concatenate(weights, axis=0), preferred_element_type=jnp.float32)
            parts.append((t, top, total, part))
        for t, top, total, part in parts:
            old = max_s[t]
            new = jnp.maximum(old, top)
            a = jnp.exp2(old - new)
            b = jnp.exp2(top - new)
            max_s[t] = new
            sum_s[t] = sum_s[t] * a + total * b
            acc_s[t] = acc_s[t] * a + part * b
        return 0

    lax.fori_loop(0, meta[1], body, 0)

    def finish(t, _):
        inverse = 1.0 / jnp.maximum(sum_s[t], 1e-30)
        out_ref[t] = (acc_s[t] * inverse).astype(jnp.bfloat16)
        return 0

    lax.fori_loop(0, CHIPS, finish, 0)


def attend(query_at, meta, q_of, k_of, valid_of, own, other, query):
    smem = pl.BlockSpec(memory_space=pltpu.SMEM)
    hbm = pl.BlockSpec(memory_space=pl.ANY)
    return pl.pallas_call(
        functools.partial(attend_kernel, TILE**-0.5 * LOG2E, query_at),
        in_specs=[smem] * 4 + [hbm] * 3,
        out_specs=pl.BlockSpec(memory_space=pltpu.VMEM),
        out_shape=jax.ShapeDtypeStruct((CHIPS, TILE, TILE), jnp.bfloat16),
        scratch_shapes=[
            pltpu.VMEM((2, CHIPS, 4, TILE, TILE), jnp.bfloat16),
            pltpu.VMEM((CHIPS, 1, TILE, TILE), jnp.bfloat16),
            pltpu.VMEM((CHIPS, TILE, TILE), jnp.float32),
            pltpu.VMEM((CHIPS, 1, TILE), jnp.float32),
            pltpu.VMEM((CHIPS, 1, TILE), jnp.float32),
            pltpu.SemaphoreType.DMA((3,)),
        ],
        compiler_params=pltpu.CompilerParams(vmem_limit_bytes=24 * 2**20),
    )(meta, q_of, k_of, valid_of, own, other, query)


def item_lists(allowed, mine):
    tiles = allowed.shape[1]
    count = jnp.sum(allowed, axis=1) * mine
    groups = (count + GROUP - 1) // GROUP
    slots = jnp.arange(groups.shape[0])
    end = jnp.sum(jnp.where(slots[None, :] <= slots[:, None], groups[None, :], 0), axis=1)
    steps = (end[-1] + UNROLL - 1) // UNROLL
    key_ids = jnp.arange(tiles)
    before = jnp.sum(allowed[:, None, :] * (key_ids[None, :] < key_ids[:, None])[None].astype(jnp.int32), axis=2)
    held_at = (key_ids // 2 % 2) * 64 + key_ids // 4 * 4 + key_ids % 2
    listed = jnp.sum(
        jnp.where((before[:, :, None] == key_ids[None, None, :]) & (allowed[:, :, None] > 0), held_at[None, :, None], 0),
        axis=1,
    )
    item = jnp.arange(ITEMS)
    real = (item < end[-1]).astype(jnp.int32)
    held = jnp.maximum(jnp.minimum(item, end[-1] - 1), 0)
    q_of = jnp.minimum(jnp.sum((end[None, :] <= held[:, None]).astype(jnp.int32), axis=1), CHIPS - 1)
    pick = (q_of[:, None] == slots[None, :]).astype(jnp.int32)
    start = GROUP * (held - jnp.sum(pick * (end - groups)[None, :], axis=1))
    left = jnp.sum(pick * count[None, :], axis=1) - start
    rows = jnp.dot(pick.astype(jnp.float32), listed.astype(jnp.float32))
    offset = jnp.arange(GROUP)
    where = start[:, None] + jnp.where(offset[None, :] < left[:, None], offset[None, :], 0)
    k_of = jnp.sum(jnp.where(where[:, :, None] == key_ids[None, None, :], rows[:, None, :], 0.0), axis=2)
    valid = jnp.minimum(left, GROUP) * real
    return steps, q_of, k_of.astype(jnp.int32).reshape(-1), valid


def select_kernel(source, got_ref, out_ref):
    for i in range(PLANE_HEADS):
        out_ref[:, pl.ds(i * TILE, TILE)] = got_ref[source[i]].T


def select(source, got):
    vmem = pl.BlockSpec(memory_space=pltpu.VMEM)
    return pl.pallas_call(
        select_kernel,
        in_specs=[pl.BlockSpec(memory_space=pltpu.SMEM), vmem],
        out_specs=vmem,
        out_shape=jax.ShapeDtypeStruct((TILE, PLANE_HEADS * TILE), jnp.bfloat16),
    )(source, got)


def exchange(block):
    return lax.all_to_all(block, TOKENS_AXES, split_axis=0, concat_axis=0, tiled=True)


def along_y(block, step):
    return lax.ppermute(block, "y", [(i, (i + step) % PLANES) for i in range(PLANES)])


def swap(block):
    return lax.ppermute(block, "c", [(0, 1), (1, 0)])


def shards(residual_in, queries, keys, values, w_out, gate_scale, tile_mask):
    chip = lax.axis_index("x") * 4 + lax.axis_index("z")
    plane = lax.axis_index("y")
    core = lax.axis_index("c")
    tile_work = jnp.sum(tile_mask, axis=2)
    head_at, work_at = head_plan(jnp.sum(tile_work, axis=1))
    plane_heads = lax.dynamic_slice_in_dim(head_at, plane * PLANE_HEADS, PLANE_HEADS)
    chips, first = chip_plan(lax.dynamic_slice_in_dim(work_at, plane * PLANE_HEADS, PLANE_HEADS))
    chip_ids = jnp.arange(CHIPS)
    on_chip = (first[None, :] <= chip_ids[:, None]) & (chip_ids[:, None] < (first + chips)[None, :])
    chip_heads = jnp.sum(jnp.where(on_chip, plane_heads[None, :], 0), axis=1)
    first_send, second_send = pack(queries, keys, values, chip_heads, core)
    got = exchange(first_send).reshape(CHIPS, 5, TILE, TILE)

    half_work = lax.dynamic_index_in_dim(tile_work.reshape(HEADS, CHIPS, 2, 2), core, 2, keepdims=False)
    half_work = jnp.take(half_work.reshape(HEADS, 2 * CHIPS), plane_heads, axis=0, mode="clip")
    tile_ids = jnp.arange(2 * CHIPS)
    done = jnp.sum(
        jnp.where((tile_ids[None, :] < tile_ids[:, None])[None], half_work[:, None, :], 0), axis=2
    )
    total = jnp.sum(half_work, axis=1, keepdims=True)
    owner = first[:, None] + ((2 * done + half_work) * chips[:, None]) // (2 * total)
    my_slot = jnp.sum(jnp.where(on_chip[chip], jnp.arange(PLANE_HEADS), 0))
    my_head = chip_heads[chip]
    mine_tiles = (owner[my_slot] == chip).astype(jnp.int32).reshape(CHIPS, 2)
    allowed = lax.dynamic_index_in_dim(tile_mask, my_head, 0, keepdims=False)
    allowed = lax.dynamic_index_in_dim(allowed.reshape(CHIPS, 2, 2, 4 * CHIPS), core, 1, keepdims=False)
    source = lax.dynamic_slice_in_dim(owner, 2 * chip, 2, 1)

    w_heads = w_out.reshape(HEADS, TILE, w_out.shape[1])
    weights = []
    for ahead in (0, 3, 1, 2):
        w_order = lax.dynamic_slice_in_dim(head_at, (plane + ahead) % PLANES * PLANE_HEADS, PLANE_HEADS)
        weights.append(jnp.take(w_heads, w_order, axis=0, mode="clip").reshape(PLANE_HEADS * TILE, -1))
    lists = [item_lists(allowed[:, sub], mine_tiles[:, sub]) for sub in range(2)]
    got, lists, weights, second_send = lax.optimization_barrier((got, lists, weights, second_send))
    got_other = swap(got)
    late = exchange(second_send).reshape(CHIPS, 1, TILE, TILE)

    halves = []
    for sub in range(2):
        steps, q_of, k_of, valid = lists[sub]
        meta = jnp.stack([core, steps]).astype(jnp.int32)
        query_at, query = ((4, got), (0, late))[sub]
        attended = attend(query_at, meta, q_of, k_of, valid, got, got_other, query)
        own = select(source[:, sub], exchange(attended))
        blocks = [own, along_y(own, 1), along_y(own, 3), along_y(own, 2)]
        total = jnp.zeros((2 * TILE, w_out.shape[1]), jnp.float32)
        for k, block in enumerate(blocks):
            both = jnp.concatenate([block, swap(block)], axis=0)
            total = total + jnp.dot(both, weights[k], preferred_element_type=jnp.float32)
        halves.append(total.reshape(2, TILE, -1))
    mine, theirs = (jnp.concatenate([halves[0][i], halves[1][i]], axis=0) for i in range(2))
    low = jnp.where(core == 0, mine, theirs)
    high = jnp.where(core == 0, theirs, mine)
    projected = jnp.concatenate([low, high], axis=0)
    return (residual_in.astype(jnp.float32) + gate_scale * projected).astype(jnp.bfloat16)


def solution(mesh):
    fine = Mesh(mesh.devices.reshape(4, 4, 4, 2), ("x", "z", "y", "c"))
    seq, rep = TOKENS_AXES, ("y", "c")
    in_specs = (
        P(seq, rep),
        P(seq, None),
        P(seq, None),
        P(seq, None),
        P(None, rep),
        P(rep),
        P(),
    )
    return jax.shard_map(shards, mesh=fine, in_specs=in_specs, out_specs=P(seq, rep), check_vma=False)
```

```python
import functools

import jax
import jax.numpy as jnp
from jax import lax
from jax.experimental import pallas as pl
from jax.experimental.pallas import tpu as pltpu
from jax.sharding import Mesh
from jax.sharding import PartitionSpec as P

TILE = 128
HEADS = 40
PLANES = 4
PLANE_HEADS = HEADS // PLANES
CHIPS = 16
HALF = 256
GROUP = 4
UNROLL = 16
ITEMS = 256
LOG2E = 1.4426950408889634
TOKENS_AXES = ("x", "z")
LOW = -1e30


def head_plan(work):
    ids = jnp.arange(HEADS)
    ahead = (work[None, :] > work[:, None]) | ((work[None, :] == work[:, None]) & (ids[None, :] < ids[:, None]))
    rank = jnp.sum(ahead.astype(jnp.int32), axis=1)
    row, col = rank // PLANES, rank % PLANES
    plane = jnp.where(row % 2 == 1, PLANES - 1 - col, col)
    place = plane * PLANE_HEADS + row
    hit = (place[None, :] == ids[:, None]).astype(jnp.int32)
    head_at = jnp.sum(hit * ids[None, :], axis=1)
    work_at = jnp.sum(hit * work[None, :], axis=1)
    return head_at, work_at


def chip_plan(work_at):
    extra = CHIPS - PLANE_HEADS
    quota = (work_at[:, None].astype(jnp.float32) / jnp.arange(1, extra + 1).astype(jnp.float32)[None, :]).reshape(-1)
    ids = jnp.arange(quota.shape[0])
    ahead = (quota[None, :] > quota[:, None]) | ((quota[None, :] == quota[:, None]) & (ids[None, :] < ids[:, None]))
    won = (jnp.sum(ahead.astype(jnp.int32), axis=1) < extra).astype(jnp.int32)
    chips = 1 + jnp.sum(won.reshape(PLANE_HEADS, extra), axis=1)
    slots = jnp.arange(PLANE_HEADS)
    first = jnp.sum(jnp.where(slots[None, :] < slots[:, None], chips[None, :], 0), axis=1)
    return chips, first


def pack_kernel(heads, q_ref, k_ref, v_ref, first_ref, second_ref, held, turned, sem_in, sem_out):
    start = pl.multiple_of(heads[CHIPS] * HALF, HALF)
    rows = pl.ds(start, HALF)
    loads, stores = [], []
    for t in range(CHIPS):
        cols = pl.ds(pl.multiple_of(heads[t] * TILE, TILE), TILE)
        loads.append(
            [
                pltpu.make_async_copy(k_ref.at[rows, cols], held.at[t, pl.ds(0, HALF)], sem_in.at[t, 0]),
                pltpu.make_async_copy(v_ref.at[rows, cols], held.at[t, pl.ds(HALF, HALF)], sem_in.at[t, 1]),
                pltpu.make_async_copy(q_ref.at[rows, cols], held.at[t, pl.ds(2 * HALF, HALF)], sem_in.at[t, 2]),
            ]
        )
        for load in loads[-1]:
            load.start()
    for t in range(CHIPS):
        for load in loads[t]:
            load.wait()
        for sub in range(2):
            part = pl.ds(sub * TILE, TILE)
            turned[t, part, :] = held[t, pl.ds(HALF + sub * TILE, TILE), :].T
        stores += [
            pltpu.make_async_copy(held.at[t, pl.ds(0, HALF)], first_ref.at[t, pl.ds(0, HALF)], sem_out.at[t, 0]),
            pltpu.make_async_copy(turned.at[t], first_ref.at[t, pl.ds(HALF, HALF)], sem_out.at[t, 1]),
            pltpu.make_async_copy(
                held.at[t, pl.ds(2 * HALF, TILE)], first_ref.at[t, pl.ds(2 * HALF, TILE)], sem_out.at[t, 2]
            ),
            pltpu.make_async_copy(held.at[t, pl.ds(2 * HALF + TILE, TILE)], second_ref.at[t], sem_out.at[t, 3]),
        ]
        for store in stores[-4:]:
            store.start()
    for store in stores:
        store.wait()


def pack(queries, keys, values, chip_heads, core):
    scalars = jnp.concatenate([chip_heads, core[None]]).astype(jnp.int32)
    hbm = pl.BlockSpec(memory_space=pl.ANY)
    return pl.pallas_call(
        pack_kernel,
        in_specs=[pl.BlockSpec(memory_space=pltpu.SMEM)] + [hbm] * 3,
        out_specs=[hbm, hbm],
        out_shape=[
            jax.ShapeDtypeStruct((CHIPS, 5 * TILE, TILE), jnp.bfloat16),
            jax.ShapeDtypeStruct((CHIPS, TILE, TILE), jnp.bfloat16),
        ],
        scratch_shapes=[
            pltpu.VMEM((CHIPS, 3 * HALF, TILE), jnp.bfloat16),
            pltpu.VMEM((CHIPS, HALF, TILE), jnp.bfloat16),
            pltpu.SemaphoreType.DMA((CHIPS, 3)),
            pltpu.SemaphoreType.DMA((CHIPS, 4)),
        ],
        compiler_params=pltpu.CompilerParams(vmem_limit_bytes=60 * 2**20),
    )(scalars, queries, keys, values)


def attend_kernel(
    scale, query_at, meta, q_of, k_of, valid_of, own_ref, other_ref, query_ref, out_ref, kv_s, q_s, acc_s, max_s, sum_s, sems
):
    core = meta[0]
    loads = [
        pltpu.make_async_copy(own_ref.at[:, pl.ds(0, 4)], kv_s.at[core], sems.at[0]),
        pltpu.make_async_copy(other_ref.at[:, pl.ds(0, 4)], kv_s.at[1 - core], sems.at[1]),
        pltpu.make_async_copy(query_ref.at[:, pl.ds(query_at, 1)], q_s, sems.at[2]),
    ]
    for load in loads:
        load.start()
    acc_s[...] = jnp.zeros_like(acc_s)
    sum_s[...] = jnp.zeros_like(sum_s)
    max_s[...] = jnp.full_like(max_s, LOW)
    for load in loads:
        load.wait()

    def body(step, _):
        parts = []
        for u in range(UNROLL):
            e = step * UNROLL + u
            t = q_of[e]
            kid = [k_of[e * GROUP + g] for g in range(GROUP)]
            valid = valid_of[e]
            keys = jnp.concatenate([kv_s[i // 64, i % 64 // 4, i % 4] for i in kid], axis=0)
            scores = lax.dot_general(keys, q_s[t, 0], (((1,), (1,)), ((), ())), preferred_element_type=jnp.float32)
            top = jnp.max(scores, axis=0, keepdims=True) * scale
            weights = []
            total = jnp.zeros((1, TILE), jnp.float32)
            for g in range(GROUP):
                shift = top + jnp.where(g < valid, 0.0, -LOW)
                w = jnp.exp2(scores[g * TILE : (g + 1) * TILE] * scale - shift)
                total = total + jnp.sum(w, axis=0, keepdims=True)
                weights.append(w.astype(jnp.bfloat16))
            vals = jnp.concatenate([kv_s[i // 64, i % 64 // 4, i % 4 + 2] for i in kid], axis=1)
            part = jnp.dot(vals, jnp.concatenate(weights, axis=0), preferred_element_type=jnp.float32)
            parts.append((t, top, total, part))
        for t, top, total, part in parts:
            old = max_s[t]
            new = jnp.maximum(old, top)
            a = jnp.exp2(old - new)
            b = jnp.exp2(top - new)
            max_s[t] = new
            sum_s[t] = sum_s[t] * a + total * b
            acc_s[t] = acc_s[t] * a + part * b
        return 0

    lax.fori_loop(0, meta[1], body, 0)

    def finish(t, _):
        inverse = 1.0 / jnp.maximum(sum_s[t], 1e-30)
        out_ref[t] = (acc_s[t] * inverse).astype(jnp.bfloat16)
        return 0

    lax.fori_loop(0, CHIPS, finish, 0)


def attend(query_at, meta, q_of, k_of, valid_of, own, other, query):
    smem = pl.BlockSpec(memory_space=pltpu.SMEM)
    hbm = pl.BlockSpec(memory_space=pl.ANY)
    return pl.pallas_call(
        functools.partial(attend_kernel, TILE**-0.5 * LOG2E, query_at),
        in_specs=[smem] * 4 + [hbm] * 3,
        out_specs=pl.BlockSpec(memory_space=pltpu.VMEM),
        out_shape=jax.ShapeDtypeStruct((CHIPS, TILE, TILE), jnp.bfloat16),
        scratch_shapes=[
            pltpu.VMEM((2, CHIPS, 4, TILE, TILE), jnp.bfloat16),
            pltpu.VMEM((CHIPS, 1, TILE, TILE), jnp.bfloat16),
            pltpu.VMEM((CHIPS, TILE, TILE), jnp.float32),
            pltpu.VMEM((CHIPS, 1, TILE), jnp.float32),
            pltpu.VMEM((CHIPS, 1, TILE), jnp.float32),
            pltpu.SemaphoreType.DMA((3,)),
        ],
        compiler_params=pltpu.CompilerParams(vmem_limit_bytes=24 * 2**20),
        cost_estimate=pl.CostEstimate(flops=8 * 10**9, bytes_accessed=8 * 2**20, transcendentals=4 * 10**6),
    )(meta, q_of, k_of, valid_of, own, other, query)


def gather_kernel(heads, w_ref, *rest):
    out_refs, sems = rest[:PLANES], rest[PLANES]
    copies = []
    for n in range(HEADS):
        rows = pl.ds(pl.multiple_of(heads[n] * TILE, TILE), TILE)
        part = out_refs[n // PLANE_HEADS].at[pl.ds(n % PLANE_HEADS * TILE, TILE)]
        copies.append(pltpu.make_async_copy(w_ref.at[rows], part, sems.at[n]))
        copies[-1].start()
    for copy in copies:
        copy.wait()


def gather(w_out, heads):
    rows = PLANE_HEADS * TILE
    return pl.pallas_call(
        gather_kernel,
        in_specs=[pl.BlockSpec(memory_space=pltpu.SMEM), pl.BlockSpec(memory_space=pl.ANY)],
        out_specs=[pl.BlockSpec(memory_space=pltpu.VMEM)] * PLANES,
        out_shape=[jax.ShapeDtypeStruct((rows, w_out.shape[1]), w_out.dtype)] * PLANES,
        scratch_shapes=[pltpu.SemaphoreType.DMA((HEADS,))],
        compiler_params=pltpu.CompilerParams(vmem_limit_bytes=20 * 2**20),
        cost_estimate=pl.CostEstimate(flops=0, bytes_accessed=13 * 2**20, transcendentals=0),
    )(heads, w_out)


def item_lists(allowed, mine):
    tiles = allowed.shape[1]
    count = jnp.sum(allowed, axis=1) * mine
    groups = (count + GROUP - 1) // GROUP
    slots = jnp.arange(groups.shape[0])
    end = jnp.sum(jnp.where(slots[None, :] <= slots[:, None], groups[None, :], 0), axis=1)
    steps = (end[-1] + UNROLL - 1) // UNROLL
    key_ids = jnp.arange(tiles)
    before = jnp.sum(allowed[:, None, :] * (key_ids[None, :] < key_ids[:, None])[None].astype(jnp.int32), axis=2)
    held_at = (key_ids // 2 % 2) * 64 + key_ids // 4 * 4 + key_ids % 2
    listed = jnp.sum(
        jnp.where((before[:, :, None] == key_ids[None, None, :]) & (allowed[:, :, None] > 0), held_at[None, :, None], 0),
        axis=1,
    )
    item = jnp.arange(ITEMS)
    real = (item < end[-1]).astype(jnp.int32)
    held = jnp.maximum(jnp.minimum(item, end[-1] - 1), 0)
    q_of = jnp.minimum(jnp.sum((end[None, :] <= held[:, None]).astype(jnp.int32), axis=1), CHIPS - 1)
    pick = (q_of[:, None] == slots[None, :]).astype(jnp.int32)
    start = GROUP * (held - jnp.sum(pick * (end - groups)[None, :], axis=1))
    left = jnp.sum(pick * count[None, :], axis=1) - start
    rows = jnp.dot(pick.astype(jnp.float32), listed.astype(jnp.float32))
    offset = jnp.arange(GROUP)
    where = start[:, None] + jnp.where(offset[None, :] < left[:, None], offset[None, :], 0)
    k_of = jnp.sum(jnp.where(where[:, :, None] == key_ids[None, None, :], rows[:, None, :], 0.0), axis=2)
    valid = jnp.minimum(left, GROUP) * real
    return steps, q_of, k_of.astype(jnp.int32).reshape(-1), valid


def select_kernel(source, got_ref, out_ref):
    for i in range(PLANE_HEADS):
        out_ref[:, pl.ds(i * TILE, TILE)] = got_ref[source[i]].T


def select(source, got):
    vmem = pl.BlockSpec(memory_space=pltpu.VMEM)
    return pl.pallas_call(
        select_kernel,
        in_specs=[pl.BlockSpec(memory_space=pltpu.SMEM), vmem],
        out_specs=vmem,
        out_shape=jax.ShapeDtypeStruct((TILE, PLANE_HEADS * TILE), jnp.bfloat16),
    )(source, got)


def exchange(block):
    return lax.all_to_all(block, TOKENS_AXES, split_axis=0, concat_axis=0, tiled=True)


def along_y(block, step):
    return lax.ppermute(block, "y", [(i, (i + step) % PLANES) for i in range(PLANES)])


def swap(block):
    return lax.ppermute(block, "c", [(0, 1), (1, 0)])


def shards(residual_in, queries, keys, values, w_out, gate_scale, tile_mask):
    chip = lax.axis_index("x") * 4 + lax.axis_index("z")
    plane = lax.axis_index("y")
    core = lax.axis_index("c")
    tile_work = jnp.sum(tile_mask, axis=1)
    head_at, work_at = head_plan(jnp.sum(tile_work, axis=1))
    plane_heads = lax.dynamic_slice_in_dim(head_at, plane * PLANE_HEADS, PLANE_HEADS)
    chips, first = chip_plan(lax.dynamic_slice_in_dim(work_at, plane * PLANE_HEADS, PLANE_HEADS))
    chip_ids = jnp.arange(CHIPS)
    on_chip = (first[None, :] <= chip_ids[:, None]) & (chip_ids[:, None] < (first + chips)[None, :])
    chip_heads = jnp.sum(jnp.where(on_chip, plane_heads[None, :], 0), axis=1)
    first_send, second_send = pack(queries, keys, values, chip_heads, core)
    got = exchange(first_send).reshape(CHIPS, 5, TILE, TILE)

    half_work = lax.dynamic_index_in_dim(tile_work.reshape(HEADS, CHIPS, 2, 2), core, 2, keepdims=False)
    half_work = jnp.take(half_work.reshape(HEADS, 2 * CHIPS), plane_heads, axis=0, mode="clip")
    tile_ids = jnp.arange(2 * CHIPS)
    done = jnp.sum(
        jnp.where((tile_ids[None, :] < tile_ids[:, None])[None], half_work[:, None, :], 0), axis=2
    )
    total = jnp.sum(half_work, axis=1, keepdims=True)
    owner = first[:, None] + ((2 * done + half_work) * chips[:, None]) // (2 * total)
    my_slot = jnp.sum(jnp.where(on_chip[chip], jnp.arange(PLANE_HEADS), 0))
    my_head = chip_heads[chip]
    mine_tiles = (owner[my_slot] == chip).astype(jnp.int32).reshape(CHIPS, 2)
    allowed = lax.dynamic_index_in_dim(tile_mask, my_head, 0, keepdims=False)
    allowed = lax.dynamic_index_in_dim(allowed.reshape(CHIPS, 2, 2, 4 * CHIPS), core, 1, keepdims=False)
    source = lax.dynamic_slice_in_dim(owner, 2 * chip, 2, 1)

    w_order = jnp.concatenate(
        [lax.dynamic_slice_in_dim(head_at, (plane + k) % PLANES * PLANE_HEADS, PLANE_HEADS) for k in (0, 3, 1, 2)]
    )
    weights = gather(w_out, w_order)
    lists = [item_lists(allowed[:, sub], mine_tiles[:, sub]) for sub in range(2)]
    got, lists, weights, second_send = lax.optimization_barrier((got, lists, weights, second_send))
    got_other = swap(got)
    late = exchange(second_send).reshape(CHIPS, 1, TILE, TILE)

    halves = []
    for sub in range(2):
        steps, q_of, k_of, valid = lists[sub]
        meta = jnp.stack([core, steps]).astype(jnp.int32)
        query_at, query = ((4, got), (0, late))[sub]
        attended = attend(query_at, meta, q_of, k_of, valid, got, got_other, query)
        own = select(source[:, sub], exchange(attended))
        blocks = [own, along_y(own, 1), along_y(own, 3), along_y(own, 2)]
        total = jnp.zeros((2 * TILE, w_out.shape[1]), jnp.float32)
        for k, block in enumerate(blocks):
            both = jnp.concatenate([block, swap(block)], axis=0)
            total = total + jnp.dot(both, weights[k], preferred_element_type=jnp.float32)
        halves.append(total.reshape(2, TILE, -1))
    mine, theirs = (jnp.concatenate([halves[0][i], halves[1][i]], axis=0) for i in range(2))
    low = jnp.where(core == 0, mine, theirs)
    high = jnp.where(core == 0, theirs, mine)
    projected = jnp.concatenate([low, high], axis=0)
    return (residual_in.astype(jnp.float32) + gate_scale * projected).astype(jnp.bfloat16)


def solution(mesh):
    fine = Mesh(mesh.devices.reshape(4, 4, 4, 2), ("x", "z", "y", "c"))
    seq, rep = TOKENS_AXES, ("y", "c")
    in_specs = (
        P(seq, rep),
        P(seq, None),
        P(seq, None),
        P(seq, None),
        P(None, rep),
        P(rep),
        P(),
    )
    return jax.shard_map(shards, mesh=fine, in_specs=in_specs, out_specs=P(seq, rep), check_vma=False)
```

```python
import functools

import jax
import jax.numpy as jnp
from jax import lax
from jax.experimental import pallas as pl
from jax.experimental.pallas import tpu as pltpu
from jax.sharding import Mesh
from jax.sharding import PartitionSpec as P

TILE = 128
HEADS = 40
PLANES = 4
PLANE_HEADS = HEADS // PLANES
CHIPS = 16
HALF = 256
GROUP = 4
UNROLL = 16
ITEMS = 256
LOG2E = 1.4426950408889634
TOKENS_AXES = ("x", "z")
LOW = -1e30


def head_plan(work):
    ids = jnp.arange(HEADS)
    ahead = (work[None, :] > work[:, None]) | ((work[None, :] == work[:, None]) & (ids[None, :] < ids[:, None]))
    rank = jnp.sum(ahead.astype(jnp.int32), axis=1)
    row, col = rank // PLANES, rank % PLANES
    plane = jnp.where(row % 2 == 1, PLANES - 1 - col, col)
    place = plane * PLANE_HEADS + row
    hit = (place[None, :] == ids[:, None]).astype(jnp.int32)
    head_at = jnp.sum(hit * ids[None, :], axis=1)
    work_at = jnp.sum(hit * work[None, :], axis=1)
    return head_at, work_at


def chip_plan(work_at):
    extra = CHIPS - PLANE_HEADS
    quota = (work_at[:, None].astype(jnp.float32) / jnp.arange(1, extra + 1).astype(jnp.float32)[None, :]).reshape(-1)
    ids = jnp.arange(quota.shape[0])
    ahead = (quota[None, :] > quota[:, None]) | ((quota[None, :] == quota[:, None]) & (ids[None, :] < ids[:, None]))
    won = (jnp.sum(ahead.astype(jnp.int32), axis=1) < extra).astype(jnp.int32)
    chips = 1 + jnp.sum(won.reshape(PLANE_HEADS, extra), axis=1)
    slots = jnp.arange(PLANE_HEADS)
    first = jnp.sum(jnp.where(slots[None, :] < slots[:, None], chips[None, :], 0), axis=1)
    return chips, first


def pack_kernel(heads, q_ref, k_ref, v_ref, out_ref, held, turned, sem_in, sem_out):
    start = pl.multiple_of(heads[CHIPS] * HALF, HALF)
    rows = pl.ds(start, HALF)
    loads, stores = [], []
    for t in range(CHIPS):
        cols = pl.ds(pl.multiple_of(heads[t] * TILE, TILE), TILE)
        loads.append(
            [
                pltpu.make_async_copy(k_ref.at[rows, cols], held.at[t, pl.ds(0, HALF)], sem_in.at[t, 0]),
                pltpu.make_async_copy(v_ref.at[rows, cols], held.at[t, pl.ds(HALF, HALF)], sem_in.at[t, 1]),
                pltpu.make_async_copy(q_ref.at[rows, cols], held.at[t, pl.ds(2 * HALF, HALF)], sem_in.at[t, 2]),
            ]
        )
        for load in loads[-1]:
            load.start()
    for t in range(CHIPS):
        for load in loads[t]:
            load.wait()
        for sub in range(2):
            part = pl.ds(sub * TILE, TILE)
            turned[t, part, :] = held[t, pl.ds(HALF + sub * TILE, TILE), :].T
        stores += [
            pltpu.make_async_copy(held.at[t, pl.ds(0, HALF)], out_ref.at[t, pl.ds(0, HALF)], sem_out.at[t, 0]),
            pltpu.make_async_copy(turned.at[t], out_ref.at[t, pl.ds(HALF, HALF)], sem_out.at[t, 1]),
            pltpu.make_async_copy(
                held.at[t, pl.ds(2 * HALF, HALF)], out_ref.at[t, pl.ds(2 * HALF, HALF)], sem_out.at[t, 2]
            ),
        ]
        for store in stores[-3:]:
            store.start()
    for store in stores:
        store.wait()


def pack(queries, keys, values, chip_heads, core):
    scalars = jnp.concatenate([chip_heads, core[None]]).astype(jnp.int32)
    hbm = pl.BlockSpec(memory_space=pl.ANY)
    return pl.pallas_call(
        pack_kernel,
        in_specs=[pl.BlockSpec(memory_space=pltpu.SMEM)] + [hbm] * 3,
        out_specs=hbm,
        out_shape=jax.ShapeDtypeStruct((CHIPS, 6 * TILE, TILE), jnp.bfloat16),
        scratch_shapes=[
            pltpu.VMEM((CHIPS, 3 * HALF, TILE), jnp.bfloat16),
            pltpu.VMEM((CHIPS, HALF, TILE), jnp.bfloat16),
            pltpu.SemaphoreType.DMA((CHIPS, 3)),
            pltpu.SemaphoreType.DMA((CHIPS, 3)),
        ],
        compiler_params=pltpu.CompilerParams(vmem_limit_bytes=60 * 2**20),
    )(scalars, queries, keys, values)


def attend_kernel(
    scale, query_at, meta, q_of, k_of, valid_of, own_ref, other_ref, out_ref, kv_s, q_s, acc_s, max_s, sum_s, sems
):
    core = meta[0]
    loads = [
        pltpu.make_async_copy(own_ref.at[:, pl.ds(0, 4)], kv_s.at[core], sems.at[0]),
        pltpu.make_async_copy(other_ref.at[:, pl.ds(0, 4)], kv_s.at[1 - core], sems.at[1]),
        pltpu.make_async_copy(own_ref.at[:, pl.ds(query_at, 1)], q_s, sems.at[2]),
    ]
    for load in loads:
        load.start()
    acc_s[...] = jnp.zeros_like(acc_s)
    sum_s[...] = jnp.zeros_like(sum_s)
    max_s[...] = jnp.full_like(max_s, LOW)
    for load in loads:
        load.wait()

    def body(step, _):
        parts = []
        for u in range(UNROLL):
            e = step * UNROLL + u
            t = q_of[e]
            kid = [k_of[e * GROUP + g] for g in range(GROUP)]
            valid = valid_of[e]
            keys = jnp.concatenate([kv_s[i // 64, i % 64 // 4, i % 4] for i in kid], axis=0)
            scores = lax.dot_general(keys, q_s[t, 0], (((1,), (1,)), ((), ())), preferred_element_type=jnp.float32)
            top = jnp.max(scores, axis=0, keepdims=True) * scale
            weights = []
            total = jnp.zeros((1, TILE), jnp.float32)
            for g in range(GROUP):
                shift = top + jnp.where(g < valid, 0.0, -LOW)
                w = jnp.exp2(scores[g * TILE : (g + 1) * TILE] * scale - shift)
                total = total + jnp.sum(w, axis=0, keepdims=True)
                weights.append(w.astype(jnp.bfloat16))
            vals = jnp.concatenate([kv_s[i // 64, i % 64 // 4, i % 4 + 2] for i in kid], axis=1)
            part = jnp.dot(vals, jnp.concatenate(weights, axis=0), preferred_element_type=jnp.float32)
            parts.append((t, top, total, part))
        for t, top, total, part in parts:
            old = max_s[t]
            new = jnp.maximum(old, top)
            a = jnp.exp2(old - new)
            b = jnp.exp2(top - new)
            max_s[t] = new
            sum_s[t] = sum_s[t] * a + total * b
            acc_s[t] = acc_s[t] * a + part * b
        return 0

    lax.fori_loop(0, meta[1], body, 0)

    def finish(t, _):
        inverse = 1.0 / jnp.maximum(sum_s[t], 1e-30)
        out_ref[t] = (acc_s[t] * inverse).astype(jnp.bfloat16)
        return 0

    lax.fori_loop(0, CHIPS, finish, 0)


def attend(query_at, meta, q_of, k_of, valid_of, own, other):
    smem = pl.BlockSpec(memory_space=pltpu.SMEM)
    hbm = pl.BlockSpec(memory_space=pl.ANY)
    return pl.pallas_call(
        functools.partial(attend_kernel, TILE**-0.5 * LOG2E, query_at),
        in_specs=[smem] * 4 + [hbm] * 2,
        out_specs=pl.BlockSpec(memory_space=pltpu.VMEM),
        out_shape=jax.ShapeDtypeStruct((CHIPS, TILE, TILE), jnp.bfloat16),
        scratch_shapes=[
            pltpu.VMEM((2, CHIPS, 4, TILE, TILE), jnp.bfloat16),
            pltpu.VMEM((CHIPS, 1, TILE, TILE), jnp.bfloat16),
            pltpu.VMEM((CHIPS, TILE, TILE), jnp.float32),
            pltpu.VMEM((CHIPS, 1, TILE), jnp.float32),
            pltpu.VMEM((CHIPS, 1, TILE), jnp.float32),
            pltpu.SemaphoreType.DMA((3,)),
        ],
        compiler_params=pltpu.CompilerParams(vmem_limit_bytes=24 * 2**20),
    )(meta, q_of, k_of, valid_of, own, other)


def item_lists(allowed, mine):
    tiles = allowed.shape[1]
    count = jnp.sum(allowed, axis=1) * mine
    groups = (count + GROUP - 1) // GROUP
    slots = jnp.arange(groups.shape[0])
    end = jnp.sum(jnp.where(slots[None, :] <= slots[:, None], groups[None, :], 0), axis=1)
    steps = (end[-1] + UNROLL - 1) // UNROLL
    key_ids = jnp.arange(tiles)
    before = jnp.sum(allowed[:, None, :] * (key_ids[None, :] < key_ids[:, None])[None].astype(jnp.int32), axis=2)
    held_at = (key_ids // 2 % 2) * 64 + key_ids // 4 * 4 + key_ids % 2
    listed = jnp.sum(
        jnp.where((before[:, :, None] == key_ids[None, None, :]) & (allowed[:, :, None] > 0), held_at[None, :, None], 0),
        axis=1,
    )
    item = jnp.arange(ITEMS)
    real = (item < end[-1]).astype(jnp.int32)
    held = jnp.maximum(jnp.minimum(item, end[-1] - 1), 0)
    q_of = jnp.minimum(jnp.sum((end[None, :] <= held[:, None]).astype(jnp.int32), axis=1), CHIPS - 1)
    pick = (q_of[:, None] == slots[None, :]).astype(jnp.int32)
    start = GROUP * (held - jnp.sum(pick * (end - groups)[None, :], axis=1))
    left = jnp.sum(pick * count[None, :], axis=1) - start
    rows = jnp.dot(pick.astype(jnp.float32), listed.astype(jnp.float32))
    offset = jnp.arange(GROUP)
    where = start[:, None] + jnp.where(offset[None, :] < left[:, None], offset[None, :], 0)
    k_of = jnp.sum(jnp.where(where[:, :, None] == key_ids[None, None, :], rows[:, None, :], 0.0), axis=2)
    valid = jnp.minimum(left, GROUP) * real
    return steps, q_of, k_of.astype(jnp.int32).reshape(-1), valid


def select_kernel(source, got_ref, out_ref):
    for i in range(PLANE_HEADS):
        out_ref[:, pl.ds(i * TILE, TILE)] = got_ref[source[i]].T


def select(source, got):
    vmem = pl.BlockSpec(memory_space=pltpu.VMEM)
    return pl.pallas_call(
        select_kernel,
        in_specs=[pl.BlockSpec(memory_space=pltpu.SMEM), vmem],
        out_specs=vmem,
        out_shape=jax.ShapeDtypeStruct((TILE, PLANE_HEADS * TILE), jnp.bfloat16),
    )(source, got)


def exchange(block):
    return lax.all_to_all(block, TOKENS_AXES, split_axis=0, concat_axis=0, tiled=True)


def along_y(block, step):
    return lax.ppermute(block, "y", [(i, (i + step) % PLANES) for i in range(PLANES)])


def swap(block):
    return lax.ppermute(block, "c", [(0, 1), (1, 0)])


def shards(residual_in, queries, keys, values, w_out, gate_scale, tile_mask):
    chip = lax.axis_index("x") * 4 + lax.axis_index("z")
    plane = lax.axis_index("y")
    core = lax.axis_index("c")
    tile_work = jnp.sum(tile_mask, axis=1)
    head_at, work_at = head_plan(jnp.sum(tile_work, axis=1))
    plane_heads = lax.dynamic_slice_in_dim(head_at, plane * PLANE_HEADS, PLANE_HEADS)
    chips, first = chip_plan(lax.dynamic_slice_in_dim(work_at, plane * PLANE_HEADS, PLANE_HEADS))
    chip_ids = jnp.arange(CHIPS)
    on_chip = (first[None, :] <= chip_ids[:, None]) & (chip_ids[:, None] < (first + chips)[None, :])
    chip_heads = jnp.sum(jnp.where(on_chip, plane_heads[None, :], 0), axis=1)
    got = exchange(pack(queries, keys, values, chip_heads, core)).reshape(CHIPS, 6, TILE, TILE)

    half_work = lax.dynamic_index_in_dim(tile_work.reshape(HEADS, CHIPS, 2, 2), core, 2, keepdims=False)
    half_work = jnp.take(half_work.reshape(HEADS, 2 * CHIPS), plane_heads, axis=0, mode="clip")
    tile_ids = jnp.arange(2 * CHIPS)
    done = jnp.sum(
        jnp.where((tile_ids[None, :] < tile_ids[:, None])[None], half_work[:, None, :], 0), axis=2
    )
    total = jnp.sum(half_work, axis=1, keepdims=True)
    owner = first[:, None] + ((2 * done + half_work) * chips[:, None]) // (2 * total)
    my_slot = jnp.sum(jnp.where(on_chip[chip], jnp.arange(PLANE_HEADS), 0))
    my_head = chip_heads[chip]
    mine_tiles = (owner[my_slot] == chip).astype(jnp.int32).reshape(CHIPS, 2)
    allowed = lax.dynamic_index_in_dim(tile_mask, my_head, 0, keepdims=False)
    allowed = lax.dynamic_index_in_dim(allowed.reshape(CHIPS, 2, 2, 4 * CHIPS), core, 1, keepdims=False)
    source = lax.dynamic_slice_in_dim(owner, 2 * chip, 2, 1)

    w_heads = w_out.reshape(HEADS, TILE, w_out.shape[1])
    weights = []
    for ahead in (0, 3, 1, 2):
        w_order = lax.dynamic_slice_in_dim(head_at, (plane + ahead) % PLANES * PLANE_HEADS, PLANE_HEADS)
        weights.append(jnp.take(w_heads, w_order, axis=0, mode="clip").reshape(PLANE_HEADS * TILE, -1))
    lists = [item_lists(allowed[:, sub], mine_tiles[:, sub]) for sub in range(2)]
    got, lists, weights = lax.optimization_barrier((got, lists, weights))
    got_other = swap(got)

    halves = []
    for sub in range(2):
        steps, q_of, k_of, valid = lists[sub]
        meta = jnp.stack([core, steps]).astype(jnp.int32)
        attended = attend(4 + sub, meta, q_of, k_of, valid, got, got_other)
        own = select(source[:, sub], exchange(attended))
        blocks = [own, along_y(own, 1), along_y(own, 3), along_y(own, 2)]
        total = jnp.zeros((2 * TILE, w_out.shape[1]), jnp.float32)
        for k, block in enumerate(blocks):
            both = jnp.concatenate([block, swap(block)], axis=0)
            total = total + jnp.dot(both, weights[k], preferred_element_type=jnp.float32)
        halves.append(total.reshape(2, TILE, -1))
    mine, theirs = (jnp.concatenate([halves[0][i], halves[1][i]], axis=0) for i in range(2))
    low = jnp.where(core == 0, mine, theirs)
    high = jnp.where(core == 0, theirs, mine)
    projected = jnp.concatenate([low, high], axis=0)
    return (residual_in.astype(jnp.float32) + gate_scale * projected).astype(jnp.bfloat16)


def solution(mesh):
    fine = Mesh(mesh.devices.reshape(4, 4, 4, 2), ("x", "z", "y", "c"))
    seq, rep = TOKENS_AXES, ("y", "c")
    in_specs = (
        P(seq, rep),
        P(seq, None),
        P(seq, None),
        P(seq, None),
        P(None, rep),
        P(rep),
        P(),
    )
    return jax.shard_map(shards, mesh=fine, in_specs=in_specs, out_specs=P(seq, rep), check_vma=False)
```

```python
import functools

import jax
import jax.numpy as jnp
from jax import lax
from jax.experimental import pallas as pl
from jax.experimental.pallas import tpu as pltpu
from jax.sharding import Mesh
from jax.sharding import PartitionSpec as P

TILE = 128
HEADS = 40
PLANES = 4
PLANE_HEADS = HEADS // PLANES
CHIPS = 16
HALF = 256
GROUP = 4
UNROLL = 16
ITEMS = 512
LOG2E = 1.4426950408889634
TOKENS_AXES = ("x", "z")
LOW = -1e30


def head_plan(work):
    ids = jnp.arange(HEADS)
    ahead = (work[None, :] > work[:, None]) | ((work[None, :] == work[:, None]) & (ids[None, :] < ids[:, None]))
    rank = jnp.sum(ahead.astype(jnp.int32), axis=1)
    row, col = rank // PLANES, rank % PLANES
    plane = jnp.where(row % 2 == 1, PLANES - 1 - col, col)
    place = plane * PLANE_HEADS + row
    hit = (place[None, :] == ids[:, None]).astype(jnp.int32)
    head_at = jnp.sum(hit * ids[None, :], axis=1)
    work_at = jnp.sum(hit * work[None, :], axis=1)
    return head_at, work_at


def chip_plan(work_at):
    extra = CHIPS - PLANE_HEADS
    quota = (work_at[:, None].astype(jnp.float32) / jnp.arange(1, extra + 1).astype(jnp.float32)[None, :]).reshape(-1)
    ids = jnp.arange(quota.shape[0])
    ahead = (quota[None, :] > quota[:, None]) | ((quota[None, :] == quota[:, None]) & (ids[None, :] < ids[:, None]))
    won = (jnp.sum(ahead.astype(jnp.int32), axis=1) < extra).astype(jnp.int32)
    chips = 1 + jnp.sum(won.reshape(PLANE_HEADS, extra), axis=1)
    slots = jnp.arange(PLANE_HEADS)
    first = jnp.sum(jnp.where(slots[None, :] < slots[:, None], chips[None, :], 0), axis=1)
    return chips, first


def pack_kernel(heads, q_ref, k_ref, v_ref, out_ref, held, turned, sem_in, sem_out):
    start = pl.multiple_of(heads[CHIPS] * HALF, HALF)
    rows = pl.ds(start, HALF)
    loads, stores = [], []
    for t in range(CHIPS):
        cols = pl.ds(pl.multiple_of(heads[t] * TILE, TILE), TILE)
        loads.append(
            [
                pltpu.make_async_copy(k_ref.at[rows, cols], held.at[t, pl.ds(0, HALF)], sem_in.at[t, 0]),
                pltpu.make_async_copy(v_ref.at[rows, cols], held.at[t, pl.ds(HALF, HALF)], sem_in.at[t, 1]),
                pltpu.make_async_copy(q_ref.at[rows, cols], held.at[t, pl.ds(2 * HALF, HALF)], sem_in.at[t, 2]),
            ]
        )
        for load in loads[-1]:
            load.start()
    for t in range(CHIPS):
        for load in loads[t]:
            load.wait()
        for sub in range(2):
            part = pl.ds(sub * TILE, TILE)
            turned[t, part, :] = held[t, pl.ds(HALF + sub * TILE, TILE), :].T
        stores += [
            pltpu.make_async_copy(held.at[t, pl.ds(0, HALF)], out_ref.at[t, pl.ds(0, HALF)], sem_out.at[t, 0]),
            pltpu.make_async_copy(turned.at[t], out_ref.at[t, pl.ds(HALF, HALF)], sem_out.at[t, 1]),
            pltpu.make_async_copy(
                held.at[t, pl.ds(2 * HALF, HALF)], out_ref.at[t, pl.ds(2 * HALF, HALF)], sem_out.at[t, 2]
            ),
        ]
        for store in stores[-3:]:
            store.start()
    for store in stores:
        store.wait()


def pack(queries, keys, values, chip_heads, core):
    scalars = jnp.concatenate([chip_heads, core[None]]).astype(jnp.int32)
    hbm = pl.BlockSpec(memory_space=pl.ANY)
    return pl.pallas_call(
        pack_kernel,
        in_specs=[pl.BlockSpec(memory_space=pltpu.SMEM)] + [hbm] * 3,
        out_specs=hbm,
        out_shape=jax.ShapeDtypeStruct((CHIPS, 6 * TILE, TILE), jnp.bfloat16),
        scratch_shapes=[
            pltpu.VMEM((CHIPS, 3 * HALF, TILE), jnp.bfloat16),
            pltpu.VMEM((CHIPS, HALF, TILE), jnp.bfloat16),
            pltpu.SemaphoreType.DMA((CHIPS, 3)),
            pltpu.SemaphoreType.DMA((CHIPS, 3)),
        ],
        compiler_params=pltpu.CompilerParams(vmem_limit_bytes=60 * 2**20),
    )(scalars, queries, keys, values)


def attend_kernel(
    scale, meta, q_of, k_of, valid_of, own_ref, other_ref, out_ref, kv_s, q_s, acc_s, max_s, sum_s, sems
):
    core = meta[0]
    loads = [
        pltpu.make_async_copy(own_ref.at[:, pl.ds(0, 4)], kv_s.at[core], sems.at[0]),
        pltpu.make_async_copy(other_ref.at[:, pl.ds(0, 4)], kv_s.at[1 - core], sems.at[1]),
        pltpu.make_async_copy(own_ref.at[:, pl.ds(4, 2)], q_s, sems.at[2]),
    ]
    for load in loads:
        load.start()
    acc_s[...] = jnp.zeros_like(acc_s)
    sum_s[...] = jnp.zeros_like(sum_s)
    max_s[...] = jnp.full_like(max_s, LOW)
    for load in loads:
        load.wait()

    def body(step, _):
        parts = []
        for u in range(UNROLL):
            e = step * UNROLL + u
            t = q_of[e]
            kid = [k_of[e * GROUP + g] for g in range(GROUP)]
            valid = valid_of[e]
            keys = jnp.concatenate([kv_s[i // 64, i % 64 // 4, i % 4] for i in kid], axis=0)
            scores = lax.dot_general(keys, q_s[t // 2, t % 2], (((1,), (1,)), ((), ())), preferred_element_type=jnp.float32)
            top = jnp.max(scores, axis=0, keepdims=True) * scale
            weights = []
            total = jnp.zeros((1, TILE), jnp.float32)
            for g in range(GROUP):
                shift = top + jnp.where(g < valid, 0.0, -LOW)
                w = jnp.exp2(scores[g * TILE : (g + 1) * TILE] * scale - shift)
                total = total + jnp.sum(w, axis=0, keepdims=True)
                weights.append(w.astype(jnp.bfloat16))
            vals = jnp.concatenate([kv_s[i // 64, i % 64 // 4, i % 4 + 2] for i in kid], axis=1)
            part = jnp.dot(vals, jnp.concatenate(weights, axis=0), preferred_element_type=jnp.float32)
            parts.append((t, top, total, part))
        for t, top, total, part in parts:
            old = max_s[t]
            new = jnp.maximum(old, top)
            a = jnp.exp2(old - new)
            b = jnp.exp2(top - new)
            max_s[t] = new
            sum_s[t] = sum_s[t] * a + total * b
            acc_s[t] = acc_s[t] * a + part * b
        return 0

    lax.fori_loop(0, meta[1], body, 0)

    def finish(t, _):
        inverse = 1.0 / jnp.maximum(sum_s[t], 1e-30)
        out_ref[t] = (acc_s[t] * inverse).astype(jnp.bfloat16)
        return 0

    lax.fori_loop(0, 2 * CHIPS, finish, 0)


def attend(meta, q_of, k_of, valid_of, own, other):
    smem = pl.BlockSpec(memory_space=pltpu.SMEM)
    hbm = pl.BlockSpec(memory_space=pl.ANY)
    return pl.pallas_call(
        functools.partial(attend_kernel, TILE**-0.5 * LOG2E),
        in_specs=[smem] * 4 + [hbm] * 2,
        out_specs=pl.BlockSpec(memory_space=pltpu.VMEM),
        out_shape=jax.ShapeDtypeStruct((2 * CHIPS, TILE, TILE), jnp.bfloat16),
        scratch_shapes=[
            pltpu.VMEM((2, CHIPS, 4, TILE, TILE), jnp.bfloat16),
            pltpu.VMEM((CHIPS, 2, TILE, TILE), jnp.bfloat16),
            pltpu.VMEM((2 * CHIPS, TILE, TILE), jnp.float32),
            pltpu.VMEM((2 * CHIPS, 1, TILE), jnp.float32),
            pltpu.VMEM((2 * CHIPS, 1, TILE), jnp.float32),
            pltpu.SemaphoreType.DMA((3,)),
        ],
        compiler_params=pltpu.CompilerParams(vmem_limit_bytes=20 * 2**20),
    )(meta, q_of, k_of, valid_of, own, other)


def item_lists(allowed, mine):
    tiles = allowed.shape[1]
    count = jnp.sum(allowed, axis=1) * mine
    groups = (count + GROUP - 1) // GROUP
    slots = jnp.arange(groups.shape[0])
    end = jnp.sum(jnp.where(slots[None, :] <= slots[:, None], groups[None, :], 0), axis=1)
    steps = (end[-1] + UNROLL - 1) // UNROLL
    key_ids = jnp.arange(tiles)
    before = jnp.sum(allowed[:, None, :] * (key_ids[None, :] < key_ids[:, None])[None].astype(jnp.int32), axis=2)
    held_at = (key_ids // 2 % 2) * 64 + key_ids // 4 * 4 + key_ids % 2
    listed = jnp.sum(
        jnp.where((before[:, :, None] == key_ids[None, None, :]) & (allowed[:, :, None] > 0), held_at[None, :, None], 0),
        axis=1,
    )
    item = jnp.arange(ITEMS)
    real = (item < end[-1]).astype(jnp.int32)
    held = jnp.maximum(jnp.minimum(item, end[-1] - 1), 0)
    q_of = jnp.minimum(jnp.sum((end[None, :] <= held[:, None]).astype(jnp.int32), axis=1), 2 * CHIPS - 1)
    pick = (q_of[:, None] == slots[None, :]).astype(jnp.int32)
    start = GROUP * (held - jnp.sum(pick * (end - groups)[None, :], axis=1))
    left = jnp.sum(pick * count[None, :], axis=1) - start
    rows = jnp.dot(pick.astype(jnp.float32), listed.astype(jnp.float32))
    offset = jnp.arange(GROUP)
    where = start[:, None] + jnp.where(offset[None, :] < left[:, None], offset[None, :], 0)
    k_of = jnp.sum(jnp.where(where[:, :, None] == key_ids[None, None, :], rows[:, None, :], 0.0), axis=2)
    valid = jnp.minimum(left, GROUP) * real
    return steps, q_of, k_of.astype(jnp.int32).reshape(-1), valid


def select_kernel(source, got_ref, *out_refs):
    for sub, out_ref in enumerate(out_refs):
        for i in range(PLANE_HEADS):
            out_ref[:, pl.ds(i * TILE, TILE)] = got_ref[source[2 * i + sub], sub].T


def select(source, got):
    vmem = pl.BlockSpec(memory_space=pltpu.VMEM)
    return pl.pallas_call(
        select_kernel,
        in_specs=[pl.BlockSpec(memory_space=pltpu.SMEM), vmem],
        out_specs=[vmem] * 2,
        out_shape=[jax.ShapeDtypeStruct((TILE, PLANE_HEADS * TILE), jnp.bfloat16)] * 2,
    )(source, got)


def exchange(block):
    return lax.all_to_all(block, TOKENS_AXES, split_axis=0, concat_axis=0, tiled=True)


def along_y(block, step):
    return lax.ppermute(block, "y", [(i, (i + step) % PLANES) for i in range(PLANES)])


def swap(block):
    return lax.ppermute(block, "c", [(0, 1), (1, 0)])


def shards(residual_in, queries, keys, values, w_out, gate_scale, tile_mask):
    chip = lax.axis_index("x") * 4 + lax.axis_index("z")
    plane = lax.axis_index("y")
    core = lax.axis_index("c")
    tile_work = jnp.sum(tile_mask, axis=1)
    head_at, work_at = head_plan(jnp.sum(tile_work, axis=1))
    plane_heads = lax.dynamic_slice_in_dim(head_at, plane * PLANE_HEADS, PLANE_HEADS)
    chips, first = chip_plan(lax.dynamic_slice_in_dim(work_at, plane * PLANE_HEADS, PLANE_HEADS))
    chip_ids = jnp.arange(CHIPS)
    on_chip = (first[None, :] <= chip_ids[:, None]) & (chip_ids[:, None] < (first + chips)[None, :])
    chip_heads = jnp.sum(jnp.where(on_chip, plane_heads[None, :], 0), axis=1)
    got = exchange(pack(queries, keys, values, chip_heads, core)).reshape(CHIPS, 6, TILE, TILE)

    half_work = lax.dynamic_index_in_dim(tile_work.reshape(HEADS, CHIPS, 2, 2), core, 2, keepdims=False)
    half_work = jnp.take(half_work.reshape(HEADS, 2 * CHIPS), plane_heads, axis=0, mode="clip")
    tile_ids = jnp.arange(2 * CHIPS)
    done = jnp.sum(
        jnp.where((tile_ids[None, :] < tile_ids[:, None])[None], half_work[:, None, :], 0), axis=2
    )
    total = jnp.sum(half_work, axis=1, keepdims=True)
    owner = first[:, None] + ((2 * done + half_work) * chips[:, None]) // (2 * total)
    my_slot = jnp.sum(jnp.where(on_chip[chip], jnp.arange(PLANE_HEADS), 0))
    my_head = chip_heads[chip]
    mine_tiles = (owner[my_slot] == chip).astype(jnp.int32)
    allowed = lax.dynamic_index_in_dim(tile_mask, my_head, 0, keepdims=False)
    allowed = lax.dynamic_index_in_dim(allowed.reshape(CHIPS, 2, 2, 4 * CHIPS), core, 1, keepdims=False)
    source = lax.dynamic_slice_in_dim(owner, 2 * chip, 2, 1).reshape(-1)

    w_heads = w_out.reshape(HEADS, TILE, w_out.shape[1])
    weights = []
    for ahead in (0, 3, 1, 2):
        w_order = lax.dynamic_slice_in_dim(head_at, (plane + ahead) % PLANES * PLANE_HEADS, PLANE_HEADS)
        weights.append(jnp.take(w_heads, w_order, axis=0, mode="clip").reshape(PLANE_HEADS * TILE, -1))
    lists = item_lists(allowed.reshape(2 * CHIPS, 4 * CHIPS), mine_tiles)
    got, lists, source, weights = lax.optimization_barrier((got, lists, source, weights))
    got_other = swap(got)

    def project(block, weight):
        both = jnp.concatenate([block, swap(block)], axis=0)
        return jnp.dot(both, weight, preferred_element_type=jnp.float32)

    def by_rows(total):
        mine, theirs = total[:TILE], total[TILE:]
        return jnp.where(core == 0, mine, theirs), jnp.where(core == 0, theirs, mine)

    steps, q_of, k_of, valid = lists
    meta = jnp.stack([core, steps]).astype(jnp.int32)
    attended = attend(meta, q_of, k_of, valid, got, got_other)
    own_rows = select(source, exchange(attended.reshape(CHIPS, 2, TILE, TILE)))

    residual = residual_in.astype(jnp.float32).reshape(2, 2, TILE, -1)
    width = PLANE_HEADS * TILE // 2
    halves = []
    for sub, own in enumerate(own_rows):
        below, above = along_y(own, 1), along_y(own, 3)
        far_low, far_high = along_y(below[:, :width], 1), along_y(above[:, width:], 3)
        total = project(own, weights[0]) + project(below, weights[1]) + project(above, weights[2])
        near = lax.optimization_barrier([residual[c, sub] + gate_scale * rows for c, rows in enumerate(by_rows(total))])
        far = project(jnp.concatenate([far_low, far_high], axis=1), weights[3])
        halves.append([(near[c] + gate_scale * rows).astype(jnp.bfloat16) for c, rows in enumerate(by_rows(far))])
    return jnp.concatenate([halves[0][0], halves[1][0], halves[0][1], halves[1][1]], axis=0)


def solution(mesh):
    fine = Mesh(mesh.devices.reshape(4, 4, 4, 2), ("x", "z", "y", "c"))
    seq, rep = TOKENS_AXES, ("y", "c")
    in_specs = (
        P(seq, rep),
        P(seq, None),
        P(seq, None),
        P(seq, None),
        P(None, rep),
        P(rep),
        P(),
    )
    return jax.shard_map(shards, mesh=fine, in_specs=in_specs, out_specs=P(seq, rep), check_vma=False)
```

```python
import functools

import jax
import jax.numpy as jnp
from jax import lax
from jax.experimental import pallas as pl
from jax.experimental.pallas import tpu as pltpu
from jax.sharding import Mesh
from jax.sharding import PartitionSpec as P

TILE = 128
HEADS = 40
PLANES = 4
PLANE_HEADS = HEADS // PLANES
CHIPS = 16
HALF = 256
GROUP = 4
UNROLL = 16
ITEMS = 256
LOG2E = 1.4426950408889634
TOKENS_AXES = ("x", "z")
LOW = -1e30


def head_plan(work):
    ids = jnp.arange(HEADS)
    ahead = (work[None, :] > work[:, None]) | ((work[None, :] == work[:, None]) & (ids[None, :] < ids[:, None]))
    rank = jnp.sum(ahead.astype(jnp.int32), axis=1)
    row, col = rank // PLANES, rank % PLANES
    plane = jnp.where(row % 2 == 1, PLANES - 1 - col, col)
    place = plane * PLANE_HEADS + row
    hit = (place[None, :] == ids[:, None]).astype(jnp.int32)
    head_at = jnp.sum(hit * ids[None, :], axis=1)
    work_at = jnp.sum(hit * work[None, :], axis=1)
    return head_at, work_at


def chip_plan(work_at):
    extra = CHIPS - PLANE_HEADS
    quota = (work_at[:, None].astype(jnp.float32) / jnp.arange(1, extra + 1).astype(jnp.float32)[None, :]).reshape(-1)
    ids = jnp.arange(quota.shape[0])
    ahead = (quota[None, :] > quota[:, None]) | ((quota[None, :] == quota[:, None]) & (ids[None, :] < ids[:, None]))
    won = (jnp.sum(ahead.astype(jnp.int32), axis=1) < extra).astype(jnp.int32)
    chips = 1 + jnp.sum(won.reshape(PLANE_HEADS, extra), axis=1)
    slots = jnp.arange(PLANE_HEADS)
    first = jnp.sum(jnp.where(slots[None, :] < slots[:, None], chips[None, :], 0), axis=1)
    return chips, first


def pack_kernel(heads, q_ref, k_ref, v_ref, out_ref, held, turned, sem_in, sem_out):
    start = pl.multiple_of(heads[CHIPS] * HALF, HALF)
    rows = pl.ds(start, HALF)
    loads, stores = [], []
    for t in range(CHIPS):
        cols = pl.ds(pl.multiple_of(heads[t] * TILE, TILE), TILE)
        loads.append(
            [
                pltpu.make_async_copy(k_ref.at[rows, cols], held.at[t, pl.ds(0, HALF)], sem_in.at[t, 0]),
                pltpu.make_async_copy(v_ref.at[rows, cols], held.at[t, pl.ds(HALF, HALF)], sem_in.at[t, 1]),
                pltpu.make_async_copy(q_ref.at[rows, cols], held.at[t, pl.ds(2 * HALF, HALF)], sem_in.at[t, 2]),
            ]
        )
        for load in loads[-1]:
            load.start()
    for t in range(CHIPS):
        for load in loads[t]:
            load.wait()
        for sub in range(2):
            part = pl.ds(sub * TILE, TILE)
            turned[t, part, :] = held[t, pl.ds(HALF + sub * TILE, TILE), :].T
        stores += [
            pltpu.make_async_copy(held.at[t, pl.ds(0, HALF)], out_ref.at[t, pl.ds(0, HALF)], sem_out.at[t, 0]),
            pltpu.make_async_copy(turned.at[t], out_ref.at[t, pl.ds(HALF, HALF)], sem_out.at[t, 1]),
            pltpu.make_async_copy(
                held.at[t, pl.ds(2 * HALF, HALF)], out_ref.at[t, pl.ds(2 * HALF, HALF)], sem_out.at[t, 2]
            ),
        ]
        for store in stores[-3:]:
            store.start()
    for store in stores:
        store.wait()


def pack(queries, keys, values, chip_heads, core):
    scalars = jnp.concatenate([chip_heads, core[None]]).astype(jnp.int32)
    hbm = pl.BlockSpec(memory_space=pl.ANY)
    return pl.pallas_call(
        pack_kernel,
        in_specs=[pl.BlockSpec(memory_space=pltpu.SMEM)] + [hbm] * 3,
        out_specs=hbm,
        out_shape=jax.ShapeDtypeStruct((CHIPS, 6 * TILE, TILE), jnp.bfloat16),
        scratch_shapes=[
            pltpu.VMEM((CHIPS, 3 * HALF, TILE), jnp.bfloat16),
            pltpu.VMEM((CHIPS, HALF, TILE), jnp.bfloat16),
            pltpu.SemaphoreType.DMA((CHIPS, 3)),
            pltpu.SemaphoreType.DMA((CHIPS, 3)),
        ],
        compiler_params=pltpu.CompilerParams(vmem_limit_bytes=60 * 2**20),
    )(scalars, queries, keys, values)


def attend_items(scale, meta, q_of, k_of, valid_of, query_ref, key_ref, acc_ref, max_ref, sum_ref):
    def body(step, _):
        parts = []
        for u in range(UNROLL):
            e = step * UNROLL + u
            t = q_of[e]
            kid = [k_of[e * GROUP + g] for g in range(GROUP)]
            valid = valid_of[e]
            keys = jnp.concatenate([key_ref[i // 2, i % 2] for i in kid], axis=0)
            scores = lax.dot_general(
                keys, query_ref[t // 2, 4 + t % 2], (((1,), (1,)), ((), ())), preferred_element_type=jnp.float32
            )
            top = jnp.max(scores, axis=0, keepdims=True) * scale
            weights = []
            total = jnp.zeros((1, TILE), jnp.float32)
            for g in range(GROUP):
                shift = top + jnp.where(g < valid, 0.0, -LOW)
                w = jnp.exp2(scores[g * TILE : (g + 1) * TILE] * scale - shift)
                total = total + jnp.sum(w, axis=0, keepdims=True)
                weights.append(w.astype(jnp.bfloat16))
            vals = jnp.concatenate([key_ref[i // 2, 2 + i % 2] for i in kid], axis=1)
            part = jnp.dot(vals, jnp.concatenate(weights, axis=0), preferred_element_type=jnp.float32)
            parts.append((t, top, total, part))
        for t, top, total, part in parts:
            old = max_ref[t]
            new = jnp.maximum(old, top)
            a = jnp.exp2(old - new)
            b = jnp.exp2(top - new)
            max_ref[t] = new
            sum_ref[t] = sum_ref[t] * a + total * b
            acc_ref[t] = acc_ref[t] * a + part * b
        return 0

    lax.fori_loop(0, meta[0], body, 0)


def first_kernel(scale, meta, q_of, k_of, valid_of, own_ref, acc_ref, max_ref, sum_ref):
    acc_ref[...] = jnp.zeros_like(acc_ref)
    sum_ref[...] = jnp.zeros_like(sum_ref)
    max_ref[...] = jnp.full_like(max_ref, LOW)
    attend_items(scale, meta, q_of, k_of, valid_of, own_ref, own_ref, acc_ref, max_ref, sum_ref)


def second_kernel(scale, meta, q_of, k_of, valid_of, own_ref, other_ref, acc_in, max_in, sum_in, out_ref, acc_s, max_s, sum_s):
    acc_s[...] = acc_in[...]
    max_s[...] = max_in[...]
    sum_s[...] = sum_in[...]
    attend_items(scale, meta, q_of, k_of, valid_of, own_ref, other_ref, acc_s, max_s, sum_s)

    def finish(t, _):
        inverse = 1.0 / jnp.maximum(sum_s[t], 1e-30)
        out_ref[t] = (acc_s[t] * inverse).astype(jnp.bfloat16)
        return 0

    lax.fori_loop(0, 2 * CHIPS, finish, 0)


def attend(lists, own, other=None, state=None):
    tiles = 2 * CHIPS
    smem = pl.BlockSpec(memory_space=pltpu.SMEM)
    vmem = pl.BlockSpec(memory_space=pltpu.VMEM)
    shapes = [((tiles, TILE, TILE), jnp.float32), ((tiles, 1, TILE), jnp.float32), ((tiles, 1, TILE), jnp.float32)]
    options = dict(
        compiler_params=pltpu.CompilerParams(vmem_limit_bytes=24 * 2**20),
        cost_estimate=pl.CostEstimate(flops=4 * 10**9, bytes_accessed=8 * 2**20, transcendentals=4 * 10**6),
    )
    scale = TILE**-0.5 * LOG2E
    if other is None:
        return pl.pallas_call(
            functools.partial(first_kernel, scale),
            in_specs=[smem] * 4 + [vmem],
            out_specs=[vmem] * 3,
            out_shape=[jax.ShapeDtypeStruct(*shape) for shape in shapes],
            **options,
        )(*lists, own)
    return pl.pallas_call(
        functools.partial(second_kernel, scale),
        in_specs=[smem] * 4 + [vmem] * 5,
        out_specs=vmem,
        out_shape=jax.ShapeDtypeStruct((tiles, TILE, TILE), jnp.bfloat16),
        scratch_shapes=[pltpu.VMEM(*shape) for shape in shapes],
        **options,
    )(*lists, own, other, *state)


def item_lists(allowed, mine):
    tiles = allowed.shape[1]
    count = jnp.sum(allowed, axis=1) * mine
    groups = (count + GROUP - 1) // GROUP
    slots = jnp.arange(groups.shape[0])
    end = jnp.sum(jnp.where(slots[None, :] <= slots[:, None], groups[None, :], 0), axis=1)
    steps = (end[-1] + UNROLL - 1) // UNROLL
    key_ids = jnp.arange(tiles)
    before = jnp.sum(allowed[:, None, :] * (key_ids[None, :] < key_ids[:, None])[None].astype(jnp.int32), axis=2)
    listed = jnp.sum(
        jnp.where((before[:, :, None] == key_ids[None, None, :]) & (allowed[:, :, None] > 0), key_ids[None, :, None], 0),
        axis=1,
    )
    item = jnp.arange(ITEMS)
    real = (item < end[-1]).astype(jnp.int32)
    held = jnp.maximum(jnp.minimum(item, end[-1] - 1), 0)
    q_of = jnp.minimum(jnp.sum((end[None, :] <= held[:, None]).astype(jnp.int32), axis=1), 2 * CHIPS - 1)
    pick = (q_of[:, None] == slots[None, :]).astype(jnp.int32)
    start = GROUP * (held - jnp.sum(pick * (end - groups)[None, :], axis=1))
    left = jnp.sum(pick * count[None, :], axis=1) - start
    rows = jnp.dot(pick.astype(jnp.float32), listed.astype(jnp.float32))
    offset = jnp.arange(GROUP)
    where = start[:, None] + jnp.where(offset[None, :] < left[:, None], offset[None, :], 0)
    k_of = jnp.sum(jnp.where(where[:, :, None] == key_ids[None, None, :], rows[:, None, :], 0.0), axis=2)
    valid = jnp.minimum(left, GROUP) * real
    return steps[None], q_of, k_of.astype(jnp.int32).reshape(-1), valid


def select_kernel(source, got_ref, *out_refs):
    for sub, out_ref in enumerate(out_refs):
        for i in range(PLANE_HEADS):
            out_ref[:, pl.ds(i * TILE, TILE)] = got_ref[source[2 * i + sub], sub].T


def select(source, got):
    vmem = pl.BlockSpec(memory_space=pltpu.VMEM)
    return pl.pallas_call(
        select_kernel,
        in_specs=[pl.BlockSpec(memory_space=pltpu.SMEM), vmem],
        out_specs=[vmem] * 2,
        out_shape=[jax.ShapeDtypeStruct((TILE, PLANE_HEADS * TILE), jnp.bfloat16)] * 2,
    )(source, got)


def exchange(block):
    return lax.all_to_all(block, TOKENS_AXES, split_axis=0, concat_axis=0, tiled=True)


def along_y(block, step):
    return lax.ppermute(block, "y", [(i, (i + step) % PLANES) for i in range(PLANES)])


def swap(block):
    return lax.ppermute(block, "c", [(0, 1), (1, 0)])


def shards(residual_in, queries, keys, values, w_out, gate_scale, tile_mask):
    chip = lax.axis_index("x") * 4 + lax.axis_index("z")
    plane = lax.axis_index("y")
    core = lax.axis_index("c")
    tile_work = jnp.sum(tile_mask, axis=1)
    head_at, work_at = head_plan(jnp.sum(tile_work, axis=1))
    plane_heads = lax.dynamic_slice_in_dim(head_at, plane * PLANE_HEADS, PLANE_HEADS)
    chips, first = chip_plan(lax.dynamic_slice_in_dim(work_at, plane * PLANE_HEADS, PLANE_HEADS))
    chip_ids = jnp.arange(CHIPS)
    on_chip = (first[None, :] <= chip_ids[:, None]) & (chip_ids[:, None] < (first + chips)[None, :])
    chip_heads = jnp.sum(jnp.where(on_chip, plane_heads[None, :], 0), axis=1)
    got = exchange(pack(queries, keys, values, chip_heads, core)).reshape(CHIPS, 6, TILE, TILE)

    half_work = lax.dynamic_index_in_dim(tile_work.reshape(HEADS, CHIPS, 2, 2), core, 2, keepdims=False)
    half_work = jnp.take(half_work.reshape(HEADS, 2 * CHIPS), plane_heads, axis=0, mode="clip")
    tile_ids = jnp.arange(2 * CHIPS)
    done = jnp.sum(
        jnp.where((tile_ids[None, :] < tile_ids[:, None])[None], half_work[:, None, :], 0), axis=2
    )
    total = jnp.sum(half_work, axis=1, keepdims=True)
    owner = first[:, None] + ((2 * done + half_work) * chips[:, None]) // (2 * total)
    my_slot = jnp.sum(jnp.where(on_chip[chip], jnp.arange(PLANE_HEADS), 0))
    my_head = chip_heads[chip]
    mine_tiles = (owner[my_slot] == chip).astype(jnp.int32)
    allowed = lax.dynamic_index_in_dim(tile_mask, my_head, 0, keepdims=False)
    allowed = lax.dynamic_index_in_dim(allowed.reshape(CHIPS, 2, 2, 4 * CHIPS), core, 1, keepdims=False)
    source = lax.dynamic_slice_in_dim(owner, 2 * chip, 2, 1).reshape(-1)

    w_heads = w_out.reshape(HEADS, TILE, w_out.shape[1])
    weights = []
    for ahead in (0, 3, 1, 2):
        w_order = lax.dynamic_slice_in_dim(head_at, (plane + ahead) % PLANES * PLANE_HEADS, PLANE_HEADS)
        weights.append(jnp.take(w_heads, w_order, axis=0, mode="clip").reshape(PLANE_HEADS * TILE, -1))
    allowed = allowed.reshape(2 * CHIPS, CHIPS, 2, 2)
    lists = [
        item_lists(lax.dynamic_index_in_dim(allowed, c, 2, keepdims=False).reshape(2 * CHIPS, 2 * CHIPS), mine_tiles)
        for c in (core, 1 - core)
    ]
    got, lists, source, weights = lax.optimization_barrier((got, lists, source, weights))
    got_other = swap(got)

    def project(block, weight):
        both = jnp.concatenate([block, swap(block)], axis=0)
        return jnp.dot(both, weight, preferred_element_type=jnp.float32)

    def by_rows(total):
        mine, theirs = total[:TILE], total[TILE:]
        return jnp.where(core == 0, mine, theirs), jnp.where(core == 0, theirs, mine)

    attended = attend(lists[1], got, got_other, attend(lists[0], got))
    own_rows = select(source, exchange(attended.reshape(CHIPS, 2, TILE, TILE)))

    residual = residual_in.astype(jnp.float32).reshape(2, 2, TILE, -1)
    width = PLANE_HEADS * TILE // 2
    halves = []
    for sub, own in enumerate(own_rows):
        below, above = along_y(own, 1), along_y(own, 3)
        far_low, far_high = along_y(below[:, :width], 1), along_y(above[:, width:], 3)
        total = project(own, weights[0]) + project(below, weights[1]) + project(above, weights[2])
        near = lax.optimization_barrier([residual[c, sub] + gate_scale * rows for c, rows in enumerate(by_rows(total))])
        far = project(jnp.concatenate([far_low, far_high], axis=1), weights[3])
        halves.append([(near[c] + gate_scale * rows).astype(jnp.bfloat16) for c, rows in enumerate(by_rows(far))])
    return jnp.concatenate([halves[0][0], halves[1][0], halves[0][1], halves[1][1]], axis=0)


def solution(mesh):
    fine = Mesh(mesh.devices.reshape(4, 4, 4, 2), ("x", "z", "y", "c"))
    seq, rep = TOKENS_AXES, ("y", "c")
    in_specs = (
        P(seq, rep),
        P(seq, None),
        P(seq, None),
        P(seq, None),
        P(None, rep),
        P(rep),
        P(),
    )
    return jax.shard_map(shards, mesh=fine, in_specs=in_specs, out_specs=P(seq, rep), check_vma=False)
```

```python
import functools

import jax
import jax.numpy as jnp
from jax import lax
from jax.experimental import pallas as pl
from jax.experimental.pallas import tpu as pltpu
from jax.sharding import Mesh
from jax.sharding import PartitionSpec as P

TILE = 128
HEADS = 40
PLANES = 4
PLANE_HEADS = HEADS // PLANES
CHIPS = 16
HALF = 256
GROUP = 4
UNROLL = 16
ITEMS = 256
LOG2E = 1.4426950408889634
TOKENS_AXES = ("x", "z")
LOW = -1e30


def head_plan(work):
    ids = jnp.arange(HEADS)
    ahead = (work[None, :] > work[:, None]) | ((work[None, :] == work[:, None]) & (ids[None, :] < ids[:, None]))
    rank = jnp.sum(ahead.astype(jnp.int32), axis=1)
    row, col = rank // PLANES, rank % PLANES
    plane = jnp.where(row % 2 == 1, PLANES - 1 - col, col)
    place = plane * PLANE_HEADS + row
    hit = (place[None, :] == ids[:, None]).astype(jnp.int32)
    head_at = jnp.sum(hit * ids[None, :], axis=1)
    work_at = jnp.sum(hit * work[None, :], axis=1)
    return head_at, work_at


def chip_plan(work_at):
    extra = CHIPS - PLANE_HEADS
    quota = (work_at[:, None].astype(jnp.float32) / jnp.arange(1, extra + 1).astype(jnp.float32)[None, :]).reshape(-1)
    ids = jnp.arange(quota.shape[0])
    ahead = (quota[None, :] > quota[:, None]) | ((quota[None, :] == quota[:, None]) & (ids[None, :] < ids[:, None]))
    won = (jnp.sum(ahead.astype(jnp.int32), axis=1) < extra).astype(jnp.int32)
    chips = 1 + jnp.sum(won.reshape(PLANE_HEADS, extra), axis=1)
    slots = jnp.arange(PLANE_HEADS)
    first = jnp.sum(jnp.where(slots[None, :] < slots[:, None], chips[None, :], 0), axis=1)
    return chips, first


def pack_kernel(heads, q_ref, k_ref, v_ref, out_ref, held, turned, sem_in, sem_out):
    start = pl.multiple_of(heads[CHIPS] * HALF, HALF)
    rows = pl.ds(start, HALF)
    loads, stores = [], []
    for t in range(CHIPS):
        cols = pl.ds(pl.multiple_of(heads[t] * TILE, TILE), TILE)
        loads.append(
            [
                pltpu.make_async_copy(k_ref.at[rows, cols], held.at[t, pl.ds(0, HALF)], sem_in.at[t, 0]),
                pltpu.make_async_copy(v_ref.at[rows, cols], held.at[t, pl.ds(HALF, HALF)], sem_in.at[t, 1]),
                pltpu.make_async_copy(q_ref.at[rows, cols], held.at[t, pl.ds(2 * HALF, HALF)], sem_in.at[t, 2]),
            ]
        )
        for load in loads[-1]:
            load.start()
    for t in range(CHIPS):
        for load in loads[t]:
            load.wait()
        for sub in range(2):
            part = pl.ds(sub * TILE, TILE)
            turned[t, part, :] = held[t, pl.ds(HALF + sub * TILE, TILE), :].T
        stores += [
            pltpu.make_async_copy(held.at[t, pl.ds(0, HALF)], out_ref.at[t, pl.ds(0, HALF)], sem_out.at[t, 0]),
            pltpu.make_async_copy(turned.at[t], out_ref.at[t, pl.ds(HALF, HALF)], sem_out.at[t, 1]),
            pltpu.make_async_copy(
                held.at[t, pl.ds(2 * HALF, HALF)], out_ref.at[t, pl.ds(2 * HALF, HALF)], sem_out.at[t, 2]
            ),
        ]
        for store in stores[-3:]:
            store.start()
    for store in stores:
        store.wait()


def pack(queries, keys, values, chip_heads, core):
    scalars = jnp.concatenate([chip_heads, core[None]]).astype(jnp.int32)
    hbm = pl.BlockSpec(memory_space=pl.ANY)
    return pl.pallas_call(
        pack_kernel,
        in_specs=[pl.BlockSpec(memory_space=pltpu.SMEM)] + [hbm] * 3,
        out_specs=hbm,
        out_shape=jax.ShapeDtypeStruct((CHIPS, 6 * TILE, TILE), jnp.bfloat16),
        scratch_shapes=[
            pltpu.VMEM((CHIPS, 3 * HALF, TILE), jnp.bfloat16),
            pltpu.VMEM((CHIPS, HALF, TILE), jnp.bfloat16),
            pltpu.SemaphoreType.DMA((CHIPS, 3)),
            pltpu.SemaphoreType.DMA((CHIPS, 3)),
        ],
        compiler_params=pltpu.CompilerParams(vmem_limit_bytes=60 * 2**20),
    )(scalars, queries, keys, values)


def attend_items(scale, meta, q_of, k_of, valid_of, query_ref, key_ref, acc_ref, max_ref, sum_ref):
    def body(step, _):
        parts = []
        for u in range(UNROLL):
            e = step * UNROLL + u
            t = q_of[e]
            kid = [k_of[e * GROUP + g] for g in range(GROUP)]
            valid = valid_of[e]
            keys = jnp.concatenate([key_ref[i // 2, i % 2] for i in kid], axis=0)
            scores = lax.dot_general(
                keys, query_ref[t // 2, 4 + t % 2], (((1,), (1,)), ((), ())), preferred_element_type=jnp.float32
            )
            top = jnp.max(scores, axis=0, keepdims=True) * scale
            weights = []
            total = jnp.zeros((1, TILE), jnp.float32)
            for g in range(GROUP):
                shift = top + jnp.where(g < valid, 0.0, -LOW)
                w = jnp.exp2(scores[g * TILE : (g + 1) * TILE] * scale - shift)
                total = total + jnp.sum(w, axis=0, keepdims=True)
                weights.append(w.astype(jnp.bfloat16))
            vals = jnp.concatenate([key_ref[i // 2, 2 + i % 2] for i in kid], axis=1)
            part = jnp.dot(vals, jnp.concatenate(weights, axis=0), preferred_element_type=jnp.float32)
            parts.append((t, top, total, part))
        for t, top, total, part in parts:
            old = max_ref[t]
            new = jnp.maximum(old, top)
            a = jnp.exp2(old - new)
            b = jnp.exp2(top - new)
            max_ref[t] = new
            sum_ref[t] = sum_ref[t] * a + total * b
            acc_ref[t] = acc_ref[t] * a + part * b
        return 0

    lax.fori_loop(0, meta[0], body, 0)


def first_kernel(scale, meta, q_of, k_of, valid_of, own_ref, acc_ref, max_ref, sum_ref):
    acc_ref[...] = jnp.zeros_like(acc_ref)
    sum_ref[...] = jnp.zeros_like(sum_ref)
    max_ref[...] = jnp.full_like(max_ref, LOW)
    attend_items(scale, meta, q_of, k_of, valid_of, own_ref, own_ref, acc_ref, max_ref, sum_ref)


def second_kernel(scale, meta, q_of, k_of, valid_of, own_ref, other_ref, acc_in, max_in, sum_in, out_ref, acc_s, max_s, sum_s):
    acc_s[...] = acc_in[...]
    max_s[...] = max_in[...]
    sum_s[...] = sum_in[...]
    attend_items(scale, meta, q_of, k_of, valid_of, own_ref, other_ref, acc_s, max_s, sum_s)

    def finish(t, _):
        inverse = 1.0 / jnp.maximum(sum_s[t], 1e-30)
        out_ref[t // 2, t % 2] = (acc_s[t] * inverse).astype(jnp.bfloat16)
        return 0

    lax.fori_loop(0, 2 * CHIPS, finish, 0)


def attend(lists, own, other=None, state=None):
    tiles = 2 * CHIPS
    smem = pl.BlockSpec(memory_space=pltpu.SMEM)
    vmem = pl.BlockSpec(memory_space=pltpu.VMEM)
    shapes = [((tiles, TILE, TILE), jnp.float32), ((tiles, 1, TILE), jnp.float32), ((tiles, 1, TILE), jnp.float32)]
    options = dict(
        compiler_params=pltpu.CompilerParams(vmem_limit_bytes=24 * 2**20),
        cost_estimate=pl.CostEstimate(flops=4 * 10**9, bytes_accessed=8 * 2**20, transcendentals=4 * 10**6),
    )
    scale = TILE**-0.5 * LOG2E
    if other is None:
        return pl.pallas_call(
            functools.partial(first_kernel, scale),
            in_specs=[smem] * 4 + [vmem],
            out_specs=[vmem] * 3,
            out_shape=[jax.ShapeDtypeStruct(*shape) for shape in shapes],
            **options,
        )(*lists, own)
    return pl.pallas_call(
        functools.partial(second_kernel, scale),
        in_specs=[smem] * 4 + [vmem] * 5,
        out_specs=vmem,
        out_shape=jax.ShapeDtypeStruct((CHIPS, 2, TILE, TILE), jnp.bfloat16),
        scratch_shapes=[pltpu.VMEM(*shape) for shape in shapes],
        **options,
    )(*lists, own, other, *state)


def item_lists(allowed, mine):
    tiles = allowed.shape[1]
    count = jnp.sum(allowed, axis=1) * mine
    groups = (count + GROUP - 1) // GROUP
    slots = jnp.arange(groups.shape[0])
    end = jnp.sum(jnp.where(slots[None, :] <= slots[:, None], groups[None, :], 0), axis=1)
    steps = (end[-1] + UNROLL - 1) // UNROLL
    key_ids = jnp.arange(tiles)
    before = jnp.sum(allowed[:, None, :] * (key_ids[None, :] < key_ids[:, None])[None].astype(jnp.int32), axis=2)
    listed = jnp.sum(
        jnp.where((before[:, :, None] == key_ids[None, None, :]) & (allowed[:, :, None] > 0), key_ids[None, :, None], 0),
        axis=1,
    )
    item = jnp.arange(ITEMS)
    real = (item < end[-1]).astype(jnp.int32)
    held = jnp.maximum(jnp.minimum(item, end[-1] - 1), 0)
    q_of = jnp.minimum(jnp.sum((end[None, :] <= held[:, None]).astype(jnp.int32), axis=1), 2 * CHIPS - 1)
    pick = (q_of[:, None] == slots[None, :]).astype(jnp.int32)
    start = GROUP * (held - jnp.sum(pick * (end - groups)[None, :], axis=1))
    left = jnp.sum(pick * count[None, :], axis=1) - start
    rows = jnp.dot(pick.astype(jnp.float32), listed.astype(jnp.float32))
    offset = jnp.arange(GROUP)
    where = start[:, None] + jnp.where(offset[None, :] < left[:, None], offset[None, :], 0)
    k_of = jnp.sum(jnp.where(where[:, :, None] == key_ids[None, None, :], rows[:, None, :], 0.0), axis=2)
    valid = jnp.minimum(left, GROUP) * real
    return steps[None], q_of, k_of.astype(jnp.int32).reshape(-1), valid


def select_kernel(source, got_ref, out_ref):
    for sub in range(2):
        for i in range(PLANE_HEADS):
            out_ref[pl.ds(sub * TILE, TILE), pl.ds(i * TILE, TILE)] = got_ref[source[2 * i + sub], sub].T


def select(source, got):
    vmem = pl.BlockSpec(memory_space=pltpu.VMEM)
    return pl.pallas_call(
        select_kernel,
        in_specs=[pl.BlockSpec(memory_space=pltpu.SMEM), vmem],
        out_specs=vmem,
        out_shape=jax.ShapeDtypeStruct((HALF, PLANE_HEADS * TILE), jnp.bfloat16),
    )(source, got)


def gather_kernel(heads, w_ref, *rest):
    out_refs, (held, sem_in, sem_out) = rest[:PLANES], rest[PLANES:]
    loads, stores = [], []
    for n in range(HEADS):
        rows = pl.ds(pl.multiple_of(heads[n] * TILE, TILE), TILE)
        loads.append(pltpu.make_async_copy(w_ref.at[rows], held.at[n], sem_in.at[n]))
        loads[n].start()
    for n in range(HEADS):
        loads[n].wait()
        part = out_refs[n // PLANE_HEADS].at[pl.ds(n % PLANE_HEADS * TILE, TILE)]
        stores.append(pltpu.make_async_copy(held.at[n], part, sem_out.at[n]))
        stores[n].start()
    for store in stores:
        store.wait()


def gather(w_out, heads):
    cols = w_out.shape[1]
    hbm = pl.BlockSpec(memory_space=pl.ANY)
    return pl.pallas_call(
        gather_kernel,
        in_specs=[pl.BlockSpec(memory_space=pltpu.SMEM), hbm],
        out_specs=[hbm] * PLANES,
        out_shape=[jax.ShapeDtypeStruct((PLANE_HEADS * TILE, cols), w_out.dtype)] * PLANES,
        scratch_shapes=[
            pltpu.VMEM((HEADS, TILE, cols), w_out.dtype),
            pltpu.SemaphoreType.DMA((HEADS,)),
            pltpu.SemaphoreType.DMA((HEADS,)),
        ],
        compiler_params=pltpu.CompilerParams(vmem_limit_bytes=56 * 2**20),
    )(heads, w_out)


def exchange(block):
    return lax.all_to_all(block, TOKENS_AXES, split_axis=0, concat_axis=0, tiled=True)


def along_y(block, step):
    return lax.ppermute(block, "y", [(i, (i + step) % PLANES) for i in range(PLANES)])


def swap(block):
    return lax.ppermute(block, "c", [(0, 1), (1, 0)])


def shards(residual_in, queries, keys, values, w_out, gate_scale, tile_mask):
    chip = lax.axis_index("x") * 4 + lax.axis_index("z")
    plane = lax.axis_index("y")
    core = lax.axis_index("c")
    tile_work = jnp.sum(tile_mask, axis=1)
    head_at, work_at = head_plan(jnp.sum(tile_work, axis=1))
    plane_heads = lax.dynamic_slice_in_dim(head_at, plane * PLANE_HEADS, PLANE_HEADS)
    chips, first = chip_plan(lax.dynamic_slice_in_dim(work_at, plane * PLANE_HEADS, PLANE_HEADS))
    chip_ids = jnp.arange(CHIPS)
    on_chip = (first[None, :] <= chip_ids[:, None]) & (chip_ids[:, None] < (first + chips)[None, :])
    chip_heads = jnp.sum(jnp.where(on_chip, plane_heads[None, :], 0), axis=1)
    got = exchange(pack(queries, keys, values, chip_heads, core)).reshape(CHIPS, 6, TILE, TILE)

    half_work = lax.dynamic_index_in_dim(tile_work.reshape(HEADS, CHIPS, 2, 2), core, 2, keepdims=False)
    half_work = jnp.take(half_work.reshape(HEADS, 2 * CHIPS), plane_heads, axis=0, mode="clip")
    tile_ids = jnp.arange(2 * CHIPS)
    done = jnp.sum(
        jnp.where((tile_ids[None, :] < tile_ids[:, None])[None], half_work[:, None, :], 0), axis=2
    )
    total = jnp.sum(half_work, axis=1, keepdims=True)
    owner = first[:, None] + ((2 * done + half_work) * chips[:, None]) // (2 * total)
    my_slot = jnp.sum(jnp.where(on_chip[chip], jnp.arange(PLANE_HEADS), 0))
    my_head = chip_heads[chip]
    mine_tiles = (owner[my_slot] == chip).astype(jnp.int32)
    allowed = lax.dynamic_index_in_dim(tile_mask, my_head, 0, keepdims=False)
    allowed = lax.dynamic_index_in_dim(allowed.reshape(CHIPS, 2, 2, 4 * CHIPS), core, 1, keepdims=False)
    source = lax.dynamic_slice_in_dim(owner, 2 * chip, 2, 1).reshape(-1)

    w_order = jnp.concatenate(
        [lax.dynamic_slice_in_dim(head_at, (plane + k) % PLANES * PLANE_HEADS, PLANE_HEADS) for k in (0, 3, 1, 2)]
    )
    weights = gather(w_out, w_order)
    allowed = allowed.reshape(2 * CHIPS, CHIPS, 2, 2)
    lists = [
        item_lists(lax.dynamic_index_in_dim(allowed, c, 2, keepdims=False).reshape(2 * CHIPS, 2 * CHIPS), mine_tiles)
        for c in (core, 1 - core)
    ]
    got, lists, source, weights = lax.optimization_barrier((got, lists, source, weights))
    got_other = swap(got)

    def project(block, weight):
        both = jnp.concatenate([block, swap(block)], axis=0)
        return jnp.dot(both, weight, preferred_element_type=jnp.float32)

    def by_rows(total):
        mine, theirs = total[:HALF], total[HALF:]
        return jnp.concatenate([jnp.where(core == 0, mine, theirs), jnp.where(core == 0, theirs, mine)], axis=0)

    attended = attend(lists[1], got, got_other, attend(lists[0], got))
    own = select(source, exchange(attended))
    below, above = along_y(own, 1), along_y(own, 3)
    width = PLANE_HEADS * TILE // 2
    far_low, far_high = along_y(below[:, :width], 1), along_y(above[:, width:], 3)
    total = project(own, weights[0]) + project(below, weights[1]) + project(above, weights[2])
    base = residual_in.astype(jnp.float32) + gate_scale * by_rows(total)
    base, far_low, far_high = lax.optimization_barrier((base, far_low, far_high))
    far = project(far_low, weights[3][:width]) + project(far_high, weights[3][width:])
    return (base + gate_scale * by_rows(far)).astype(jnp.bfloat16)


def solution(mesh):
    fine = Mesh(mesh.devices.reshape(4, 4, 4, 2), ("x", "z", "y", "c"))
    seq, rep = TOKENS_AXES, ("y", "c")
    in_specs = (
        P(seq, rep),
        P(seq, None),
        P(seq, None),
        P(seq, None),
        P(None, rep),
        P(rep),
        P(),
    )
    return jax.shard_map(shards, mesh=fine, in_specs=in_specs, out_specs=P(seq, rep), check_vma=False)
```

```python
import functools

import jax
import jax.numpy as jnp
from jax import lax
from jax.experimental import pallas as pl
from jax.experimental.pallas import tpu as pltpu
from jax.sharding import Mesh
from jax.sharding import PartitionSpec as P

TILE = 128
HEADS = 40
PLANES = 4
PLANE_HEADS = HEADS // PLANES
PART_HEADS = PLANE_HEADS // 2
CHIPS = 16
HALF = 256
GROUP = 4
UNROLL = 16
ITEMS = 256
LOG2E = 1.4426950408889634
TOKENS_AXES = ("x", "z")
LOW = -1e30


def head_plan(work):
    ids = jnp.arange(HEADS)
    ahead = (work[None, :] > work[:, None]) | ((work[None, :] == work[:, None]) & (ids[None, :] < ids[:, None]))
    rank = jnp.sum(ahead.astype(jnp.int32), axis=1)
    row, col = rank // PLANES, rank % PLANES
    plane = jnp.where(row % 2 == 1, PLANES - 1 - col, col)
    place = plane * PLANE_HEADS + row
    hit = (place[None, :] == ids[:, None]).astype(jnp.int32)
    head_at = jnp.sum(hit * ids[None, :], axis=1)
    work_at = jnp.sum(hit * work[None, :], axis=1)
    return head_at, work_at


def chip_plan(work_at):
    extra = CHIPS - PLANE_HEADS
    quota = (work_at[:, None].astype(jnp.float32) / jnp.arange(1, extra + 1).astype(jnp.float32)[None, :]).reshape(-1)
    ids = jnp.arange(quota.shape[0])
    ahead = (quota[None, :] > quota[:, None]) | ((quota[None, :] == quota[:, None]) & (ids[None, :] < ids[:, None]))
    won = (jnp.sum(ahead.astype(jnp.int32), axis=1) < extra).astype(jnp.int32)
    chips = 1 + jnp.sum(won.reshape(PLANE_HEADS, extra), axis=1)
    slots = jnp.arange(PLANE_HEADS)
    first = jnp.sum(jnp.where(slots[None, :] < slots[:, None], chips[None, :], 0), axis=1)
    return chips, first


def pack_kernel(heads, q_ref, k_ref, v_ref, out_ref, held, turned, sem_in, sem_out):
    start = pl.multiple_of(heads[CHIPS] * HALF, HALF)
    rows = pl.ds(start, HALF)
    loads, stores = [], []
    for t in range(CHIPS):
        cols = pl.ds(pl.multiple_of(heads[t] * TILE, TILE), TILE)
        loads.append(
            [
                pltpu.make_async_copy(k_ref.at[rows, cols], held.at[t, pl.ds(0, HALF)], sem_in.at[t, 0]),
                pltpu.make_async_copy(v_ref.at[rows, cols], held.at[t, pl.ds(HALF, HALF)], sem_in.at[t, 1]),
                pltpu.make_async_copy(q_ref.at[rows, cols], held.at[t, pl.ds(2 * HALF, HALF)], sem_in.at[t, 2]),
            ]
        )
        for load in loads[-1]:
            load.start()
    for t in range(CHIPS):
        for load in loads[t]:
            load.wait()
        for sub in range(2):
            part = pl.ds(sub * TILE, TILE)
            turned[t, part, :] = held[t, pl.ds(HALF + sub * TILE, TILE), :].T
        stores += [
            pltpu.make_async_copy(held.at[t, pl.ds(0, HALF)], out_ref.at[t, pl.ds(0, HALF)], sem_out.at[t, 0]),
            pltpu.make_async_copy(turned.at[t], out_ref.at[t, pl.ds(HALF, HALF)], sem_out.at[t, 1]),
            pltpu.make_async_copy(
                held.at[t, pl.ds(2 * HALF, HALF)], out_ref.at[t, pl.ds(2 * HALF, HALF)], sem_out.at[t, 2]
            ),
        ]
        for store in stores[-3:]:
            store.start()
    for store in stores:
        store.wait()


def pack(queries, keys, values, chip_heads, core):
    scalars = jnp.concatenate([chip_heads, core[None]]).astype(jnp.int32)
    hbm = pl.BlockSpec(memory_space=pl.ANY)
    return pl.pallas_call(
        pack_kernel,
        in_specs=[pl.BlockSpec(memory_space=pltpu.SMEM)] + [hbm] * 3,
        out_specs=hbm,
        out_shape=jax.ShapeDtypeStruct((CHIPS, 6 * TILE, TILE), jnp.bfloat16),
        scratch_shapes=[
            pltpu.VMEM((CHIPS, 3 * HALF, TILE), jnp.bfloat16),
            pltpu.VMEM((CHIPS, HALF, TILE), jnp.bfloat16),
            pltpu.SemaphoreType.DMA((CHIPS, 3)),
            pltpu.SemaphoreType.DMA((CHIPS, 3)),
        ],
        compiler_params=pltpu.CompilerParams(vmem_limit_bytes=60 * 2**20),
    )(scalars, queries, keys, values)


def attend_items(scale, meta, q_of, k_of, valid_of, query_ref, key_ref, acc_ref, max_ref, sum_ref):
    def body(step, _):
        parts = []
        for u in range(UNROLL):
            e = step * UNROLL + u
            t = q_of[e]
            kid = [k_of[e * GROUP + g] for g in range(GROUP)]
            valid = valid_of[e]
            keys = jnp.concatenate([key_ref[i // 2, i % 2] for i in kid], axis=0)
            scores = lax.dot_general(
                keys, query_ref[t // 2, 4 + t % 2], (((1,), (1,)), ((), ())), preferred_element_type=jnp.float32
            )
            top = jnp.max(scores, axis=0, keepdims=True) * scale
            weights = []
            total = jnp.zeros((1, TILE), jnp.float32)
            for g in range(GROUP):
                shift = top + jnp.where(g < valid, 0.0, -LOW)
                w = jnp.exp2(scores[g * TILE : (g + 1) * TILE] * scale - shift)
                total = total + jnp.sum(w, axis=0, keepdims=True)
                weights.append(w.astype(jnp.bfloat16))
            vals = jnp.concatenate([key_ref[i // 2, 2 + i % 2] for i in kid], axis=1)
            part = jnp.dot(vals, jnp.concatenate(weights, axis=0), preferred_element_type=jnp.float32)
            parts.append((t, top, total, part))
        for t, top, total, part in parts:
            old = max_ref[t]
            new = jnp.maximum(old, top)
            a = jnp.exp2(old - new)
            b = jnp.exp2(top - new)
            max_ref[t] = new
            sum_ref[t] = sum_ref[t] * a + total * b
            acc_ref[t] = acc_ref[t] * a + part * b
        return 0

    lax.fori_loop(0, meta[0], body, 0)


def first_kernel(scale, meta, q_of, k_of, valid_of, own_ref, acc_ref, max_ref, sum_ref):
    acc_ref[...] = jnp.zeros_like(acc_ref)
    sum_ref[...] = jnp.zeros_like(sum_ref)
    max_ref[...] = jnp.full_like(max_ref, LOW)
    attend_items(scale, meta, q_of, k_of, valid_of, own_ref, own_ref, acc_ref, max_ref, sum_ref)


def second_kernel(scale, meta, q_of, k_of, valid_of, own_ref, other_ref, acc_in, max_in, sum_in, out_ref, acc_s, max_s, sum_s):
    acc_s[...] = acc_in[...]
    max_s[...] = max_in[...]
    sum_s[...] = sum_in[...]
    attend_items(scale, meta, q_of, k_of, valid_of, own_ref, other_ref, acc_s, max_s, sum_s)

    def finish(t, _):
        inverse = 1.0 / jnp.maximum(sum_s[t], 1e-30)
        out_ref[t // 2, t % 2] = (acc_s[t] * inverse).astype(jnp.bfloat16)
        return 0

    lax.fori_loop(0, 2 * CHIPS, finish, 0)


def attend(lists, own, other=None, state=None):
    tiles = 2 * CHIPS
    smem = pl.BlockSpec(memory_space=pltpu.SMEM)
    vmem = pl.BlockSpec(memory_space=pltpu.VMEM)
    shapes = [((tiles, TILE, TILE), jnp.float32), ((tiles, 1, TILE), jnp.float32), ((tiles, 1, TILE), jnp.float32)]
    options = dict(
        compiler_params=pltpu.CompilerParams(vmem_limit_bytes=24 * 2**20),
        cost_estimate=pl.CostEstimate(flops=4 * 10**9, bytes_accessed=8 * 2**20, transcendentals=4 * 10**6),
    )
    scale = TILE**-0.5 * LOG2E
    if other is None:
        return pl.pallas_call(
            functools.partial(first_kernel, scale),
            in_specs=[smem] * 4 + [vmem],
            out_specs=[vmem] * 3,
            out_shape=[jax.ShapeDtypeStruct(*shape) for shape in shapes],
            **options,
        )(*lists, own)
    return pl.pallas_call(
        functools.partial(second_kernel, scale),
        in_specs=[smem] * 4 + [vmem] * 5,
        out_specs=vmem,
        out_shape=jax.ShapeDtypeStruct((CHIPS, 2, TILE, TILE), jnp.bfloat16),
        scratch_shapes=[pltpu.VMEM(*shape) for shape in shapes],
        **options,
    )(*lists, own, other, *state)


def item_lists(allowed, mine):
    tiles = allowed.shape[1]
    count = jnp.sum(allowed, axis=1) * mine
    groups = (count + GROUP - 1) // GROUP
    slots = jnp.arange(groups.shape[0])
    end = jnp.sum(jnp.where(slots[None, :] <= slots[:, None], groups[None, :], 0), axis=1)
    steps = (end[-1] + UNROLL - 1) // UNROLL
    key_ids = jnp.arange(tiles)
    before = jnp.sum(allowed[:, None, :] * (key_ids[None, :] < key_ids[:, None])[None].astype(jnp.int32), axis=2)
    listed = jnp.sum(
        jnp.where((before[:, :, None] == key_ids[None, None, :]) & (allowed[:, :, None] > 0), key_ids[None, :, None], 0),
        axis=1,
    )
    item = jnp.arange(ITEMS)
    real = (item < end[-1]).astype(jnp.int32)
    held = jnp.maximum(jnp.minimum(item, end[-1] - 1), 0)
    q_of = jnp.minimum(jnp.sum((end[None, :] <= held[:, None]).astype(jnp.int32), axis=1), 2 * CHIPS - 1)
    pick = (q_of[:, None] == slots[None, :]).astype(jnp.int32)
    start = GROUP * (held - jnp.sum(pick * (end - groups)[None, :], axis=1))
    left = jnp.sum(pick * count[None, :], axis=1) - start
    rows = jnp.dot(pick.astype(jnp.float32), listed.astype(jnp.float32))
    offset = jnp.arange(GROUP)
    where = start[:, None] + jnp.where(offset[None, :] < left[:, None], offset[None, :], 0)
    k_of = jnp.sum(jnp.where(where[:, :, None] == key_ids[None, None, :], rows[:, None, :], 0.0), axis=2)
    valid = jnp.minimum(left, GROUP) * real
    return steps[None], q_of, k_of.astype(jnp.int32).reshape(-1), valid


def select_kernel(source, got_ref, out_ref, low_ref, high_ref):
    for i in range(PLANE_HEADS):
        part_ref, at = (low_ref, i) if i < PART_HEADS else (high_ref, i - PART_HEADS)
        for sub in range(2):
            rows = pl.ds(sub * TILE, TILE)
            tile = got_ref[source[2 * i + sub], sub].T
            out_ref[rows, pl.ds(i * TILE, TILE)] = tile
            part_ref[rows, pl.ds(at * TILE, TILE)] = tile


def select(source, got):
    vmem = pl.BlockSpec(memory_space=pltpu.VMEM)
    return pl.pallas_call(
        select_kernel,
        in_specs=[pl.BlockSpec(memory_space=pltpu.SMEM), vmem],
        out_specs=[vmem] * 3,
        out_shape=[
            jax.ShapeDtypeStruct((HALF, heads * TILE), jnp.bfloat16) for heads in (PLANE_HEADS, PART_HEADS, PART_HEADS)
        ],
    )(source, got)


def gather_kernel(counts, heads, w_ref, *rest):
    out_refs, (held, sem_in, sem_out) = rest[: len(counts)], rest[len(counts) :]
    loads, stores = [], []
    for n in range(HEADS):
        rows = pl.ds(pl.multiple_of(heads[n] * TILE, TILE), TILE)
        loads.append(pltpu.make_async_copy(w_ref.at[rows], held.at[n], sem_in.at[n]))
        loads[n].start()
    n = 0
    for out_ref, count in zip(out_refs, counts):
        for at in range(count):
            loads[n].wait()
            stores.append(pltpu.make_async_copy(held.at[n], out_ref.at[pl.ds(at * TILE, TILE)], sem_out.at[n]))
            stores[n].start()
            n += 1
    for store in stores:
        store.wait()


def gather(w_out, heads, counts):
    cols = w_out.shape[1]
    hbm = pl.BlockSpec(memory_space=pl.ANY)
    return pl.pallas_call(
        functools.partial(gather_kernel, counts),
        in_specs=[pl.BlockSpec(memory_space=pltpu.SMEM), hbm],
        out_specs=[hbm] * len(counts),
        out_shape=[jax.ShapeDtypeStruct((count * TILE, cols), w_out.dtype) for count in counts],
        scratch_shapes=[
            pltpu.VMEM((HEADS, TILE, cols), w_out.dtype),
            pltpu.SemaphoreType.DMA((HEADS,)),
            pltpu.SemaphoreType.DMA((HEADS,)),
        ],
        compiler_params=pltpu.CompilerParams(vmem_limit_bytes=56 * 2**20),
    )(heads, w_out)


def exchange(block):
    return lax.all_to_all(block, TOKENS_AXES, split_axis=0, concat_axis=0, tiled=True)


def along_y(block, step):
    return lax.ppermute(block, "y", [(i, (i + step) % PLANES) for i in range(PLANES)])


def swap(block):
    return lax.ppermute(block, "c", [(0, 1), (1, 0)])


def shards(residual_in, queries, keys, values, w_out, gate_scale, tile_mask):
    chip = lax.axis_index("x") * 4 + lax.axis_index("z")
    plane = lax.axis_index("y")
    core = lax.axis_index("c")
    tile_work = jnp.sum(tile_mask, axis=1)
    head_at, work_at = head_plan(jnp.sum(tile_work, axis=1))
    plane_heads = lax.dynamic_slice_in_dim(head_at, plane * PLANE_HEADS, PLANE_HEADS)
    chips, first = chip_plan(lax.dynamic_slice_in_dim(work_at, plane * PLANE_HEADS, PLANE_HEADS))
    chip_ids = jnp.arange(CHIPS)
    on_chip = (first[None, :] <= chip_ids[:, None]) & (chip_ids[:, None] < (first + chips)[None, :])
    chip_heads = jnp.sum(jnp.where(on_chip, plane_heads[None, :], 0), axis=1)
    got = exchange(pack(queries, keys, values, chip_heads, core)).reshape(CHIPS, 6, TILE, TILE)

    half_work = lax.dynamic_index_in_dim(tile_work.reshape(HEADS, CHIPS, 2, 2), core, 2, keepdims=False)
    half_work = jnp.take(half_work.reshape(HEADS, 2 * CHIPS), plane_heads, axis=0, mode="clip")
    tile_ids = jnp.arange(2 * CHIPS)
    done = jnp.sum(
        jnp.where((tile_ids[None, :] < tile_ids[:, None])[None], half_work[:, None, :], 0), axis=2
    )
    total = jnp.sum(half_work, axis=1, keepdims=True)
    owner = first[:, None] + ((2 * done + half_work) * chips[:, None]) // (2 * total)
    my_slot = jnp.sum(jnp.where(on_chip[chip], jnp.arange(PLANE_HEADS), 0))
    my_head = chip_heads[chip]
    mine_tiles = (owner[my_slot] == chip).astype(jnp.int32)
    allowed = lax.dynamic_index_in_dim(tile_mask, my_head, 0, keepdims=False)
    allowed = lax.dynamic_index_in_dim(allowed.reshape(CHIPS, 2, 2, 4 * CHIPS), core, 1, keepdims=False)
    source = lax.dynamic_slice_in_dim(owner, 2 * chip, 2, 1).reshape(-1)

    w_order = jnp.concatenate(
        [lax.dynamic_slice_in_dim(head_at, (plane + k) % PLANES * PLANE_HEADS, PLANE_HEADS) for k in (0, 3, 1, 2)]
    )
    weights = gather(w_out, w_order, (PLANE_HEADS,) + (PART_HEADS,) * 6)
    allowed = allowed.reshape(2 * CHIPS, CHIPS, 2, 2)
    lists = [
        item_lists(lax.dynamic_index_in_dim(allowed, c, 2, keepdims=False).reshape(2 * CHIPS, 2 * CHIPS), mine_tiles)
        for c in (core, 1 - core)
    ]
    got, lists, source, weights = lax.optimization_barrier((got, lists, source, weights))
    got_other = swap(got)

    def product(block, other, weight):
        return jnp.dot(jnp.concatenate([block, other], axis=0), weight, preferred_element_type=jnp.float32)

    def project(block, weight):
        return product(block, swap(block), weight)

    def by_rows(total):
        mine, theirs = total[:HALF], total[HALF:]
        return jnp.concatenate([jnp.where(core == 0, mine, theirs), jnp.where(core == 0, theirs, mine)], axis=0)

    attended = attend(lists[1], got, got_other, attend(lists[0], got))
    own, low, high = select(source, exchange(attended))
    below_low, above_high = along_y(low, 1), along_y(high, 3)
    own_other, low, high = lax.optimization_barrier((swap(own), low, high))
    below_high, above_low = along_y(high, 1), along_y(low, 3)
    far_low, far_high = along_y(below_low, 1), along_y(above_high, 3)
    total = product(own, own_other, weights[0])
    for block, weight in zip((below_low, above_high, below_high, above_low), (weights[1], weights[4], weights[2], weights[3])):
        total = total + project(block, weight)
    base = residual_in.astype(jnp.float32) + gate_scale * by_rows(total)
    base, far_low, far_high = lax.optimization_barrier((base, far_low, far_high))
    far = project(far_low, weights[5]) + project(far_high, weights[6])
    return (base + gate_scale * by_rows(far)).astype(jnp.bfloat16)


def solution(mesh):
    fine = Mesh(mesh.devices.reshape(4, 4, 4, 2), ("x", "z", "y", "c"))
    seq, rep = TOKENS_AXES, ("y", "c")
    in_specs = (
        P(seq, rep),
        P(seq, None),
        P(seq, None),
        P(seq, None),
        P(None, rep),
        P(rep),
        P(),
    )
    return jax.shard_map(shards, mesh=fine, in_specs=in_specs, out_specs=P(seq, rep), check_vma=False)
```

```python
import functools

import jax
import jax.numpy as jnp
from jax import lax
from jax.experimental import pallas as pl
from jax.experimental.pallas import tpu as pltpu
from jax.sharding import Mesh
from jax.sharding import PartitionSpec as P

TILE = 128
HEADS = 40
PLANES = 4
PLANE_HEADS = HEADS // PLANES
PART_HEADS = PLANE_HEADS // 2
CHIPS = 16
HALF = 256
GROUP = 4
UNROLL = 16
ITEMS = 256
LOG2E = 1.4426950408889634
TOKENS_AXES = ("x", "z")
LOW = -1e30


def head_plan(work):
    ids = jnp.arange(HEADS)
    ahead = (work[None, :] > work[:, None]) | ((work[None, :] == work[:, None]) & (ids[None, :] < ids[:, None]))
    rank = jnp.sum(ahead.astype(jnp.int32), axis=1)
    row, col = rank // PLANES, rank % PLANES
    plane = jnp.where(row % 2 == 1, PLANES - 1 - col, col)
    place = plane * PLANE_HEADS + row
    hit = (place[None, :] == ids[:, None]).astype(jnp.int32)
    head_at = jnp.sum(hit * ids[None, :], axis=1)
    work_at = jnp.sum(hit * work[None, :], axis=1)
    return head_at, work_at


def chip_plan(work_at):
    extra = CHIPS - PLANE_HEADS
    quota = (work_at[:, None].astype(jnp.float32) / jnp.arange(1, extra + 1).astype(jnp.float32)[None, :]).reshape(-1)
    ids = jnp.arange(quota.shape[0])
    ahead = (quota[None, :] > quota[:, None]) | ((quota[None, :] == quota[:, None]) & (ids[None, :] < ids[:, None]))
    won = (jnp.sum(ahead.astype(jnp.int32), axis=1) < extra).astype(jnp.int32)
    chips = 1 + jnp.sum(won.reshape(PLANE_HEADS, extra), axis=1)
    slots = jnp.arange(PLANE_HEADS)
    first = jnp.sum(jnp.where(slots[None, :] < slots[:, None], chips[None, :], 0), axis=1)
    return chips, first


def pack_kernel(heads, q_ref, k_ref, v_ref, out_ref, held, values, sem_v, sem_kq, sem_out):
    rows = pl.ds(pl.multiple_of(heads[CHIPS] * HALF, HALF), HALF)
    cols = [pl.ds(pl.multiple_of(heads[t] * TILE, TILE), TILE) for t in range(CHIPS)]
    first = [pltpu.make_async_copy(v_ref.at[rows, cols[t]], values.at[t], sem_v.at[t]) for t in range(CHIPS)]
    others = [
        pltpu.make_async_copy(ref.at[rows, cols[t]], held.at[t, pl.ds(at * HALF, HALF)], sem_kq.at[t, at // 2])
        for t in range(CHIPS)
        for ref, at in ((k_ref, 0), (q_ref, 2))
    ]
    for load in first + others:
        load.start()
    stores = []
    for t in range(CHIPS):
        first[t].wait()
        for sub in range(2):
            held[t, pl.ds(HALF + sub * TILE, TILE), :] = values[t, pl.ds(sub * TILE, TILE), :].T
        for load in others[2 * t : 2 * t + 2]:
            load.wait()
        stores.append(pltpu.make_async_copy(held.at[t], out_ref.at[t], sem_out.at[t]))
        stores[t].start()
    for store in stores:
        store.wait()


def pack(queries, keys, values, chip_heads, core):
    scalars = jnp.concatenate([chip_heads, core[None]]).astype(jnp.int32)
    hbm = pl.BlockSpec(memory_space=pl.ANY)
    return pl.pallas_call(
        pack_kernel,
        in_specs=[pl.BlockSpec(memory_space=pltpu.SMEM)] + [hbm] * 3,
        out_specs=hbm,
        out_shape=jax.ShapeDtypeStruct((CHIPS, 6 * TILE, TILE), jnp.bfloat16),
        scratch_shapes=[
            pltpu.VMEM((CHIPS, 3 * HALF, TILE), jnp.bfloat16),
            pltpu.VMEM((CHIPS, HALF, TILE), jnp.bfloat16),
            pltpu.SemaphoreType.DMA((CHIPS,)),
            pltpu.SemaphoreType.DMA((CHIPS, 2)),
            pltpu.SemaphoreType.DMA((CHIPS,)),
        ],
        compiler_params=pltpu.CompilerParams(vmem_limit_bytes=60 * 2**20),
    )(scalars, queries, keys, values)


def attend_items(scale, meta, q_of, k_of, valid_of, query_ref, key_ref, acc_ref, max_ref, sum_ref):
    def body(step, _):
        parts = []
        for u in range(UNROLL):
            e = step * UNROLL + u
            t = q_of[e]
            kid = [k_of[e * GROUP + g] for g in range(GROUP)]
            valid = valid_of[e]
            keys = jnp.concatenate([key_ref[i // 2, i % 2] for i in kid], axis=0)
            scores = lax.dot_general(
                keys, query_ref[t // 2, 4 + t % 2], (((1,), (1,)), ((), ())), preferred_element_type=jnp.float32
            )
            top = jnp.max(scores, axis=0, keepdims=True) * scale
            weights = []
            total = jnp.zeros((1, TILE), jnp.float32)
            for g in range(GROUP):
                shift = top + jnp.where(g < valid, 0.0, -LOW)
                w = jnp.exp2(scores[g * TILE : (g + 1) * TILE] * scale - shift)
                total = total + jnp.sum(w, axis=0, keepdims=True)
                weights.append(w.astype(jnp.bfloat16))
            vals = jnp.concatenate([key_ref[i // 2, 2 + i % 2] for i in kid], axis=1)
            part = jnp.dot(vals, jnp.concatenate(weights, axis=0), preferred_element_type=jnp.float32)
            parts.append((t, top, total, part))
        for t, top, total, part in parts:
            old = max_ref[t]
            new = jnp.maximum(old, top)
            a = jnp.exp2(old - new)
            b = jnp.exp2(top - new)
            max_ref[t] = new
            sum_ref[t] = sum_ref[t] * a + total * b
            acc_ref[t] = acc_ref[t] * a + part * b
        return 0

    lax.fori_loop(0, meta[0], body, 0)


def first_kernel(scale, meta, q_of, k_of, valid_of, own_ref, acc_ref, max_ref, sum_ref):
    acc_ref[...] = jnp.zeros_like(acc_ref)
    sum_ref[...] = jnp.zeros_like(sum_ref)
    max_ref[...] = jnp.full_like(max_ref, LOW)
    attend_items(scale, meta, q_of, k_of, valid_of, own_ref, own_ref, acc_ref, max_ref, sum_ref)


def second_kernel(scale, meta, q_of, k_of, valid_of, own_ref, other_ref, acc_in, max_in, sum_in, out_ref, acc_s, max_s, sum_s):
    acc_s[...] = acc_in[...]
    max_s[...] = max_in[...]
    sum_s[...] = sum_in[...]
    attend_items(scale, meta, q_of, k_of, valid_of, own_ref, other_ref, acc_s, max_s, sum_s)

    def finish(t, _):
        inverse = 1.0 / jnp.maximum(sum_s[t], 1e-30)
        out_ref[t // 2, t % 2] = (acc_s[t] * inverse).astype(jnp.bfloat16)
        return 0

    lax.fori_loop(0, 2 * CHIPS, finish, 0)


def attend(lists, own, other=None, state=None):
    tiles = 2 * CHIPS
    smem = pl.BlockSpec(memory_space=pltpu.SMEM)
    vmem = pl.BlockSpec(memory_space=pltpu.VMEM)
    shapes = [((tiles, TILE, TILE), jnp.float32), ((tiles, 1, TILE), jnp.float32), ((tiles, 1, TILE), jnp.float32)]
    options = dict(
        compiler_params=pltpu.CompilerParams(vmem_limit_bytes=24 * 2**20),
        cost_estimate=pl.CostEstimate(flops=4 * 10**9, bytes_accessed=8 * 2**20, transcendentals=4 * 10**6),
    )
    scale = TILE**-0.5 * LOG2E
    if other is None:
        return pl.pallas_call(
            functools.partial(first_kernel, scale),
            in_specs=[smem] * 4 + [vmem],
            out_specs=[vmem] * 3,
            out_shape=[jax.ShapeDtypeStruct(*shape) for shape in shapes],
            **options,
        )(*lists, own)
    return pl.pallas_call(
        functools.partial(second_kernel, scale),
        in_specs=[smem] * 4 + [vmem] * 5,
        out_specs=vmem,
        out_shape=jax.ShapeDtypeStruct((CHIPS, 2, TILE, TILE), jnp.bfloat16),
        scratch_shapes=[pltpu.VMEM(*shape) for shape in shapes],
        **options,
    )(*lists, own, other, *state)


def item_lists(allowed, mine):
    tiles = allowed.shape[1]
    count = jnp.sum(allowed, axis=1) * mine
    groups = (count + GROUP - 1) // GROUP
    slots = jnp.arange(groups.shape[0])
    end = jnp.sum(jnp.where(slots[None, :] <= slots[:, None], groups[None, :], 0), axis=1)
    steps = (end[-1] + UNROLL - 1) // UNROLL
    key_ids = jnp.arange(tiles)
    before = jnp.sum(allowed[:, None, :] * (key_ids[None, :] < key_ids[:, None])[None].astype(jnp.int32), axis=2)
    listed = jnp.sum(
        jnp.where((before[:, :, None] == key_ids[None, None, :]) & (allowed[:, :, None] > 0), key_ids[None, :, None], 0),
        axis=1,
    )
    item = jnp.arange(ITEMS)
    real = (item < end[-1]).astype(jnp.int32)
    held = jnp.maximum(jnp.minimum(item, end[-1] - 1), 0)
    q_of = jnp.minimum(jnp.sum((end[None, :] <= held[:, None]).astype(jnp.int32), axis=1), 2 * CHIPS - 1)
    pick = (q_of[:, None] == slots[None, :]).astype(jnp.int32)
    start = GROUP * (held - jnp.sum(pick * (end - groups)[None, :], axis=1))
    left = jnp.sum(pick * count[None, :], axis=1) - start
    rows = jnp.dot(pick.astype(jnp.float32), listed.astype(jnp.float32))
    offset = jnp.arange(GROUP)
    where = start[:, None] + jnp.where(offset[None, :] < left[:, None], offset[None, :], 0)
    k_of = jnp.sum(jnp.where(where[:, :, None] == key_ids[None, None, :], rows[:, None, :], 0.0), axis=2)
    valid = jnp.minimum(left, GROUP) * real
    return steps[None], q_of, k_of.astype(jnp.int32).reshape(-1), valid


def select_kernel(source, got_ref, out_ref, low_ref, high_ref):
    for i in range(PLANE_HEADS):
        part_ref, at = (low_ref, i) if i < PART_HEADS else (high_ref, i - PART_HEADS)
        for sub in range(2):
            rows = pl.ds(sub * TILE, TILE)
            tile = got_ref[source[2 * i + sub], sub].T
            out_ref[rows, pl.ds(i * TILE, TILE)] = tile
            part_ref[rows, pl.ds(at * TILE, TILE)] = tile


def select(source, got):
    vmem = pl.BlockSpec(memory_space=pltpu.VMEM)
    return pl.pallas_call(
        select_kernel,
        in_specs=[pl.BlockSpec(memory_space=pltpu.SMEM), vmem],
        out_specs=[vmem] * 3,
        out_shape=[
            jax.ShapeDtypeStruct((HALF, heads * TILE), jnp.bfloat16) for heads in (PLANE_HEADS, PART_HEADS, PART_HEADS)
        ],
    )(source, got)


def gather_kernel(counts, heads, w_ref, *rest):
    out_refs, (held, sem_in, sem_out) = rest[: len(counts)], rest[len(counts) :]
    loads, stores = [], []
    for n in range(HEADS):
        rows = pl.ds(pl.multiple_of(heads[n] * TILE, TILE), TILE)
        loads.append(pltpu.make_async_copy(w_ref.at[rows], held.at[n], sem_in.at[n]))
        loads[n].start()
    n = 0
    for out_ref, count in zip(out_refs, counts):
        for at in range(count):
            loads[n].wait()
            stores.append(pltpu.make_async_copy(held.at[n], out_ref.at[pl.ds(at * TILE, TILE)], sem_out.at[n]))
            stores[n].start()
            n += 1
    for store in stores:
        store.wait()


def gather(w_out, heads, counts):
    cols = w_out.shape[1]
    hbm = pl.BlockSpec(memory_space=pl.ANY)
    return pl.pallas_call(
        functools.partial(gather_kernel, counts),
        in_specs=[pl.BlockSpec(memory_space=pltpu.SMEM), hbm],
        out_specs=[hbm] * len(counts),
        out_shape=[jax.ShapeDtypeStruct((count * TILE, cols), w_out.dtype) for count in counts],
        scratch_shapes=[
            pltpu.VMEM((HEADS, TILE, cols), w_out.dtype),
            pltpu.SemaphoreType.DMA((HEADS,)),
            pltpu.SemaphoreType.DMA((HEADS,)),
        ],
        compiler_params=pltpu.CompilerParams(vmem_limit_bytes=56 * 2**20),
    )(heads, w_out)


def exchange(block):
    return lax.all_to_all(block, TOKENS_AXES, split_axis=0, concat_axis=0, tiled=True)


def along_y(block, step):
    return lax.ppermute(block, "y", [(i, (i + step) % PLANES) for i in range(PLANES)])


def swap(block):
    return lax.ppermute(block, "c", [(0, 1), (1, 0)])


def shards(residual_in, queries, keys, values, w_out, gate_scale, tile_mask):
    chip = lax.axis_index("x") * 4 + lax.axis_index("z")
    plane = lax.axis_index("y")
    core = lax.axis_index("c")
    tile_work = jnp.sum(tile_mask, axis=1)
    head_at, work_at = head_plan(jnp.sum(tile_work, axis=1))
    plane_heads = lax.dynamic_slice_in_dim(head_at, plane * PLANE_HEADS, PLANE_HEADS)
    chips, first = chip_plan(lax.dynamic_slice_in_dim(work_at, plane * PLANE_HEADS, PLANE_HEADS))
    chip_ids = jnp.arange(CHIPS)
    on_chip = (first[None, :] <= chip_ids[:, None]) & (chip_ids[:, None] < (first + chips)[None, :])
    chip_heads = jnp.sum(jnp.where(on_chip, plane_heads[None, :], 0), axis=1)
    got = exchange(pack(queries, keys, values, chip_heads, core)).reshape(CHIPS, 6, TILE, TILE)

    half_work = lax.dynamic_index_in_dim(tile_work.reshape(HEADS, CHIPS, 2, 2), core, 2, keepdims=False)
    half_work = jnp.take(half_work.reshape(HEADS, 2 * CHIPS), plane_heads, axis=0, mode="clip")
    tile_ids = jnp.arange(2 * CHIPS)
    done = jnp.sum(
        jnp.where((tile_ids[None, :] < tile_ids[:, None])[None], half_work[:, None, :], 0), axis=2
    )
    total = jnp.sum(half_work, axis=1, keepdims=True)
    owner = first[:, None] + ((2 * done + half_work) * chips[:, None]) // (2 * total)
    my_slot = jnp.sum(jnp.where(on_chip[chip], jnp.arange(PLANE_HEADS), 0))
    my_head = chip_heads[chip]
    mine_tiles = (owner[my_slot] == chip).astype(jnp.int32)
    allowed = lax.dynamic_index_in_dim(tile_mask, my_head, 0, keepdims=False)
    allowed = lax.dynamic_index_in_dim(allowed.reshape(CHIPS, 2, 2, 4 * CHIPS), core, 1, keepdims=False)
    source = lax.dynamic_slice_in_dim(owner, 2 * chip, 2, 1).reshape(-1)

    w_order = jnp.concatenate(
        [lax.dynamic_slice_in_dim(head_at, (plane + k) % PLANES * PLANE_HEADS, PLANE_HEADS) for k in (0, 3, 1, 2)]
    )
    weights = gather(w_out, w_order, (PLANE_HEADS,) + (PART_HEADS,) * 6)
    allowed = allowed.reshape(2 * CHIPS, CHIPS, 2, 2)
    lists = [
        item_lists(lax.dynamic_index_in_dim(allowed, c, 2, keepdims=False).reshape(2 * CHIPS, 2 * CHIPS), mine_tiles)
        for c in (core, 1 - core)
    ]
    got, lists, source, weights = lax.optimization_barrier((got, lists, source, weights))
    got_other = swap(got)

    def product(block, other, weight):
        return jnp.dot(jnp.concatenate([block, other], axis=0), weight, preferred_element_type=jnp.float32)

    def project(block, weight):
        return product(block, swap(block), weight)

    def by_rows(total):
        mine, theirs = total[:HALF], total[HALF:]
        return jnp.concatenate([jnp.where(core == 0, mine, theirs), jnp.where(core == 0, theirs, mine)], axis=0)

    attended = attend(lists[1], got, got_other, attend(lists[0], got))
    own, low, high = select(source, exchange(attended))
    below_low, above_high = along_y(low, 1), along_y(high, 3)
    below_high = along_y(high, 1)
    own_other = swap(own)
    above_low = along_y(low, 3)
    far_low, far_high = along_y(below_low, 1), along_y(above_high, 3)
    total = product(own, own_other, weights[0])
    near = ((below_high, weights[2]), (above_low, weights[3]), (below_low, weights[1]), (above_high, weights[4]))
    for block, weight in near:
        total = total + project(block, weight)
    base = residual_in.astype(jnp.float32) + gate_scale * by_rows(total)
    base, far_low, far_high = lax.optimization_barrier((base, far_low, far_high))
    far = project(far_low, weights[5]) + project(far_high, weights[6])
    return (base + gate_scale * by_rows(far)).astype(jnp.bfloat16)


def solution(mesh):
    fine = Mesh(mesh.devices.reshape(4, 4, 4, 2), ("x", "z", "y", "c"))
    seq, rep = TOKENS_AXES, ("y", "c")
    in_specs = (
        P(seq, rep),
        P(seq, None),
        P(seq, None),
        P(seq, None),
        P(None, rep),
        P(rep),
        P(),
    )
    return jax.shard_map(shards, mesh=fine, in_specs=in_specs, out_specs=P(seq, rep), check_vma=False)
```

```python
import functools

import jax
import jax.numpy as jnp
from jax import lax
from jax.experimental import pallas as pl
from jax.experimental.pallas import tpu as pltpu
from jax.sharding import Mesh
from jax.sharding import PartitionSpec as P

TILE = 128
HEADS = 40
PLANES = 4
PLANE_HEADS = HEADS // PLANES
PART_HEADS = PLANE_HEADS // 2
CHIPS = 16
HALF = 256
GROUP = 4
UNROLL = 16
ITEMS = 256
LOG2E = 1.4426950408889634
TOKENS_AXES = ("x", "z")
LOW = -1e30


def head_plan(work):
    ids = jnp.arange(HEADS)
    ahead = (work[None, :] > work[:, None]) | ((work[None, :] == work[:, None]) & (ids[None, :] < ids[:, None]))
    rank = jnp.sum(ahead.astype(jnp.int32), axis=1)
    row, col = rank // PLANES, rank % PLANES
    plane = jnp.where(row % 2 == 1, PLANES - 1 - col, col)
    place = plane * PLANE_HEADS + row
    hit = (place[None, :] == ids[:, None]).astype(jnp.int32)
    head_at = jnp.sum(hit * ids[None, :], axis=1)
    work_at = jnp.sum(hit * work[None, :], axis=1)
    return head_at, work_at


def chip_plan(work_at):
    extra = CHIPS - PLANE_HEADS
    quota = (work_at[:, None].astype(jnp.float32) / jnp.arange(1, extra + 1).astype(jnp.float32)[None, :]).reshape(-1)
    ids = jnp.arange(quota.shape[0])
    ahead = (quota[None, :] > quota[:, None]) | ((quota[None, :] == quota[:, None]) & (ids[None, :] < ids[:, None]))
    won = (jnp.sum(ahead.astype(jnp.int32), axis=1) < extra).astype(jnp.int32)
    chips = 1 + jnp.sum(won.reshape(PLANE_HEADS, extra), axis=1)
    slots = jnp.arange(PLANE_HEADS)
    first = jnp.sum(jnp.where(slots[None, :] < slots[:, None], chips[None, :], 0), axis=1)
    return chips, first


def pack_kernel(heads, q_ref, k_ref, v_ref, out_ref, held, values, sem_v, sem_kq, sem_out):
    rows = pl.ds(pl.multiple_of(heads[CHIPS] * HALF, HALF), HALF)
    cols = [pl.ds(pl.multiple_of(heads[t] * TILE, TILE), TILE) for t in range(CHIPS)]
    first = [pltpu.make_async_copy(v_ref.at[rows, cols[t]], values.at[t], sem_v.at[t]) for t in range(CHIPS)]
    others = [
        pltpu.make_async_copy(ref.at[rows, cols[t]], held.at[t, pl.ds(at * HALF, HALF)], sem_kq.at[t, at // 2])
        for t in range(CHIPS)
        for ref, at in ((k_ref, 0), (q_ref, 2))
    ]
    for load in first + others:
        load.start()
    stores = []
    for t in range(CHIPS):
        first[t].wait()
        for sub in range(2):
            held[t, pl.ds(HALF + sub * TILE, TILE), :] = values[t, pl.ds(sub * TILE, TILE), :].T
        for load in others[2 * t : 2 * t + 2]:
            load.wait()
        stores.append(pltpu.make_async_copy(held.at[t], out_ref.at[t], sem_out.at[t]))
        stores[t].start()
    for store in stores:
        store.wait()


def pack(queries, keys, values, chip_heads, core):
    scalars = jnp.concatenate([chip_heads, core[None]]).astype(jnp.int32)
    hbm = pl.BlockSpec(memory_space=pl.ANY)
    return pl.pallas_call(
        pack_kernel,
        in_specs=[pl.BlockSpec(memory_space=pltpu.SMEM)] + [hbm] * 3,
        out_specs=hbm,
        out_shape=jax.ShapeDtypeStruct((CHIPS, 6 * TILE, TILE), jnp.bfloat16),
        scratch_shapes=[
            pltpu.VMEM((CHIPS, 3 * HALF, TILE), jnp.bfloat16),
            pltpu.VMEM((CHIPS, HALF, TILE), jnp.bfloat16),
            pltpu.SemaphoreType.DMA((CHIPS,)),
            pltpu.SemaphoreType.DMA((CHIPS, 2)),
            pltpu.SemaphoreType.DMA((CHIPS,)),
        ],
        compiler_params=pltpu.CompilerParams(vmem_limit_bytes=60 * 2**20),
    )(scalars, queries, keys, values)


def attend_items(scale, meta, q_of, k_of, valid_of, query_ref, key_ref, acc_ref, max_ref, sum_ref):
    def body(step, _):
        parts = []
        for u in range(UNROLL):
            e = step * UNROLL + u
            t = q_of[e]
            kid = [k_of[e * GROUP + g] for g in range(GROUP)]
            valid = valid_of[e]
            keys = jnp.concatenate([key_ref[i // 2, i % 2] for i in kid], axis=0)
            scores = lax.dot_general(
                keys, query_ref[t // 2, 4 + t % 2], (((1,), (1,)), ((), ())), preferred_element_type=jnp.float32
            )
            top = jnp.max(scores, axis=0, keepdims=True) * scale
            weights = []
            total = jnp.zeros((1, TILE), jnp.float32)
            for g in range(GROUP):
                shift = top + jnp.where(g < valid, 0.0, -LOW)
                w = jnp.exp2(scores[g * TILE : (g + 1) * TILE] * scale - shift)
                total = total + jnp.sum(w, axis=0, keepdims=True)
                weights.append(w.astype(jnp.bfloat16))
            vals = jnp.concatenate([key_ref[i // 2, 2 + i % 2] for i in kid], axis=1)
            part = jnp.dot(vals, jnp.concatenate(weights, axis=0), preferred_element_type=jnp.float32)
            parts.append((t, top, total, part))
        for t, top, total, part in parts:
            old = max_ref[t]
            new = jnp.maximum(old, top)
            a = jnp.exp2(old - new)
            b = jnp.exp2(top - new)
            max_ref[t] = new
            sum_ref[t] = sum_ref[t] * a + total * b
            acc_ref[t] = acc_ref[t] * a + part * b
        return 0

    lax.fori_loop(0, meta[0], body, 0)


def first_kernel(scale, meta, q_of, k_of, valid_of, own_ref, acc_ref, max_ref, sum_ref):
    acc_ref[...] = jnp.zeros_like(acc_ref)
    sum_ref[...] = jnp.zeros_like(sum_ref)
    max_ref[...] = jnp.full_like(max_ref, LOW)
    attend_items(scale, meta, q_of, k_of, valid_of, own_ref, own_ref, acc_ref, max_ref, sum_ref)


def second_kernel(scale, meta, q_of, k_of, valid_of, own_ref, other_ref, acc_in, max_in, sum_in, out_ref, acc_s, max_s, sum_s):
    acc_s[...] = acc_in[...]
    max_s[...] = max_in[...]
    sum_s[...] = sum_in[...]
    attend_items(scale, meta, q_of, k_of, valid_of, own_ref, other_ref, acc_s, max_s, sum_s)

    def finish(t, _):
        inverse = 1.0 / jnp.maximum(sum_s[t], 1e-30)
        out_ref[t // 2, t % 2] = (acc_s[t] * inverse).astype(jnp.bfloat16)
        return 0

    lax.fori_loop(0, 2 * CHIPS, finish, 0)


def attend(lists, own, other=None, state=None):
    tiles = 2 * CHIPS
    smem = pl.BlockSpec(memory_space=pltpu.SMEM)
    vmem = pl.BlockSpec(memory_space=pltpu.VMEM)
    shapes = [((tiles, TILE, TILE), jnp.float32), ((tiles, 1, TILE), jnp.float32), ((tiles, 1, TILE), jnp.float32)]
    options = dict(
        compiler_params=pltpu.CompilerParams(vmem_limit_bytes=24 * 2**20),
        cost_estimate=pl.CostEstimate(flops=4 * 10**9, bytes_accessed=8 * 2**20, transcendentals=4 * 10**6),
    )
    scale = TILE**-0.5 * LOG2E
    if other is None:
        return pl.pallas_call(
            functools.partial(first_kernel, scale),
            in_specs=[smem] * 4 + [vmem],
            out_specs=[vmem] * 3,
            out_shape=[jax.ShapeDtypeStruct(*shape) for shape in shapes],
            **options,
        )(*lists, own)
    return pl.pallas_call(
        functools.partial(second_kernel, scale),
        in_specs=[smem] * 4 + [vmem] * 5,
        out_specs=vmem,
        out_shape=jax.ShapeDtypeStruct((CHIPS, 2, TILE, TILE), jnp.bfloat16),
        scratch_shapes=[pltpu.VMEM(*shape) for shape in shapes],
        **options,
    )(*lists, own, other, *state)


def item_lists(allowed, mine):
    tiles = allowed.shape[1]
    count = jnp.sum(allowed, axis=1) * mine
    groups = (count + GROUP - 1) // GROUP
    slots = jnp.arange(groups.shape[0])
    end = jnp.sum(jnp.where(slots[None, :] <= slots[:, None], groups[None, :], 0), axis=1)
    steps = (end[-1] + UNROLL - 1) // UNROLL
    key_ids = jnp.arange(tiles)
    before = jnp.sum(allowed[:, None, :] * (key_ids[None, :] < key_ids[:, None])[None].astype(jnp.int32), axis=2)
    listed = jnp.sum(
        jnp.where((before[:, :, None] == key_ids[None, None, :]) & (allowed[:, :, None] > 0), key_ids[None, :, None], 0),
        axis=1,
    )
    item = jnp.arange(ITEMS)
    real = (item < end[-1]).astype(jnp.int32)
    held = jnp.maximum(jnp.minimum(item, end[-1] - 1), 0)
    q_of = jnp.minimum(jnp.sum((end[None, :] <= held[:, None]).astype(jnp.int32), axis=1), 2 * CHIPS - 1)
    pick = (q_of[:, None] == slots[None, :]).astype(jnp.int32)
    start = GROUP * (held - jnp.sum(pick * (end - groups)[None, :], axis=1))
    left = jnp.sum(pick * count[None, :], axis=1) - start
    rows = jnp.dot(pick.astype(jnp.float32), listed.astype(jnp.float32))
    offset = jnp.arange(GROUP)
    where = start[:, None] + jnp.where(offset[None, :] < left[:, None], offset[None, :], 0)
    k_of = jnp.sum(jnp.where(where[:, :, None] == key_ids[None, None, :], rows[:, None, :], 0.0), axis=2)
    valid = jnp.minimum(left, GROUP) * real
    return steps[None], q_of, k_of.astype(jnp.int32).reshape(-1), valid


def select_kernel(source, got_ref, out_ref, low_ref, high_ref):
    for i in range(PLANE_HEADS):
        part_ref, at = (low_ref, i) if i < PART_HEADS else (high_ref, i - PART_HEADS)
        for sub in range(2):
            rows = pl.ds(sub * TILE, TILE)
            tile = got_ref[source[2 * i + sub], sub].T
            out_ref[rows, pl.ds(i * TILE, TILE)] = tile
            part_ref[rows, pl.ds(at * TILE, TILE)] = tile


def select(source, got):
    vmem = pl.BlockSpec(memory_space=pltpu.VMEM)
    return pl.pallas_call(
        select_kernel,
        in_specs=[pl.BlockSpec(memory_space=pltpu.SMEM), vmem],
        out_specs=[vmem] * 3,
        out_shape=[
            jax.ShapeDtypeStruct((HALF, heads * TILE), jnp.bfloat16) for heads in (PLANE_HEADS, PART_HEADS, PART_HEADS)
        ],
    )(source, got)


def gather_kernel(counts, heads, w_ref, *rest):
    out_refs, (held, sem_in, sem_out) = rest[: len(counts)], rest[len(counts) :]
    loads, stores = [], []
    for n in range(HEADS):
        rows = pl.ds(pl.multiple_of(heads[n] * TILE, TILE), TILE)
        loads.append(pltpu.make_async_copy(w_ref.at[rows], held.at[n], sem_in.at[n]))
        loads[n].start()
    n = 0
    for out_ref, count in zip(out_refs, counts):
        for at in range(count):
            loads[n].wait()
            stores.append(pltpu.make_async_copy(held.at[n], out_ref.at[pl.ds(at * TILE, TILE)], sem_out.at[n]))
            stores[n].start()
            n += 1
    for store in stores:
        store.wait()


def gather(w_out, heads, counts):
    cols = w_out.shape[1]
    hbm = pl.BlockSpec(memory_space=pl.ANY)
    return pl.pallas_call(
        functools.partial(gather_kernel, counts),
        in_specs=[pl.BlockSpec(memory_space=pltpu.SMEM), hbm],
        out_specs=[hbm] * len(counts),
        out_shape=[jax.ShapeDtypeStruct((count * TILE, cols), w_out.dtype) for count in counts],
        scratch_shapes=[
            pltpu.VMEM((HEADS, TILE, cols), w_out.dtype),
            pltpu.SemaphoreType.DMA((HEADS,)),
            pltpu.SemaphoreType.DMA((HEADS,)),
        ],
        compiler_params=pltpu.CompilerParams(vmem_limit_bytes=56 * 2**20),
    )(heads, w_out)


def exchange(block):
    return lax.all_to_all(block, TOKENS_AXES, split_axis=0, concat_axis=0, tiled=True)


def along_y(block, step):
    return lax.ppermute(block, "y", [(i, (i + step) % PLANES) for i in range(PLANES)])


def swap(block):
    return lax.ppermute(block, "c", [(0, 1), (1, 0)])


def shards(residual_in, queries, keys, values, w_out, gate_scale, tile_mask):
    chip = lax.axis_index("x") * 4 + lax.axis_index("z")
    plane = lax.axis_index("y")
    core = lax.axis_index("c")
    tile_work = jnp.sum(tile_mask, axis=1)
    head_at, work_at = head_plan(jnp.sum(tile_work, axis=1))
    plane_heads = lax.dynamic_slice_in_dim(head_at, plane * PLANE_HEADS, PLANE_HEADS)
    chips, first = chip_plan(lax.dynamic_slice_in_dim(work_at, plane * PLANE_HEADS, PLANE_HEADS))
    chip_ids = jnp.arange(CHIPS)
    on_chip = (first[None, :] <= chip_ids[:, None]) & (chip_ids[:, None] < (first + chips)[None, :])
    chip_heads = jnp.sum(jnp.where(on_chip, plane_heads[None, :], 0), axis=1)
    got = exchange(pack(queries, keys, values, chip_heads, core)).reshape(CHIPS, 6, TILE, TILE)

    half_work = lax.dynamic_index_in_dim(tile_work.reshape(HEADS, CHIPS, 2, 2), core, 2, keepdims=False)
    half_work = jnp.take(half_work.reshape(HEADS, 2 * CHIPS), plane_heads, axis=0, mode="clip")
    tile_ids = jnp.arange(2 * CHIPS)
    done = jnp.sum(
        jnp.where((tile_ids[None, :] < tile_ids[:, None])[None], half_work[:, None, :], 0), axis=2
    )
    total = jnp.sum(half_work, axis=1, keepdims=True)
    owner = first[:, None] + ((2 * done + half_work) * chips[:, None]) // (2 * total)
    my_slot = jnp.sum(jnp.where(on_chip[chip], jnp.arange(PLANE_HEADS), 0))
    my_head = chip_heads[chip]
    mine_tiles = (owner[my_slot] == chip).astype(jnp.int32)
    allowed = lax.dynamic_index_in_dim(tile_mask, my_head, 0, keepdims=False)
    allowed = lax.dynamic_index_in_dim(allowed.reshape(CHIPS, 2, 2, 4 * CHIPS), core, 1, keepdims=False)
    source = lax.dynamic_slice_in_dim(owner, 2 * chip, 2, 1).reshape(-1)

    w_order = jnp.concatenate(
        [lax.dynamic_slice_in_dim(head_at, (plane + k) % PLANES * PLANE_HEADS, PLANE_HEADS) for k in (0, 3, 1, 2)]
    )
    weights = gather(w_out, w_order, (PLANE_HEADS,) + (PART_HEADS,) * 6)
    allowed = allowed.reshape(2 * CHIPS, CHIPS, 2, 2)
    lists = [
        item_lists(lax.dynamic_index_in_dim(allowed, c, 2, keepdims=False).reshape(2 * CHIPS, 2 * CHIPS), mine_tiles)
        for c in (core, 1 - core)
    ]
    got, lists, source, weights = lax.optimization_barrier((got, lists, source, weights))
    got_other = swap(got)

    def product(block, other, weight):
        return jnp.dot(jnp.concatenate([block, other], axis=0), weight, preferred_element_type=jnp.float32)

    def project(block, weight):
        return product(block, swap(block), weight)

    def by_rows(total):
        mine, theirs = total[:HALF], total[HALF:]
        return jnp.concatenate([jnp.where(core == 0, mine, theirs), jnp.where(core == 0, theirs, mine)], axis=0)

    attended = attend(lists[1], got, got_other, attend(lists[0], got))
    own, low, high = select(source, exchange(attended))
    below_low, above_high = along_y(low, 1), along_y(high, 3)
    own_other, low, high = lax.optimization_barrier((swap(own), low, high))
    below_high, above_low = along_y(high, 1), along_y(low, 3)
    far_low, far_high = along_y(below_low, 1), along_y(above_high, 3)
    total = product(own, own_other, weights[0])
    for block, weight in zip((below_low, above_high, below_high, above_low), (weights[1], weights[4], weights[2], weights[3])):
        total = total + project(block, weight)
    base = residual_in.astype(jnp.float32) + gate_scale * by_rows(total)
    base, far_low, far_high = lax.optimization_barrier((base, far_low, far_high))

    def far_product(low, high):
        low = jnp.dot(low, weights[5], preferred_element_type=jnp.float32)
        return low + jnp.dot(high, weights[6], preferred_element_type=jnp.float32)

    mine, other_low, other_high = lax.optimization_barrier(
        (far_product(far_low, far_high), swap(far_low), swap(far_high))
    )
    theirs = far_product(other_low, other_high)
    return (base + gate_scale * by_rows(jnp.concatenate([mine, theirs], axis=0))).astype(jnp.bfloat16)


def solution(mesh):
    fine = Mesh(mesh.devices.reshape(4, 4, 4, 2), ("x", "z", "y", "c"))
    seq, rep = TOKENS_AXES, ("y", "c")
    in_specs = (
        P(seq, rep),
        P(seq, None),
        P(seq, None),
        P(seq, None),
        P(None, rep),
        P(rep),
        P(),
    )
    return jax.shard_map(shards, mesh=fine, in_specs=in_specs, out_specs=P(seq, rep), check_vma=False)
```

```python
import functools

import jax
import jax.numpy as jnp
from jax import lax
from jax.experimental import pallas as pl
from jax.experimental.pallas import tpu as pltpu
from jax.sharding import Mesh
from jax.sharding import PartitionSpec as P

TILE = 128
HEADS = 40
PLANES = 4
PLANE_HEADS = HEADS // PLANES
PART_HEADS = PLANE_HEADS // 2
CHIPS = 16
HALF = 256
GROUP = 4
UNROLL = 16
ITEMS = 256
LOG2E = 1.4426950408889634
TOKENS_AXES = ("x", "z")
LOW = -1e30


def head_plan(work):
    ids = jnp.arange(HEADS)
    ahead = (work[None, :] > work[:, None]) | ((work[None, :] == work[:, None]) & (ids[None, :] < ids[:, None]))
    rank = jnp.sum(ahead.astype(jnp.int32), axis=1)
    row, col = rank // PLANES, rank % PLANES
    plane = jnp.where(row % 2 == 1, PLANES - 1 - col, col)
    place = plane * PLANE_HEADS + row
    hit = (place[None, :] == ids[:, None]).astype(jnp.int32)
    head_at = jnp.sum(hit * ids[None, :], axis=1)
    work_at = jnp.sum(hit * work[None, :], axis=1)
    return head_at, work_at


def chip_plan(work_at):
    extra = CHIPS - PLANE_HEADS
    quota = (work_at[:, None].astype(jnp.float32) / jnp.arange(1, extra + 1).astype(jnp.float32)[None, :]).reshape(-1)
    ids = jnp.arange(quota.shape[0])
    ahead = (quota[None, :] > quota[:, None]) | ((quota[None, :] == quota[:, None]) & (ids[None, :] < ids[:, None]))
    won = (jnp.sum(ahead.astype(jnp.int32), axis=1) < extra).astype(jnp.int32)
    chips = 1 + jnp.sum(won.reshape(PLANE_HEADS, extra), axis=1)
    slots = jnp.arange(PLANE_HEADS)
    first = jnp.sum(jnp.where(slots[None, :] < slots[:, None], chips[None, :], 0), axis=1)
    return chips, first


def pack_kernel(heads, core, q_ref, k_ref, v_ref, out_ref, held, values, sem_v, sem_kq, sem_out):
    rows = pl.ds(pl.multiple_of(core[0] * HALF, HALF), HALF)
    cols = [pl.ds(pl.multiple_of(heads[t] * TILE, TILE), TILE) for t in range(CHIPS)]
    first = [pltpu.make_async_copy(v_ref.at[rows, cols[t]], values.at[t], sem_v.at[t]) for t in range(CHIPS)]
    others = [
        pltpu.make_async_copy(ref.at[rows, cols[t]], held.at[t, pl.ds(at * HALF, HALF)], sem_kq.at[t, at // 2])
        for t in range(CHIPS)
        for ref, at in ((k_ref, 0), (q_ref, 2))
    ]
    for load in first + others:
        load.start()
    stores = []
    for t in range(CHIPS):
        first[t].wait()
        for sub in range(2):
            held[t, pl.ds(HALF + sub * TILE, TILE), :] = values[t, pl.ds(sub * TILE, TILE), :].T
        for load in others[2 * t : 2 * t + 2]:
            load.wait()
        stores.append(pltpu.make_async_copy(held.at[t], out_ref.at[t], sem_out.at[t]))
        stores[t].start()
    for store in stores:
        store.wait()


def pack(queries, keys, values, chip_heads, core):
    smem = pl.BlockSpec(memory_space=pltpu.SMEM)
    hbm = pl.BlockSpec(memory_space=pl.ANY)
    return pl.pallas_call(
        pack_kernel,
        in_specs=[smem] * 2 + [hbm] * 3,
        out_specs=hbm,
        out_shape=jax.ShapeDtypeStruct((CHIPS, 6 * TILE, TILE), jnp.bfloat16),
        scratch_shapes=[
            pltpu.VMEM((CHIPS, 3 * HALF, TILE), jnp.bfloat16),
            pltpu.VMEM((CHIPS, HALF, TILE), jnp.bfloat16),
            pltpu.SemaphoreType.DMA((CHIPS,)),
            pltpu.SemaphoreType.DMA((CHIPS, 2)),
            pltpu.SemaphoreType.DMA((CHIPS,)),
        ],
        compiler_params=pltpu.CompilerParams(vmem_limit_bytes=60 * 2**20),
    )(chip_heads.astype(jnp.int32), core.reshape(1).astype(jnp.int32), queries, keys, values)


def attend_items(scale, meta, q_of, k_of, valid_of, query_ref, key_ref, acc_ref, max_ref, sum_ref):
    def body(step, _):
        parts = []
        for u in range(UNROLL):
            e = step * UNROLL + u
            t = q_of[e]
            kid = [k_of[e * GROUP + g] for g in range(GROUP)]
            valid = valid_of[e]
            keys = jnp.concatenate([key_ref[i // 2, i % 2] for i in kid], axis=0)
            scores = lax.dot_general(
                keys, query_ref[t // 2, 4 + t % 2], (((1,), (1,)), ((), ())), preferred_element_type=jnp.float32
            )
            top = jnp.max(scores, axis=0, keepdims=True) * scale
            weights = []
            total = jnp.zeros((1, TILE), jnp.float32)
            for g in range(GROUP):
                shift = top + jnp.where(g < valid, 0.0, -LOW)
                w = jnp.exp2(scores[g * TILE : (g + 1) * TILE] * scale - shift)
                total = total + jnp.sum(w, axis=0, keepdims=True)
                weights.append(w.astype(jnp.bfloat16))
            vals = jnp.concatenate([key_ref[i // 2, 2 + i % 2] for i in kid], axis=1)
            part = jnp.dot(vals, jnp.concatenate(weights, axis=0), preferred_element_type=jnp.float32)
            parts.append((t, top, total, part))
        for t, top, total, part in parts:
            old = max_ref[t]
            new = jnp.maximum(old, top)
            a = jnp.exp2(old - new)
            b = jnp.exp2(top - new)
            max_ref[t] = new
            sum_ref[t] = sum_ref[t] * a + total * b
            acc_ref[t] = acc_ref[t] * a + part * b
        return 0

    lax.fori_loop(0, meta[0], body, 0)


def first_kernel(scale, meta, q_of, k_of, valid_of, own_ref, acc_ref, max_ref, sum_ref):
    acc_ref[...] = jnp.zeros_like(acc_ref)
    sum_ref[...] = jnp.zeros_like(sum_ref)
    max_ref[...] = jnp.full_like(max_ref, LOW)
    attend_items(scale, meta, q_of, k_of, valid_of, own_ref, own_ref, acc_ref, max_ref, sum_ref)


def second_kernel(scale, meta, q_of, k_of, valid_of, own_ref, other_ref, acc_in, max_in, sum_in, out_ref, acc_s, max_s, sum_s):
    acc_s[...] = acc_in[...]
    max_s[...] = max_in[...]
    sum_s[...] = sum_in[...]
    attend_items(scale, meta, q_of, k_of, valid_of, own_ref, other_ref, acc_s, max_s, sum_s)

    def finish(t, _):
        inverse = 1.0 / jnp.maximum(sum_s[t], 1e-30)
        out_ref[t // 2, t % 2] = (acc_s[t] * inverse).astype(jnp.bfloat16)
        return 0

    lax.fori_loop(0, 2 * CHIPS, finish, 0)


def attend(lists, own, other=None, state=None):
    tiles = 2 * CHIPS
    smem = pl.BlockSpec(memory_space=pltpu.SMEM)
    vmem = pl.BlockSpec(memory_space=pltpu.VMEM)
    shapes = [((tiles, TILE, TILE), jnp.float32), ((tiles, 1, TILE), jnp.float32), ((tiles, 1, TILE), jnp.float32)]
    options = dict(
        compiler_params=pltpu.CompilerParams(vmem_limit_bytes=24 * 2**20),
        cost_estimate=pl.CostEstimate(flops=4 * 10**9, bytes_accessed=8 * 2**20, transcendentals=4 * 10**6),
    )
    scale = TILE**-0.5 * LOG2E
    if other is None:
        return pl.pallas_call(
            functools.partial(first_kernel, scale),
            in_specs=[smem] * 4 + [vmem],
            out_specs=[vmem] * 3,
            out_shape=[jax.ShapeDtypeStruct(*shape) for shape in shapes],
            **options,
        )(*lists, own)
    return pl.pallas_call(
        functools.partial(second_kernel, scale),
        in_specs=[smem] * 4 + [vmem] * 5,
        out_specs=vmem,
        out_shape=jax.ShapeDtypeStruct((CHIPS, 2, TILE, TILE), jnp.bfloat16),
        scratch_shapes=[pltpu.VMEM(*shape) for shape in shapes],
        **options,
    )(*lists, own, other, *state)


def item_lists(allowed, mine):
    tiles = allowed.shape[1]
    count = jnp.sum(allowed, axis=1) * mine
    groups = (count + GROUP - 1) // GROUP
    slots = jnp.arange(groups.shape[0])
    end = jnp.sum(jnp.where(slots[None, :] <= slots[:, None], groups[None, :], 0), axis=1)
    steps = (end[-1] + UNROLL - 1) // UNROLL
    key_ids = jnp.arange(tiles)
    before = jnp.sum(allowed[:, None, :] * (key_ids[None, :] < key_ids[:, None])[None].astype(jnp.int32), axis=2)
    listed = jnp.sum(
        jnp.where((before[:, :, None] == key_ids[None, None, :]) & (allowed[:, :, None] > 0), key_ids[None, :, None], 0),
        axis=1,
    )
    item = jnp.arange(ITEMS)
    real = (item < end[-1]).astype(jnp.int32)
    held = jnp.maximum(jnp.minimum(item, end[-1] - 1), 0)
    q_of = jnp.minimum(jnp.sum((end[None, :] <= held[:, None]).astype(jnp.int32), axis=1), 2 * CHIPS - 1)
    pick = (q_of[:, None] == slots[None, :]).astype(jnp.int32)
    start = GROUP * (held - jnp.sum(pick * (end - groups)[None, :], axis=1))
    left = jnp.sum(pick * count[None, :], axis=1) - start
    rows = jnp.dot(pick.astype(jnp.float32), listed.astype(jnp.float32))
    offset = jnp.arange(GROUP)
    where = start[:, None] + jnp.where(offset[None, :] < left[:, None], offset[None, :], 0)
    k_of = jnp.sum(jnp.where(where[:, :, None] == key_ids[None, None, :], rows[:, None, :], 0.0), axis=2)
    valid = jnp.minimum(left, GROUP) * real
    return steps[None], q_of, k_of.astype(jnp.int32).reshape(-1), valid


def select_kernel(source, got_ref, out_ref, low_ref, high_ref):
    for i in range(PLANE_HEADS):
        part_ref, at = (low_ref, i) if i < PART_HEADS else (high_ref, i - PART_HEADS)
        for sub in range(2):
            rows = pl.ds(sub * TILE, TILE)
            tile = got_ref[source[2 * i + sub], sub].T
            out_ref[rows, pl.ds(i * TILE, TILE)] = tile
            part_ref[rows, pl.ds(at * TILE, TILE)] = tile


def select(source, got):
    vmem = pl.BlockSpec(memory_space=pltpu.VMEM)
    return pl.pallas_call(
        select_kernel,
        in_specs=[pl.BlockSpec(memory_space=pltpu.SMEM), vmem],
        out_specs=[vmem] * 3,
        out_shape=[
            jax.ShapeDtypeStruct((HALF, heads * TILE), jnp.bfloat16) for heads in (PLANE_HEADS, PART_HEADS, PART_HEADS)
        ],
    )(source, got)


def gather_kernel(counts, heads, w_ref, *rest):
    out_refs, (held, sem_in, sem_out) = rest[: len(counts)], rest[len(counts) :]
    loads, stores = [], []
    for n in range(HEADS):
        rows = pl.ds(pl.multiple_of(heads[n] * TILE, TILE), TILE)
        loads.append(pltpu.make_async_copy(w_ref.at[rows], held.at[n], sem_in.at[n]))
        loads[n].start()
    n = 0
    for out_ref, count in zip(out_refs, counts):
        for at in range(count):
            loads[n].wait()
            stores.append(pltpu.make_async_copy(held.at[n], out_ref.at[pl.ds(at * TILE, TILE)], sem_out.at[n]))
            stores[n].start()
            n += 1
    for store in stores:
        store.wait()


def gather(w_out, heads, counts):
    cols = w_out.shape[1]
    hbm = pl.BlockSpec(memory_space=pl.ANY)
    return pl.pallas_call(
        functools.partial(gather_kernel, counts),
        in_specs=[pl.BlockSpec(memory_space=pltpu.SMEM), hbm],
        out_specs=[hbm] * len(counts),
        out_shape=[jax.ShapeDtypeStruct((count * TILE, cols), w_out.dtype) for count in counts],
        scratch_shapes=[
            pltpu.VMEM((HEADS, TILE, cols), w_out.dtype),
            pltpu.SemaphoreType.DMA((HEADS,)),
            pltpu.SemaphoreType.DMA((HEADS,)),
        ],
        compiler_params=pltpu.CompilerParams(vmem_limit_bytes=56 * 2**20),
    )(heads, w_out)


def exchange(block):
    return lax.all_to_all(block, TOKENS_AXES, split_axis=0, concat_axis=0, tiled=True)


def along_y(block, step):
    return lax.ppermute(block, "y", [(i, (i + step) % PLANES) for i in range(PLANES)])


def swap(block):
    return lax.ppermute(block, "c", [(0, 1), (1, 0)])


def shards(residual_in, queries, keys, values, w_out, gate_scale, tile_mask):
    chip = lax.axis_index("x") * 4 + lax.axis_index("z")
    plane = lax.axis_index("y")
    core = lax.axis_index("c")
    tile_work = jnp.sum(tile_mask, axis=1)
    head_at, work_at = head_plan(jnp.sum(tile_work, axis=1))
    plane_heads = lax.dynamic_slice_in_dim(head_at, plane * PLANE_HEADS, PLANE_HEADS)
    chips, first = chip_plan(lax.dynamic_slice_in_dim(work_at, plane * PLANE_HEADS, PLANE_HEADS))
    chip_ids = jnp.arange(CHIPS)
    on_chip = (first[None, :] <= chip_ids[:, None]) & (chip_ids[:, None] < (first + chips)[None, :])
    chip_heads = jnp.sum(jnp.where(on_chip, plane_heads[None, :], 0), axis=1)
    got = exchange(pack(queries, keys, values, chip_heads, core)).reshape(CHIPS, 6, TILE, TILE)

    half_work = lax.dynamic_index_in_dim(tile_work.reshape(HEADS, CHIPS, 2, 2), core, 2, keepdims=False)
    half_work = jnp.take(half_work.reshape(HEADS, 2 * CHIPS), plane_heads, axis=0, mode="clip")
    tile_ids = jnp.arange(2 * CHIPS)
    done = jnp.sum(
        jnp.where((tile_ids[None, :] < tile_ids[:, None])[None], half_work[:, None, :], 0), axis=2
    )
    total = jnp.sum(half_work, axis=1, keepdims=True)
    owner = first[:, None] + ((2 * done + half_work) * chips[:, None]) // (2 * total)
    my_slot = jnp.sum(jnp.where(on_chip[chip], jnp.arange(PLANE_HEADS), 0))
    my_head = chip_heads[chip]
    mine_tiles = (owner[my_slot] == chip).astype(jnp.int32)
    allowed = lax.dynamic_index_in_dim(tile_mask, my_head, 0, keepdims=False)
    allowed = lax.dynamic_index_in_dim(allowed.reshape(CHIPS, 2, 2, 4 * CHIPS), core, 1, keepdims=False)
    source = lax.dynamic_slice_in_dim(owner, 2 * chip, 2, 1).reshape(-1)

    w_order = jnp.concatenate(
        [lax.dynamic_slice_in_dim(head_at, (plane + k) % PLANES * PLANE_HEADS, PLANE_HEADS) for k in (0, 3, 1, 2)]
    )
    weights = gather(w_out, w_order, (PLANE_HEADS,) + (PART_HEADS,) * 6)
    allowed = allowed.reshape(2 * CHIPS, CHIPS, 2, 2)
    lists = [
        item_lists(lax.dynamic_index_in_dim(allowed, c, 2, keepdims=False).reshape(2 * CHIPS, 2 * CHIPS), mine_tiles)
        for c in (core, 1 - core)
    ]
    got, lists, source, weights = lax.optimization_barrier((got, lists, source, weights))
    got_other = swap(got)

    def product(block, other, weight):
        return jnp.dot(jnp.concatenate([block, other], axis=0), weight, preferred_element_type=jnp.float32)

    def project(block, weight):
        return product(block, swap(block), weight)

    def by_rows(total):
        mine, theirs = total[:HALF], total[HALF:]
        return jnp.concatenate([jnp.where(core == 0, mine, theirs), jnp.where(core == 0, theirs, mine)], axis=0)

    attended = attend(lists[1], got, got_other, attend(lists[0], got))
    own, low, high = select(source, exchange(attended))
    below_low, above_high = along_y(low, 1), along_y(high, 3)
    own_other, low, high = lax.optimization_barrier((swap(own), low, high))
    below_high, above_low = along_y(high, 1), along_y(low, 3)
    far_low, far_high = along_y(below_low, 1), along_y(above_high, 3)
    total = product(own, own_other, weights[0])
    for block, weight in zip((below_low, above_high, below_high, above_low), (weights[1], weights[4], weights[2], weights[3])):
        total = total + project(block, weight)
    base = residual_in.astype(jnp.float32) + gate_scale * by_rows(total)
    base, far_low, far_high = lax.optimization_barrier((base, far_low, far_high))
    far = project(far_low, weights[5]) + project(far_high, weights[6])
    return (base + gate_scale * by_rows(far)).astype(jnp.bfloat16)


def solution(mesh):
    fine = Mesh(mesh.devices.reshape(4, 4, 4, 2), ("x", "z", "y", "c"))
    seq, rep = TOKENS_AXES, ("y", "c")
    in_specs = (
        P(seq, rep),
        P(seq, None),
        P(seq, None),
        P(seq, None),
        P(None, rep),
        P(rep),
        P(),
    )
    return jax.shard_map(shards, mesh=fine, in_specs=in_specs, out_specs=P(seq, rep), check_vma=False)
```

```python
import functools

import jax
import jax.numpy as jnp
from jax import lax
from jax.experimental import pallas as pl
from jax.experimental.pallas import tpu as pltpu
from jax.sharding import Mesh
from jax.sharding import PartitionSpec as P

TILE = 128
HEADS = 40
PLANES = 4
PLANE_HEADS = HEADS // PLANES
PART_HEADS = PLANE_HEADS // 2
CHIPS = 16
HALF = 256
GROUP = 4
UNROLL = 16
ITEMS = 256
LOG2E = 1.4426950408889634
TOKENS_AXES = ("x", "z")
LOW = -1e30


def head_plan(work):
    ids = jnp.arange(HEADS)
    ahead = (work[None, :] > work[:, None]) | ((work[None, :] == work[:, None]) & (ids[None, :] < ids[:, None]))
    rank = jnp.sum(ahead.astype(jnp.int32), axis=1)
    row, col = rank // PLANES, rank % PLANES
    plane = jnp.where(row % 2 == 1, PLANES - 1 - col, col)
    place = plane * PLANE_HEADS + row
    hit = (place[None, :] == ids[:, None]).astype(jnp.int32)
    head_at = jnp.sum(hit * ids[None, :], axis=1)
    work_at = jnp.sum(hit * work[None, :], axis=1)
    return head_at, work_at


def chip_plan(work_at):
    extra = CHIPS - PLANE_HEADS
    quota = (work_at[:, None].astype(jnp.float32) / jnp.arange(1, extra + 1).astype(jnp.float32)[None, :]).reshape(-1)
    ids = jnp.arange(quota.shape[0])
    ahead = (quota[None, :] > quota[:, None]) | ((quota[None, :] == quota[:, None]) & (ids[None, :] < ids[:, None]))
    won = (jnp.sum(ahead.astype(jnp.int32), axis=1) < extra).astype(jnp.int32)
    chips = 1 + jnp.sum(won.reshape(PLANE_HEADS, extra), axis=1)
    slots = jnp.arange(PLANE_HEADS)
    first = jnp.sum(jnp.where(slots[None, :] < slots[:, None], chips[None, :], 0), axis=1)
    return chips, first


def pack_kernel(heads, q_ref, k_ref, v_ref, out_ref, held, values, sem_v, sem_kq, sem_out):
    rows = pl.ds(pl.multiple_of(heads[CHIPS] * HALF, HALF), HALF)
    cols = [pl.ds(pl.multiple_of(heads[t] * TILE, TILE), TILE) for t in range(CHIPS)]
    first = [pltpu.make_async_copy(v_ref.at[rows, cols[t]], values.at[t], sem_v.at[t]) for t in range(CHIPS)]
    others = [
        pltpu.make_async_copy(ref.at[rows, cols[t]], held.at[t, pl.ds(at * HALF, HALF)], sem_kq.at[t, at // 2])
        for t in range(CHIPS)
        for ref, at in ((k_ref, 0), (q_ref, 2))
    ]
    for load in first + others:
        load.start()
    stores = []
    for t in range(CHIPS):
        first[t].wait()
        for sub in range(2):
            held[t, pl.ds(HALF + sub * TILE, TILE), :] = values[t, pl.ds(sub * TILE, TILE), :].T
        for load in others[2 * t : 2 * t + 2]:
            load.wait()
        stores.append(pltpu.make_async_copy(held.at[t], out_ref.at[t], sem_out.at[t]))
        stores[t].start()
    for store in stores:
        store.wait()


def pack(queries, keys, values, chip_heads, core):
    scalars = jnp.concatenate([chip_heads, core[None]]).astype(jnp.int32)
    hbm = pl.BlockSpec(memory_space=pl.ANY)
    return pl.pallas_call(
        pack_kernel,
        in_specs=[pl.BlockSpec(memory_space=pltpu.SMEM)] + [hbm] * 3,
        out_specs=hbm,
        out_shape=jax.ShapeDtypeStruct((CHIPS, 6 * TILE, TILE), jnp.bfloat16),
        scratch_shapes=[
            pltpu.VMEM((CHIPS, 3 * HALF, TILE), jnp.bfloat16),
            pltpu.VMEM((CHIPS, HALF, TILE), jnp.bfloat16),
            pltpu.SemaphoreType.DMA((CHIPS,)),
            pltpu.SemaphoreType.DMA((CHIPS, 2)),
            pltpu.SemaphoreType.DMA((CHIPS,)),
        ],
        compiler_params=pltpu.CompilerParams(vmem_limit_bytes=60 * 2**20),
    )(scalars, queries, keys, values)


def attend_items(scale, meta, q_of, k_of, valid_of, query_ref, key_ref, acc_ref, max_ref, sum_ref):
    def body(step, _):
        parts = []
        for u in range(UNROLL):
            e = step * UNROLL + u
            t = q_of[e]
            kid = [k_of[e * GROUP + g] for g in range(GROUP)]
            valid = valid_of[e]
            keys = jnp.concatenate([key_ref[i // 2, i % 2] for i in kid], axis=0)
            scores = lax.dot_general(
                keys, query_ref[t // 2, 4 + t % 2], (((1,), (1,)), ((), ())), preferred_element_type=jnp.float32
            )
            top = jnp.max(scores, axis=0, keepdims=True) * scale
            weights = []
            total = jnp.zeros((1, TILE), jnp.float32)
            for g in range(GROUP):
                shift = top + jnp.where(g < valid, 0.0, -LOW)
                w = jnp.exp2(scores[g * TILE : (g + 1) * TILE] * scale - shift)
                total = total + jnp.sum(w, axis=0, keepdims=True)
                weights.append(w.astype(jnp.bfloat16))
            vals = jnp.concatenate([key_ref[i // 2, 2 + i % 2] for i in kid], axis=1)
            part = jnp.dot(vals, jnp.concatenate(weights, axis=0), preferred_element_type=jnp.float32)
            parts.append((t, top, total, part))
        for t, top, total, part in parts:
            old = max_ref[t]
            new = jnp.maximum(old, top)
            a = jnp.exp2(old - new)
            b = jnp.exp2(top - new)
            max_ref[t] = new
            sum_ref[t] = sum_ref[t] * a + total * b
            acc_ref[t] = acc_ref[t] * a + part * b
        return 0

    lax.fori_loop(0, meta[0], body, 0)


def first_kernel(scale, meta, q_of, k_of, valid_of, own_ref, acc_ref, max_ref, sum_ref):
    acc_ref[...] = jnp.zeros_like(acc_ref)
    sum_ref[...] = jnp.zeros_like(sum_ref)
    max_ref[...] = jnp.full_like(max_ref, LOW)
    attend_items(scale, meta, q_of, k_of, valid_of, own_ref, own_ref, acc_ref, max_ref, sum_ref)


def second_kernel(scale, meta, q_of, k_of, valid_of, own_ref, other_ref, acc_in, max_in, sum_in, out_ref, acc_s, max_s, sum_s):
    acc_s[...] = acc_in[...]
    max_s[...] = max_in[...]
    sum_s[...] = sum_in[...]
    attend_items(scale, meta, q_of, k_of, valid_of, own_ref, other_ref, acc_s, max_s, sum_s)

    def finish(t, _):
        inverse = 1.0 / jnp.maximum(sum_s[t], 1e-30)
        out_ref[t // 2, t % 2] = (acc_s[t] * inverse).astype(jnp.bfloat16)
        return 0

    lax.fori_loop(0, 2 * CHIPS, finish, 0)


def attend(lists, own, other=None, state=None):
    tiles = 2 * CHIPS
    smem = pl.BlockSpec(memory_space=pltpu.SMEM)
    vmem = pl.BlockSpec(memory_space=pltpu.VMEM)
    shapes = [((tiles, TILE, TILE), jnp.float32), ((tiles, 1, TILE), jnp.float32), ((tiles, 1, TILE), jnp.float32)]
    options = dict(
        compiler_params=pltpu.CompilerParams(vmem_limit_bytes=24 * 2**20),
        cost_estimate=pl.CostEstimate(flops=4 * 10**9, bytes_accessed=8 * 2**20, transcendentals=4 * 10**6),
    )
    scale = TILE**-0.5 * LOG2E
    if other is None:
        return pl.pallas_call(
            functools.partial(first_kernel, scale),
            in_specs=[smem] * 4 + [vmem],
            out_specs=[vmem] * 3,
            out_shape=[jax.ShapeDtypeStruct(*shape) for shape in shapes],
            **options,
        )(*lists, own)
    return pl.pallas_call(
        functools.partial(second_kernel, scale),
        in_specs=[smem] * 4 + [vmem] * 5,
        out_specs=vmem,
        out_shape=jax.ShapeDtypeStruct((CHIPS, 2, TILE, TILE), jnp.bfloat16),
        scratch_shapes=[pltpu.VMEM(*shape) for shape in shapes],
        **options,
    )(*lists, own, other, *state)


def item_lists(allowed, mine):
    tiles = allowed.shape[1]
    count = jnp.sum(allowed, axis=1) * mine
    groups = (count + GROUP - 1) // GROUP
    slots = jnp.arange(groups.shape[0])
    end = jnp.sum(jnp.where(slots[None, :] <= slots[:, None], groups[None, :], 0), axis=1)
    steps = (end[-1] + UNROLL - 1) // UNROLL
    key_ids = jnp.arange(tiles)
    before = jnp.sum(allowed[:, None, :] * (key_ids[None, :] < key_ids[:, None])[None].astype(jnp.int32), axis=2)
    listed = jnp.sum(
        jnp.where((before[:, :, None] == key_ids[None, None, :]) & (allowed[:, :, None] > 0), key_ids[None, :, None], 0),
        axis=1,
    )
    item = jnp.arange(ITEMS)
    real = (item < end[-1]).astype(jnp.int32)
    held = jnp.maximum(jnp.minimum(item, end[-1] - 1), 0)
    q_of = jnp.minimum(jnp.sum((end[None, :] <= held[:, None]).astype(jnp.int32), axis=1), 2 * CHIPS - 1)
    pick = (q_of[:, None] == slots[None, :]).astype(jnp.int32)
    start = GROUP * (held - jnp.sum(pick * (end - groups)[None, :], axis=1))
    left = jnp.sum(pick * count[None, :], axis=1) - start
    rows = jnp.dot(pick.astype(jnp.float32), listed.astype(jnp.float32))
    offset = jnp.arange(GROUP)
    where = start[:, None] + jnp.where(offset[None, :] < left[:, None], offset[None, :], 0)
    k_of = jnp.sum(jnp.where(where[:, :, None] == key_ids[None, None, :], rows[:, None, :], 0.0), axis=2)
    valid = jnp.minimum(left, GROUP) * real
    return steps[None], q_of, k_of.astype(jnp.int32).reshape(-1), valid


def select_kernel(source, got_ref, out_ref, low_ref, high_ref):
    for i in range(PLANE_HEADS):
        part_ref, at = (low_ref, i) if i < PART_HEADS else (high_ref, i - PART_HEADS)
        for sub in range(2):
            rows = pl.ds(sub * TILE, TILE)
            tile = got_ref[source[2 * i + sub], sub].T
            out_ref[rows, pl.ds(i * TILE, TILE)] = tile
            part_ref[rows, pl.ds(at * TILE, TILE)] = tile


def select(source, got):
    vmem = pl.BlockSpec(memory_space=pltpu.VMEM)
    return pl.pallas_call(
        select_kernel,
        in_specs=[pl.BlockSpec(memory_space=pltpu.SMEM), vmem],
        out_specs=[vmem] * 3,
        out_shape=[
            jax.ShapeDtypeStruct((HALF, heads * TILE), jnp.bfloat16) for heads in (PLANE_HEADS, PART_HEADS, PART_HEADS)
        ],
    )(source, got)


def gather_kernel(counts, heads, w_ref, *rest):
    out_refs, (held, sem_in, sem_out) = rest[: len(counts)], rest[len(counts) :]
    loads, stores = [], []
    for n in range(HEADS):
        rows = pl.ds(pl.multiple_of(heads[n] * TILE, TILE), TILE)
        loads.append(pltpu.make_async_copy(w_ref.at[rows], held.at[n], sem_in.at[n]))
        loads[n].start()
    n = 0
    for out_ref, count in zip(out_refs, counts):
        for at in range(count):
            loads[n].wait()
            stores.append(pltpu.make_async_copy(held.at[n], out_ref.at[pl.ds(at * TILE, TILE)], sem_out.at[n]))
            stores[n].start()
            n += 1
    for store in stores:
        store.wait()


def gather(w_out, heads, counts):
    cols = w_out.shape[1]
    hbm = pl.BlockSpec(memory_space=pl.ANY)
    return pl.pallas_call(
        functools.partial(gather_kernel, counts),
        in_specs=[pl.BlockSpec(memory_space=pltpu.SMEM), hbm],
        out_specs=[hbm] * len(counts),
        out_shape=[jax.ShapeDtypeStruct((count * TILE, cols), w_out.dtype) for count in counts],
        scratch_shapes=[
            pltpu.VMEM((HEADS, TILE, cols), w_out.dtype),
            pltpu.SemaphoreType.DMA((HEADS,)),
            pltpu.SemaphoreType.DMA((HEADS,)),
        ],
        compiler_params=pltpu.CompilerParams(vmem_limit_bytes=56 * 2**20),
    )(heads, w_out)


def exchange(block):
    return lax.all_to_all(block, TOKENS_AXES, split_axis=0, concat_axis=0, tiled=True)


def along_y(block, step):
    return lax.ppermute(block, "y", [(i, (i + step) % PLANES) for i in range(PLANES)])


def swap(block):
    return lax.ppermute(block, "c", [(0, 1), (1, 0)])


def shards(residual_in, queries, keys, values, w_out, gate_scale, tile_mask):
    chip = lax.axis_index("x") * 4 + lax.axis_index("z")
    plane = lax.axis_index("y")
    core = lax.axis_index("c")
    tile_work = jnp.sum(tile_mask, axis=1)
    head_at, work_at = head_plan(jnp.sum(tile_work, axis=1))
    plane_heads = lax.dynamic_slice_in_dim(head_at, plane * PLANE_HEADS, PLANE_HEADS)
    chips, first = chip_plan(lax.dynamic_slice_in_dim(work_at, plane * PLANE_HEADS, PLANE_HEADS))
    chip_ids = jnp.arange(CHIPS)
    on_chip = (first[None, :] <= chip_ids[:, None]) & (chip_ids[:, None] < (first + chips)[None, :])
    chip_heads = jnp.sum(jnp.where(on_chip, plane_heads[None, :], 0), axis=1)
    got = exchange(pack(queries, keys, values, chip_heads, core)).reshape(CHIPS, 6, TILE, TILE)

    half_work = lax.dynamic_index_in_dim(tile_work.reshape(HEADS, CHIPS, 2, 2), core, 2, keepdims=False)
    half_work = jnp.take(half_work.reshape(HEADS, 2 * CHIPS), plane_heads, axis=0, mode="clip")
    tile_ids = jnp.arange(2 * CHIPS)
    done = jnp.sum(
        jnp.where((tile_ids[None, :] < tile_ids[:, None])[None], half_work[:, None, :], 0), axis=2
    )
    total = jnp.sum(half_work, axis=1, keepdims=True)
    owner = first[:, None] + ((2 * done + half_work) * chips[:, None]) // (2 * total)
    my_slot = jnp.sum(jnp.where(on_chip[chip], jnp.arange(PLANE_HEADS), 0))
    my_head = chip_heads[chip]
    mine_tiles = (owner[my_slot] == chip).astype(jnp.int32)
    allowed = lax.dynamic_index_in_dim(tile_mask, my_head, 0, keepdims=False)
    allowed = lax.dynamic_index_in_dim(allowed.reshape(CHIPS, 2, 2, 4 * CHIPS), core, 1, keepdims=False)
    source = lax.dynamic_slice_in_dim(owner, 2 * chip, 2, 1).reshape(-1)

    w_order = jnp.concatenate(
        [lax.dynamic_slice_in_dim(head_at, (plane + k) % PLANES * PLANE_HEADS, PLANE_HEADS) for k in (0, 3, 1, 2)]
    )
    weights = gather(w_out, w_order, (PLANE_HEADS,) + (PART_HEADS,) * 6)
    allowed = allowed.reshape(2 * CHIPS, CHIPS, 2, 2)
    lists = [
        item_lists(lax.dynamic_index_in_dim(allowed, c, 2, keepdims=False).reshape(2 * CHIPS, 2 * CHIPS), mine_tiles)
        for c in (core, 1 - core)
    ]
    got, lists, source, weights = lax.optimization_barrier((got, lists, source, weights))
    got_other = swap(got)

    def product(block, other, weight):
        return jnp.dot(jnp.concatenate([block, other], axis=0), weight, preferred_element_type=jnp.float32)

    def project(block, weight):
        return product(block, swap(block), weight)

    def by_rows(total):
        mine, theirs = total[:HALF], total[HALF:]
        return jnp.concatenate([jnp.where(core == 0, mine, theirs), jnp.where(core == 0, theirs, mine)], axis=0)

    attended = attend(lists[1], got, got_other, attend(lists[0], got))
    own, low, high = select(source, exchange(attended))
    below_low, above_high = along_y(low, 1), along_y(high, 3)
    own_other, low, high = lax.optimization_barrier((swap(own), low, high))
    below_high, above_low = along_y(high, 1), along_y(low, 3)
    far_low, far_high = along_y(below_low, 1), along_y(above_high, 3)
    total = product(own, own_other, weights[0])
    for block, weight in zip((below_low, above_high, below_high, above_low), (weights[1], weights[4], weights[2], weights[3])):
        total = total + project(block, weight)
    base = residual_in.astype(jnp.float32) + gate_scale * by_rows(total)
    base, far_low, far_high = lax.optimization_barrier((base, far_low, far_high))
    far = project(far_low, weights[5]) + project(far_high, weights[6])
    return (base + gate_scale * by_rows(far)).astype(jnp.bfloat16)


def solution(mesh):
    fine = Mesh(mesh.devices.reshape(4, 4, 4, 2), ("x", "z", "y", "c"))
    seq, rep = TOKENS_AXES, ("y", "c")
    in_specs = (
        P(seq, rep),
        P(seq, None),
        P(seq, None),
        P(seq, None),
        P(None, rep),
        P(rep),
        P(),
    )
    return jax.shard_map(shards, mesh=fine, in_specs=in_specs, out_specs=P(seq, rep), check_vma=False)
```
